128 devices in a mesh: gx: 16 (over x, y), gz: 8 (over z, core).
Axes of the slice: x: 4, y: 4, z: 4, core: 2. Of those that a mesh axis runs over, the one named last changes fastest.
Arguments:
- pressure_now: float32 [256, 256, 512], P('gz', 'gx'), may hold values from -6 to 6
- pressure_prev: float32 [256, 256, 512], P('gz', 'gx'), may hold values from -6 to 6
- adjoint_now: float32 [256, 256, 512], P('gz', 'gx'), may hold values from -6 to 6
- adjoint_prev: float32 [256, 256, 512], P('gz', 'gx'), may hold values from -6 to 6
- speed2: float32 [256, 256, 512], P('gz', 'gx'), may hold values from 0.05 to 0.32
- layer_state: float32 [16384, 64, 128], P(('gx', 'gz')), may hold values from -3 to 3
- layer_maps: float32 [8, 64, 64], replicated, as said below
- send_rows: int32 [128, 128, 1], P(('gx', 'gz')), may hold values from -1 to 2047, as said below
- slot_patch: int32 [16384], P(('gx', 'gz')), may hold values from 0 to 1023
- patch_material: int32 [1024], replicated, may hold values from 0 to 7
Outputs:
- pressure_out: float32 [256, 256, 512], P('gz', 'gx')
- adjoint_out: float32 [256, 256, 512], P('gz', 'gx')
- patch_gradient: float32 [1024, 128], P(('gx', 'gz'))
The draws below stay inside these ranges and needn't reach their ends.
Inputs may be any that keep to these rules, and one draw needn't show every extreme that they name: `send_rows`: each device's non-negative entries are distinct rows of its tile; -1 marks an unused entry; for one device every entry aimed at it is used. `layer_maps`: each material's matrix has diagonal entries from 0.5 to 0.9.
All inputs are finite; a program needn't handle non-finite values.
Results may differ from the reference program's by a relative error of at most 0.00016.
Values sent between devices are 32-bit elements; how exact they have to be, the bound alone decides.
No kernel may reach another device: no remote copies, remote signals or barrier semaphores. Data moves between devices by JAX's collectives and lax.ppermute only.
A program may use at most 192 MiB of HBM per device.

```python
import math
import jax
import jax.numpy as jnp
import numpy as np
from jax import lax

CX = 16
CZ = 32
NY = 512
W = 128
DEPTH = 64
SLOT_DEV = 128
MATS = 8
STEPS = 4
NX = 256
NZ = 256
ROWS_TILE = 2048
CAP = 1
PATCHES = 1024
N_GX = 16
N_GZ = 8
DEVICES = 128


def draw_layer_maps(key, part):
    first, second = jax.random.split(key)
    diag = jax.random.uniform(first, (MATS, DEPTH), jnp.float32, 0.5, 0.9)
    spread = 0.4 / math.sqrt(DEPTH)
    off = jax.random.normal(second, (MATS, DEPTH, DEPTH), jnp.float32) * spread
    ident = jnp.eye(DEPTH, dtype=jnp.float32)
    return ident[None, :, :] * diag[:, :, None] + off * (1.0 - ident[None, :, :])


def draw_send_rows(key, part):
    key_fill, key_full, key_coin, key_perm = jax.random.split(key, 4)
    fill = jax.random.randint(key_fill, (DEVICES,), 300, 1001)
    fullest = jax.random.randint(key_full, (), 0, DEVICES)
    fill = jnp.where(jnp.arange(DEVICES) == fullest, 1001, fill)
    coin = jax.random.randint(key_coin, (DEVICES, DEVICES, CAP), 0, 1000)
    live = coin < fill[None, :, None]
    keys = jax.random.split(key_perm, DEVICES)
    picks = jax.vmap(lambda single: jax.random.permutation(single, ROWS_TILE)[:SLOT_DEV])(keys)
    picks = picks.reshape(DEVICES, DEVICES, CAP).astype(jnp.int32)
    return jnp.where(live, picks, -1).astype(jnp.int32)


def set_ends(result, stream_key, low, top_value):
    spot = [jax.random.randint(jax.random.fold_in(stream_key, axis), (), 0, length) for axis, length in enumerate(result.shape)]
    widest = result.shape.index(max(result.shape))
    neighbour = spot[:widest] + [(spot[widest] + 1) % result.shape[widest]] + spot[widest + 1:]
    return result.at[tuple(spot)].set(low).at[tuple(neighbour)].set(top_value)


def block_levels(rng, dims, cuts, smallest, top_value):
    loudness = 1.0
    for dim, parts in cuts:
        draws = jax.random.uniform(jax.random.fold_in(jax.random.fold_in(rng, 6), dim), (parts,), jnp.float32, smallest / len(cuts), top_value / len(cuts))
        loudness = loudness * jnp.repeat(jnp.exp(draws), dims[dim] // parts).reshape((-1,) + (1,) * (len(dims) - 1 - dim))
    return loudness


def rank_bounds(amount, lean):
    loads = [(1 << 20) // math.isqrt(grade ** lean) + 1 for grade in range(1, amount + 1)]
    width = 1 + sum(loads) // (1 << 30)
    return np.cumsum(np.array([max(1, weight // width) for weight in loads]))


def skewed_ids(key, extent, count, skew):
    grid = rank_bounds(count, skew)
    lot = jax.random.randint(jax.random.fold_in(key, 1), extent, 0, int(grid[count - 1]))
    rank = jnp.searchsorted(jnp.asarray(grid, jnp.int32), lot, side="right")
    return jax.random.permutation(jax.random.fold_in(key, 2), count)[rank].astype(jnp.int32)


def normal_values(rng, dims, deviation, reach, cuts=(), kind=jnp.bfloat16):
    entries = jax.random.normal(rng, dims, jnp.float32) * deviation
    if len(cuts) > 0:
        entries = block_levels(rng, dims, cuts, -0.22, 0.18) * entries
    return jnp.clip(entries, min=-reach, max=reach).astype(kind)


def setup_inputs(seed: int = 0) -> dict:
    seeds = jax.random.split(jax.random.key(seed), 11)
    pressure_now = normal_values(seeds[0], (NZ, NX, NY), 1.0, 6.0, ((0, 8), (1, 16)), jnp.float32)
    pressure_prev = normal_values(seeds[1], (NZ, NX, NY), 1.0, 6.0, ((0, 8), (1, 16)), jnp.float32)
    adjoint_now = normal_values(seeds[2], (NZ, NX, NY), 1.0, 6.0, ((0, 8), (1, 16)), jnp.float32)
    adjoint_prev = normal_values(seeds[3], (NZ, NX, NY), 1.0, 6.0, ((0, 8), (1, 16)), jnp.float32)
    speed2 = jnp.clip(jnp.exp(math.log(0.32) - 1.856298 * jax.random.uniform(seeds[4], (NZ, NX, NY), jnp.float32) ** block_levels(seeds[4], (NZ, NX, NY), ((0, 8), (1, 16)), -0.2, 0.2)), 0.05, 0.32)
    layer_state = normal_values(seeds[5], (DEVICES * SLOT_DEV, DEPTH, W), 0.5, 3.0, ((0, 128),), jnp.float32)
    layer_maps = draw_layer_maps(jax.random.fold_in(seeds[10], 71), 0)
    send_rows = draw_send_rows(jax.random.fold_in(seeds[10], 71), 0)
    slot_patch = set_ends(skewed_ids(seeds[8], (DEVICES * SLOT_DEV,), PATCHES, 2), jax.random.fold_in(seeds[8], 3), 0, PATCHES - 1).astype(jnp.int32)
    patch_material = set_ends(jax.random.randint(seeds[9], (PATCHES,), 0, MATS), jax.random.fold_in(seeds[9], 1), 0, MATS - 1).astype(jnp.int32)
    return dict(pressure_now=pressure_now, pressure_prev=pressure_prev, adjoint_now=adjoint_now, adjoint_prev=adjoint_prev, speed2=speed2, layer_state=layer_state, layer_maps=layer_maps, send_rows=send_rows, slot_patch=slot_patch, patch_material=patch_material)


KAPPA = 0.5
BETA = 0.3


def to_rows(field):
    blocks = field.reshape(N_GZ, CZ, N_GX, CX, NY // W, W).transpose(2, 0, 1, 3, 4, 5)
    return blocks.reshape(N_GX * N_GZ, CZ * CX * (NY // W), W)


def from_rows(rows):
    blocks = rows.reshape(N_GX, N_GZ, CZ, CX, NY // W, W).transpose(1, 2, 0, 3, 4, 5)
    return blocks.reshape(N_GZ * CZ, N_GX * CX, NY)


def laplace(field):
    padded = jnp.pad(field, 1)
    beside = padded[2:, 1:-1, 1:-1] + padded[:-2, 1:-1, 1:-1]
    beside = beside + padded[1:-1, 2:, 1:-1] + padded[1:-1, :-2, 1:-1]
    beside = beside + padded[1:-1, 1:-1, 2:] + padded[1:-1, 1:-1, :-2]
    return beside - 6.0 * field


def place_rows(target, delta):
    empty = jnp.zeros((ROWS_TILE, W), jnp.float32)
    return empty.at[target].add(delta, mode="drop")


def relay_step(field, previous, speed2, layer, maps, send_rows):
    devices = N_GX * N_GZ
    rows = to_rows(field)
    sources = send_rows.reshape(devices, SLOT_DEV)
    valid = sources >= 0
    picked = jnp.take_along_axis(rows, jnp.maximum(sources, 0)[:, :, None], axis=1)
    picked = jnp.where(valid[:, :, None], picked, 0.0)
    air = picked.reshape(devices, devices, CAP, W).transpose(1, 0, 2, 3).reshape(devices * SLOT_DEV, W)
    push = KAPPA * (air - layer[:, 0, :])
    fresh = jnp.einsum("sij,sjw->siw", maps, layer, precision=lax.Precision.HIGHEST)
    fresh = fresh + maps[:, :, 0][:, :, None] * push[:, None, :]
    back = fresh[:, 0, :].reshape(devices, devices, CAP, W).transpose(1, 0, 2, 3).reshape(devices, SLOT_DEV, W)
    delta = jnp.where(valid[:, :, None], BETA * (back - picked), 0.0)
    target = jnp.where(valid, sources, ROWS_TILE).astype(jnp.int32)
    coupling = jax.vmap(place_rows)(target, delta)
    following = 2.0 * field - previous + speed2 * laplace(field) + from_rows(coupling)
    return following, fresh


def reference(pressure_now, pressure_prev, adjoint_now, adjoint_prev, speed2, layer_state, layer_maps, send_rows, slot_patch, patch_material):
    materials = jnp.take(patch_material, slot_patch)
    forward_maps = jnp.take(layer_maps, materials, axis=0)
    adjoint_maps = jnp.swapaxes(forward_maps, 1, 2)
    layer_f = layer_state
    layer_a = jnp.zeros_like(layer_state)
    forward_layers = []
    adjoint_layers = []
    for step in range(STEPS):
        following, layer_f = relay_step(pressure_now, pressure_prev, speed2, layer_f, forward_maps, send_rows)
        pressure_prev, pressure_now = pressure_now, following
        following, layer_a = relay_step(adjoint_now, adjoint_prev, speed2, layer_a, adjoint_maps, send_rows)
        adjoint_prev, adjoint_now = adjoint_now, following
        forward_layers.append(layer_f)
        adjoint_layers.append(layer_a)
    correlation = jnp.zeros((layer_state.shape[0], W), jnp.float32)
    for step in range(STEPS):
        correlation = correlation + jnp.sum(forward_layers[step] * adjoint_layers[STEPS - 1 - step], axis=1)
    patch_gradient = jax.ops.segment_sum(correlation, slot_patch, num_segments=PATCHES)
    return pressure_now, adjoint_now, patch_gradient
```

```python
import functools

import jax
import jax.numpy as jnp
from jax import lax
from jax.experimental import pallas as pl
from jax.experimental.pallas import tpu as pltpu
from jax.sharding import PartitionSpec as P

STEPS = 4
KAPPA = 0.5
BETA = 0.3
TERMS = STEPS + 1
LINES = 8
META = TERMS
MIB = 1 << 20
VMEM = pltpu.VMEM
SMEM = pltpu.SMEM


def params(mib):
    return pltpu.CompilerParams(vmem_limit_bytes=mib * MIB)


def surface_kernel(block, maps, patch_ref, material_ref, layer, out, vectors, scalars):
    depth = maps.shape[1]
    width = layer.shape[2]
    mats = maps.shape[0]

    @pl.when(pl.program_id(0) == 0)
    def _():
        lane = lax.broadcasted_iota(jnp.int32, (1, width), 1)
        first = lax.broadcasted_iota(jnp.int32, (depth, 1), 0) == 0
        for mat in range(mats):
            matrix = maps[mat]
            turned = matrix.T
            row, col = matrix[0:1, :], turned[:, 0:1]
            kept = jnp.zeros((1, width), jnp.float32)
            for n in range(TERMS):
                if n > 0:
                    row, col = (
                        jnp.sum(matrix * col, axis=0, keepdims=True),
                        jnp.sum(turned * row, axis=1, keepdims=True),
                    )
                scaled = jnp.where(first, (1.0 - KAPPA) * col, col)
                vectors[mat, n] = jnp.broadcast_to(scaled, (depth, width))
                kept = jnp.where(lane == n + 1, col[0:1, 0:1], kept)
            scalars[mat] = jnp.broadcast_to(kept, (8, width))

    lane = lax.broadcasted_iota(jnp.int32, (1, width), 1)

    def one(j, carry):
        patch = patch_ref[pl.program_id(0) * block + j]
        mat = material_ref[patch]
        sums = [jnp.zeros((8, width), jnp.float32)] * TERMS
        for c in range(depth // 8):
            part = layer[j, pl.ds(8 * c, 8), :]
            sums = [
                s + vectors[mat, n, pl.ds(8 * c, 8), :] * part for n, s in enumerate(sums)
            ]
        rows = [jnp.sum(s, axis=0, keepdims=True) for s in sums]
        scalar_row = jnp.where(lane == 0, patch.astype(jnp.float32), scalars[mat][0:1, :])
        rows.append(scalar_row)
        rows.extend([jnp.zeros((1, width), jnp.float32)] * (LINES - len(rows)))
        out[j] = jnp.concatenate(rows, axis=0)
        return carry

    lax.fori_loop(0, block, one, 0, unroll=2)


def surface_rows(layer_maps, slot_patch, patch_material, layer_state):
    slots, depth, width = layer_state.shape
    mats = layer_maps.shape[0]
    block = 16
    return pl.pallas_call(
        functools.partial(surface_kernel, block),
        grid=(slots // block,),
        in_specs=[
            pl.BlockSpec((mats, depth, depth), lambda i: (0, 0, 0)),
            pl.BlockSpec(memory_space=SMEM),
            pl.BlockSpec(memory_space=SMEM),
            pl.BlockSpec((block, depth, width), lambda i: (i, 0, 0)),
        ],
        out_specs=pl.BlockSpec((block, LINES, width), lambda i: (i, 0, 0)),
        out_shape=jax.ShapeDtypeStruct((slots, LINES, width), jnp.float32),
        scratch_shapes=[
            pltpu.VMEM((mats, TERMS, depth, width), jnp.float32),
            pltpu.VMEM((mats, 8, width), jnp.float32),
        ],
        compiler_params=params(16),
        name="surface_rows",
    )(layer_maps, slot_patch, patch_material, layer_state)


def place(index, cells_x, parts):
    return index // (cells_x * parts), index // parts % cells_x, index % parts


def pick(rows_ref, fields, picked, tiles):
    cells_x = fields[0].shape[1]
    slots, width = picked.shape[1:]
    parts = fields[0].shape[2] // width

    def fetch(k, carry):
        z, x, part = place(jnp.maximum(rows_ref[k], 0), cells_x, parts)
        lines = pl.ds(pl.multiple_of(x // 8 * 8, 8), 8)
        lanes = pl.ds(pl.multiple_of(part * width, width), width)
        for side, field in enumerate(fields):
            tiles[side, pl.ds(pl.multiple_of(8 * k, 8), 8), :] = field[z, lines, lanes]
        return carry

    lax.fori_loop(0, slots, fetch, 0, unroll=8)

    def choose(k, carry):
        index = rows_ref[k]
        line = 8 * k + place(jnp.maximum(index, 0), cells_x, parts)[1] % 8
        for side in range(len(fields)):
            row = tiles[side, pl.ds(line, 1), :]
            picked[side, pl.ds(k, 1), :] = jnp.where(index >= 0, row, 0.0)
        return carry

    lax.fori_loop(0, slots, choose, 0, unroll=8)


def keep_sides(cells, side, z, x_low, x_high):
    last_x, width = cells.shape[0] - 1, x_low.shape[3]
    for part in range(x_low.shape[1]):
        lanes = slice(part * width, (part + 1) * width)
        x_low[side, part, pl.ds(z, 1), :] = cells[0:1, lanes]
        x_high[side, part, pl.ds(z, 1), :] = cells[last_x : last_x + 1, lanes]


def side_row(plane, side, z):
    parts = plane.shape[1]
    return jnp.concatenate([plane[side, part, pl.ds(z, 1), :] for part in range(parts)], axis=1)


def edges_kernel(rows_ref, field, adjoint, x_low, x_high, z_low, z_high, push, picked, tiles):
    last_z = field.shape[0] - 1

    def one(z, carry):
        for side, array in enumerate((field, adjoint)):
            keep_sides(array[z], side, z, x_low, x_high)
        return carry

    lax.fori_loop(0, field.shape[0], one, 0, unroll=4)
    for side, array in enumerate((field, adjoint)):
        z_low[side] = array[0]
        z_high[side] = array[last_z]
    pick(rows_ref, (field, adjoint), picked, tiles)
    push[...] = KAPPA * picked[...]


def edge_shapes(field, slots, width):
    cells_z, cells_x, along = field.shape
    f32 = jnp.float32
    return [
        jax.ShapeDtypeStruct((2, along // width, cells_z, width), f32),
        jax.ShapeDtypeStruct((2, along // width, cells_z, width), f32),
        jax.ShapeDtypeStruct((2, cells_x, along), f32),
        jax.ShapeDtypeStruct((2, cells_x, along), f32),
        jax.ShapeDtypeStruct((2, slots, width), f32),
    ]


def first_edges(rows, field, adjoint, slots, width):
    return pl.pallas_call(
        edges_kernel,
        in_specs=[pl.BlockSpec(memory_space=SMEM)] + [pl.BlockSpec(memory_space=VMEM)] * 2,
        out_specs=[pl.BlockSpec(memory_space=VMEM)] * 5,
        out_shape=edge_shapes(field, slots, width),
        scratch_shapes=[
            pltpu.VMEM((2, slots, width), jnp.float32),
            pltpu.VMEM((2, 8 * slots, width), jnp.float32),
        ],
        compiler_params=params(16),
        name="edges",
    )(rows, field, adjoint)


def column(meta, n):
    return meta[:, n : n + 1]


def step_kernel(step, *refs):
    last = step == STEPS - 1
    rows_ref, field, field_prev, adjoint, adjoint_prev, speed2 = refs[:6]
    x_before, x_after, z_before, z_after, lines = refs[6:11]
    pushes = refs[11 : 12 + step]
    refs = refs[12 + step :]
    field_out, adjoint_out = refs[:2]
    refs = refs[2:]
    if not last:
        x_low, x_high, z_low, z_high, push_out = refs[:5]
        refs = refs[5:]
        if step == STEPS - 2:
            gradient_out = refs[0]
            refs = refs[1:]
    coupling, change, picked, tiles = refs

    cells_z, cells_x, along = field.shape
    slots, width = change.shape[1:]
    parts = along // width
    meta = lines[pl.ds(META, slots, stride=LINES), :]

    def line(n):
        return lines[pl.ds(n - 1, slots, stride=LINES), :]

    scalars = [None] + [column(meta, n) for n in range(1, TERMS + 1)]
    surface = []
    pick(rows_ref, (field, adjoint), picked, tiles)
    for side in range(2):
        new = line(step + 1) if side == 0 else None
        for t in range(step + 1):
            term = scalars[step + 1 - t] * pushes[t][side]
            new = term if new is None else new + term
        surface.append(new)
        change[side] = BETA * (new - picked[side])

    coupling[...] = jnp.zeros_like(coupling)

    def put(k, carry):
        index = rows_ref[k]
        z, x, part = place(jnp.maximum(index, 0), cells_x, parts)
        z = jnp.where(index >= 0, z, cells_z)
        for side in range(2):
            coupling[side * parts + part, z, pl.ds(x, 1), :] = change[side, pl.ds(k, 1), :]
        return carry

    lax.fori_loop(0, slots, put, 0, unroll=8)

    gx, gz = lax.axis_index("gx"), lax.axis_index("gz")
    at_x_low, at_x_high = gx == 0, gx == lax.axis_size("gx") - 1
    at_z_low, at_z_high = gz == 0, gz == lax.axis_size("gz") - 1
    row_id = lax.broadcasted_iota(jnp.int32, (cells_x, along), 0)
    lane_id = lax.broadcasted_iota(jnp.int32, (cells_x, along), 1)

    def plane(z, below, above):
        speed = speed2[z]
        for side, (now, before, out) in enumerate(
            ((field, field_prev, field_out), (adjoint, adjoint_prev, adjoint_out))
        ):
            cells = now[z]
            low = jnp.where(at_x_low, 0.0, side_row(x_before, side, z))
            high = jnp.where(at_x_high, 0.0, side_row(x_after, side, z))
            beside = below(side, now) + above(side, now)
            beside = beside + jnp.where(row_id == 0, low, pltpu.roll(cells, 1, axis=0))
            beside = beside + jnp.where(
                row_id == cells_x - 1, high, pltpu.roll(cells, cells_x - 1, axis=0)
            )
            beside = beside + jnp.where(lane_id == 0, 0.0, pltpu.roll(cells, 1, axis=1))
            beside = beside + jnp.where(
                lane_id == along - 1, 0.0, pltpu.roll(cells, along - 1, axis=1)
            )
            extra = jnp.concatenate(
                [coupling[side * parts + part, z] for part in range(parts)], axis=1
            )
            new = 2.0 * cells - before[z] + speed * (beside - 6.0 * cells) + extra
            out[z] = new
            if not last:
                keep_sides(new, side, z, x_low, x_high)

    def inner(z, carry):
        plane(z, lambda side, now: now[z - 1], lambda side, now: now[z + 1])
        return carry

    plane(
        0,
        lambda side, now: jnp.where(at_z_low, 0.0, z_before[side]),
        lambda side, now: now[1],
    )
    lax.fori_loop(1, cells_z - 1, inner, 0, unroll=2)
    plane(
        cells_z - 1,
        lambda side, now: now[cells_z - 2],
        lambda side, now: jnp.where(at_z_high, 0.0, z_after[side]),
    )
    if last:
        return

    for side, out in enumerate((field_out, adjoint_out)):
        z_low[side] = out[0]
        z_high[side] = out[cells_z - 1]
    pick(rows_ref, (field_out, adjoint_out), picked, tiles)
    for side in range(2):
        push_out[side] = KAPPA * (picked[side] - surface[side])

    if step == STEPS - 2:
        forward = [pushes[t][0] for t in range(step + 1)] + [push_out[0]]
        backward = [pushes[t][1] for t in range(step + 1)] + [push_out[1]]
        total = jnp.zeros((slots, width), jnp.float32)
        for late in range(STEPS):
            inside = (STEPS - late) * line(TERMS - late)
            for t in range(STEPS - late):
                inside = inside + ((STEPS - late - t) * scalars[TERMS - late - t]) * forward[t]
            total = total + backward[late] * inside
        patches = gradient_out.shape[0]
        ids = column(meta, 0).astype(jnp.int32)
        owners = lax.broadcasted_iota(jnp.int32, (slots, patches), 1) == ids
        gradient_out[...] = lax.dot_general(
            owners.astype(jnp.float32),
            total,
            (((0,), (0,)), ((), ())),
            precision=lax.Precision.HIGHEST,
            preferred_element_type=jnp.float32,
        )


def step_call(step, rows, field, field_prev, adjoint, adjoint_prev, speed2, halos, lines, pushes, patches):
    slots, width = pushes[0].shape[1:]
    last = step == STEPS - 1
    cells_z, cells_x, along = field.shape
    parts = along // width
    shapes = [jax.ShapeDtypeStruct(field.shape, jnp.float32)] * 2
    if not last:
        shapes = shapes + edge_shapes(field, slots, width)
    if step == STEPS - 2:
        shapes = shapes + [jax.ShapeDtypeStruct((patches, width), jnp.float32)]
    operands = [field, field_prev, adjoint, adjoint_prev, speed2, *halos, lines, *pushes]
    return pl.pallas_call(
        functools.partial(step_kernel, step),
        in_specs=[pl.BlockSpec(memory_space=SMEM)]
        + [pl.BlockSpec(memory_space=VMEM)] * len(operands),
        out_specs=[pl.BlockSpec(memory_space=VMEM)] * len(shapes),
        out_shape=shapes,
        scratch_shapes=[
            pltpu.VMEM((2 * parts, cells_z + 1, cells_x, width), jnp.float32),
            pltpu.VMEM((2, slots, width), jnp.float32),
            pltpu.VMEM((2, slots, width), jnp.float32),
            pltpu.VMEM((2, 8 * slots, width), jnp.float32),
        ],
        compiler_params=params(24),
        name=f"step{step}",
    )(rows, *operands)


def ring(axis, shift):
    count = lax.axis_size(axis)
    return [(i, (i + shift) % count) for i in range(count)]


def exchange(edges):
    x_low, x_high, z_low, z_high = edges
    x_before = lax.ppermute(x_high, "gx", ring("gx", 1))
    x_after = lax.ppermute(x_low, "gx", ring("gx", -1))
    z_before = lax.ppermute(z_high, "gz", ring("gz", 1))
    z_after = lax.ppermute(z_low, "gz", ring("gz", -1))
    return x_before, x_after, z_before, z_after


def body(
    pressure_now,
    pressure_prev,
    adjoint_now,
    adjoint_prev,
    speed2,
    layer_state,
    layer_maps,
    send_rows,
    slot_patch,
    patch_material,
):
    slots, _, width = layer_state.shape
    patches = patch_material.shape[0]
    devices = lax.axis_size(("gx", "gz"))
    rows = send_rows.reshape(-1)

    *edges, push = first_edges(rows, pressure_now, adjoint_now, slots, width)
    halos = exchange(edges)
    lines = surface_rows(layer_maps, slot_patch, patch_material, layer_state)
    lines = lax.all_to_all(lines, ("gx", "gz"), split_axis=0, concat_axis=0, tiled=True)
    lines = lines.reshape(slots * LINES, width)

    fields = (pressure_now, pressure_prev, adjoint_now, adjoint_prev)
    pushes = [push]
    for step in range(STEPS):
        results = step_call(step, rows, *fields, speed2, halos, lines, pushes, patches)
        fields = (results[0], fields[0], results[1], fields[2])
        if step < STEPS - 1:
            halos = exchange(results[2:6])
            pushes.append(results[6])
        if step == STEPS - 2:
            parts = results[7].reshape(devices, patches // devices, width)
            parts = lax.all_to_all(parts, ("gx", "gz"), split_axis=0, concat_axis=0, tiled=True)
            gradient = jnp.sum(parts, axis=0)
    return fields[0], fields[2], gradient


def solution(mesh):
    grid = P("gz", "gx", None)
    split = P(("gx", "gz"), None, None)
    in_specs = (grid, grid, grid, grid, grid, split, P(), split, P(("gx", "gz")), P())
    out_specs = (grid, grid, P(("gx", "gz"), None))
    return jax.shard_map(body, mesh=mesh, in_specs=in_specs, out_specs=out_specs, check_vma=False)
```

```python
import functools

import jax
import jax.numpy as jnp
from jax import lax
from jax.experimental import pallas as pl
from jax.experimental.pallas import tpu as pltpu
from jax.sharding import PartitionSpec as P

STEPS = 4
KAPPA = 0.5
BETA = 0.3
TERMS = STEPS + 1
LINES = 8
META = TERMS
MIB = 1 << 20
VMEM = pltpu.VMEM
SMEM = pltpu.SMEM
HBM = pltpu.HBM
UNROLL = 10


def in_hbm(*arrays):
    return [pltpu.with_memory_space_constraint(array, HBM) for array in arrays]


def params(mib):
    return pltpu.CompilerParams(vmem_limit_bytes=mib * MIB)


def surface_kernel(maps_hbm, patch_hbm, material_hbm, layer_hbm, out, maps, patch_ref, material_ref, layer, vectors, scalars, sems):
    mats, _, depth = maps.shape
    slots, _, width = layer.shape
    chunks = sems.shape[0] - 3
    block = slots // chunks
    small = [
        pltpu.make_async_copy(maps_hbm, maps, sems.at[chunks]),
        pltpu.make_async_copy(patch_hbm, patch_ref, sems.at[chunks + 1]),
        pltpu.make_async_copy(material_hbm, material_ref, sems.at[chunks + 2]),
    ]
    large = [
        pltpu.make_async_copy(
            layer_hbm.at[pl.ds(i * block, block)], layer.at[pl.ds(i * block, block)], sems.at[i]
        )
        for i in range(chunks)
    ]
    for copy in small + large:
        copy.start()

    lane = lax.broadcasted_iota(jnp.int32, (1, width), 1)
    first = lax.broadcasted_iota(jnp.int32, (depth, 1), 0) == 0
    small[0].wait()
    matrices = [maps[mat] for mat in range(mats)]
    turned = [matrix.T for matrix in matrices]
    rows = [matrix[0:1, :] for matrix in matrices]
    cols = [matrix[:, 0:1] for matrix in turned]
    kept = [jnp.zeros((1, width), jnp.float32)] * mats
    for n in range(TERMS):
        for mat in range(mats):
            if n > 0:
                rows[mat], cols[mat] = (
                    jnp.sum(matrices[mat] * cols[mat], axis=0, keepdims=True),
                    jnp.sum(turned[mat] * rows[mat], axis=1, keepdims=True),
                )
            scaled = jnp.where(first, (1.0 - KAPPA) * cols[mat], cols[mat])
            vectors[mat, n] = jnp.broadcast_to(scaled, (depth, width))
            kept[mat] = jnp.where(lane == n + 1, cols[mat][0:1, 0:1], kept[mat])
    for mat in range(mats):
        scalars[mat] = jnp.broadcast_to(kept[mat], (8, width))
    small[1].wait()
    small[2].wait()

    def one(j, carry):
        patch = patch_ref[j]
        mat = material_ref[patch]
        sums = [jnp.zeros((8, width), jnp.float32)] * TERMS
        for c in range(depth // 8):
            part = layer[j, pl.ds(8 * c, 8), :]
            sums = [
                s + vectors[mat, n, pl.ds(8 * c, 8), :] * part for n, s in enumerate(sums)
            ]
        rows = [jnp.sum(s, axis=0, keepdims=True) for s in sums]
        scalar_row = jnp.where(lane == 0, patch.astype(jnp.float32), scalars[mat][0:1, :])
        rows.append(scalar_row)
        rows.extend([jnp.zeros((1, width), jnp.float32)] * (LINES - len(rows)))
        out[j] = jnp.concatenate(rows, axis=0)
        return carry

    for i in range(chunks):
        large[i].wait()
        lax.fori_loop(i * block, (i + 1) * block, one, 0, unroll=4)


def surface_rows(layer_maps, slot_patch, patch_material, layer_state):
    slots, depth, width = layer_state.shape
    mats = layer_maps.shape[0]
    chunks = 4
    return pl.pallas_call(
        surface_kernel,
        in_specs=[pl.BlockSpec(memory_space=HBM)] * 4,
        out_specs=pl.BlockSpec(memory_space=VMEM),
        out_shape=jax.ShapeDtypeStruct((slots, LINES, width), jnp.float32),
        scratch_shapes=[
            pltpu.VMEM((mats, depth, depth), jnp.float32),
            pltpu.SMEM(slot_patch.shape, jnp.int32),
            pltpu.SMEM(patch_material.shape, jnp.int32),
            pltpu.VMEM((slots, depth, width), jnp.float32),
            pltpu.VMEM((mats, TERMS, depth, width), jnp.float32),
            pltpu.VMEM((mats, 8, width), jnp.float32),
            pltpu.SemaphoreType.DMA((chunks + 3,)),
        ],
        compiler_params=params(24),
        name="surface_rows",
    )(*in_hbm(layer_maps, slot_patch, patch_material, layer_state))


def place(index, cells_x, parts):
    low, middle = parts.bit_length() - 1, cells_x.bit_length() - 1
    return (
        jnp.right_shift(index, low + middle),
        jnp.bitwise_and(jnp.right_shift(index, low), cells_x - 1),
        jnp.bitwise_and(index, parts - 1),
    )


def pick(rows_ref, fields, picked, tiles):
    cells_x = fields[0].shape[1]
    slots, width = picked.shape[1:]
    parts = fields[0].shape[2] // width

    def fetch(k, carry):
        z, x, part = place(jnp.maximum(rows_ref[k], 0), cells_x, parts)
        lines = pl.ds(pl.multiple_of(jnp.bitwise_and(x, -8), 8), 8)
        lanes = pl.ds(pl.multiple_of(part * width, width), width)
        for side, field in enumerate(fields):
            tiles[side, pl.ds(pl.multiple_of(8 * k, 8), 8), :] = field[z, lines, lanes]
        return carry

    lax.fori_loop(0, slots, fetch, 0, unroll=8)

    def choose(k, carry):
        index = rows_ref[k]
        line = 8 * k + jnp.bitwise_and(place(jnp.maximum(index, 0), cells_x, parts)[1], 7)
        for side in range(len(fields)):
            row = tiles[side, pl.ds(line, 1), :]
            picked[side, pl.ds(k, 1), :] = jnp.where(index >= 0, row, 0.0)
        return carry

    lax.fori_loop(0, slots, choose, 0, unroll=8)


def even(axis):
    return lax.axis_index(axis) % 2 == 0


def at_start(axis):
    return lax.axis_index(axis) == 0


def at_end(axis):
    return lax.axis_index(axis) == lax.axis_size(axis) - 1


def outgoing(axis, low, high):
    choice = even(axis)
    return jnp.where(choice, low, high), jnp.where(choice, high, low)


def incoming(axis, outer, inner):
    choice = even(axis)
    before = jnp.where(at_start(axis), 0.0, jnp.where(choice, outer, inner))
    after = jnp.where(at_end(axis), 0.0, jnp.where(choice, inner, outer))
    return before, after


def keep_sides(cells, side, z, x_outer, x_inner):
    last_x, width = cells.shape[0] - 1, x_outer.shape[3]
    for part in range(x_outer.shape[1]):
        lanes = slice(part * width, (part + 1) * width)
        x_outer[side, part, pl.ds(z, 1), :], x_inner[side, part, pl.ds(z, 1), :] = outgoing(
            "gx", cells[0:1, lanes], cells[last_x : last_x + 1, lanes]
        )


def side_row(plane, side, z):
    parts = plane.shape[1]
    return jnp.concatenate([plane[side, part, pl.ds(z, 1), :] for part in range(parts)], axis=1)


def edges_kernel(rows_hbm, field_hbm, adjoint_hbm, x_outer, x_inner, z_outer, z_inner, push, picked, rows_ref, field, adjoint, tiles, sems):
    fields = (field, adjoint)
    copies = [
        pltpu.make_async_copy(rows_hbm, rows_ref, sems.at[2]),
        pltpu.make_async_copy(field_hbm, field, sems.at[0]),
        pltpu.make_async_copy(adjoint_hbm, adjoint, sems.at[1]),
    ]
    for copy in copies:
        copy.start()
    for side, array in enumerate(fields):
        copies[side + 1].wait()

        def one(z, carry):
            keep_sides(array[z], side, z, x_outer, x_inner)
            return carry

        lax.fori_loop(0, array.shape[0], one, 0, unroll=8)
        z_outer[side], z_inner[side] = outgoing("gz", array[0], array[array.shape[0] - 1])
    copies[0].wait()
    pick(rows_ref, fields, picked, tiles)
    push[...] = KAPPA * picked[...]


def edge_shapes(field, slots, width):
    cells_z, cells_x, along = field.shape
    f32 = jnp.float32
    return [
        jax.ShapeDtypeStruct((2, along // width, cells_z, width), f32),
        jax.ShapeDtypeStruct((2, along // width, cells_z, width), f32),
        jax.ShapeDtypeStruct((2, cells_x, along), f32),
        jax.ShapeDtypeStruct((2, cells_x, along), f32),
        jax.ShapeDtypeStruct((2, slots, width), f32),
        jax.ShapeDtypeStruct((2, slots, width), f32),
    ]


def first_edges(rows, field, adjoint, slots, width):
    return pl.pallas_call(
        edges_kernel,
        in_specs=[pl.BlockSpec(memory_space=HBM)] * 3,
        out_specs=[pl.BlockSpec(memory_space=VMEM)] * 6,
        out_shape=edge_shapes(field, slots, width),
        scratch_shapes=[
            pltpu.SMEM((slots,), jnp.int32),
            pltpu.VMEM(field.shape, jnp.float32),
            pltpu.VMEM(field.shape, jnp.float32),
            pltpu.VMEM((2, 8 * slots, width), jnp.float32),
            pltpu.SemaphoreType.DMA((3,)),
        ],
        compiler_params=params(8),
        name="edges",
    )(*in_hbm(rows, field, adjoint))


def column(meta, n):
    return meta[:, n : n + 1]


def couple(rows_ref, change, coupling):
    parts, cells_z, cells_x = coupling.shape[0] // 2, coupling.shape[1] - 1, coupling.shape[2]

    def put(k, carry):
        index = rows_ref[k]
        z, x, part = place(jnp.maximum(index, 0), cells_x, parts)
        z = jnp.where(index >= 0, z, cells_z)
        for side in range(2):
            coupling[side * parts + part, z, pl.ds(x, 1), :] = change[side, pl.ds(k, 1), :]
        return carry

    lax.fori_loop(0, change.shape[1], put, 0, unroll=8)


def inner_planes(cells_z, plane):
    def inner(z, carry):
        plane(z, lambda side, now: now[z - 1], lambda side, now: now[z + 1])
        return carry

    lax.fori_loop(1, cells_z - 1, inner, 0, unroll=UNROLL)


def stencil(cells, before, speed, beside, low, high, extra):
    cells_x, along = cells.shape
    row_id = lax.broadcasted_iota(jnp.int32, cells.shape, 0)
    lane_id = lax.broadcasted_iota(jnp.int32, cells.shape, 1)
    low = 0.0 if low is None else low
    high = 0.0 if high is None else high
    beside = beside + jnp.where(row_id == 0, low, pltpu.roll(cells, 1, axis=0))
    beside = beside + jnp.where(row_id == cells_x - 1, high, pltpu.roll(cells, cells_x - 1, axis=0))
    beside = beside + jnp.where(lane_id == 0, 0.0, pltpu.roll(cells, 1, axis=1))
    beside = beside + jnp.where(lane_id == along - 1, 0.0, pltpu.roll(cells, along - 1, axis=1))
    return 2.0 * cells - before + speed * (beside - 6.0 * cells) + extra


def step_kernel(step, *refs):
    ahead = step == STEPS - 2
    loads = []
    rows_ref, field, field_prev, adjoint, adjoint_prev, speed2 = refs[:6]
    x_from_outer, x_from_inner, z_from_outer, z_from_inner, lines, picked = refs[6:12]
    pushes = refs[12 : 13 + step]
    refs = refs[13 + step :]
    if ahead:
        x_outer, x_inner, z_outer, z_inner, speed_low, speed_high, gradient_out = refs[:7]
        partial_hbm = refs[7:9]
        coupling, change, tiles, field_out, adjoint_out, push_out, picked_out = refs[9:16]
        partial, sems = refs[16:18], refs[18]
    else:
        field_out, adjoint_out, x_outer, x_inner, z_outer, z_inner, push_out, picked_out = refs[:8]
        refs = refs[8:]
        if step == 0:
            sources = (field, adjoint, speed2, field_prev, adjoint_prev)
            field, adjoint, speed2 = refs[:3]
            refs = refs[3:]
            field_prev, adjoint_prev, load_sems = refs[3:]
            targets = (field, adjoint, speed2, field_prev, adjoint_prev)
            loads = [
                pltpu.make_async_copy(source, target, load_sems.at[i])
                for i, (source, target) in enumerate(zip(sources, targets))
            ]
        coupling, change, tiles = refs[:3]
    for copy in loads:
        copy.start()

    cells_z, cells_x, along = field.shape
    slots, width = change.shape[1:]
    parts = along // width
    meta = lines[pl.ds(META, slots, stride=LINES), :]

    def line(n):
        return lines[pl.ds(n - 1, slots, stride=LINES), :]

    scalars = [None] + [column(meta, n) for n in range(1, TERMS + 1)]

    def surfaces(at, known):
        found = []
        for side in range(2):
            new = line(at + 1) if side == 0 else None
            for t in range(at + 1):
                term = scalars[at + 1 - t] * known[t][side]
                new = term if new is None else new + term
            found.append(new)
        return found

    def extra(side, z):
        return jnp.concatenate([coupling[side * parts + part, z] for part in range(parts)], axis=1)

    surface = surfaces(step, pushes)
    for side in range(2):
        change[side] = BETA * (surface[side] - picked[side])
    coupling[...] = jnp.zeros_like(coupling)
    couple(rows_ref, change, coupling)
    for copy in loads:
        copy.wait()

    z_halo = [incoming("gz", z_from_outer[side], z_from_inner[side]) for side in range(2)]

    def plane(z, below, above):
        speed = speed2[z]
        for side, (now, before, out) in enumerate(
            ((field, field_prev, field_out), (adjoint, adjoint_prev, adjoint_out))
        ):
            low, high = incoming(
                "gx", side_row(x_from_outer, side, z), side_row(x_from_inner, side, z)
            )
            beside = below(side, now) + above(side, now)
            new = stencil(now[z], before[z], speed, beside, low, high, extra(side, z))
            out[z] = new
            keep_sides(new, side, z, x_outer, x_inner)

    plane(
        0,
        lambda side, now: z_halo[side][0],
        lambda side, now: now[1],
    )
    inner_planes(cells_z, plane)
    plane(
        cells_z - 1,
        lambda side, now: now[cells_z - 2],
        lambda side, now: z_halo[side][1],
    )
    for side, out in enumerate((field_out, adjoint_out)):
        z_outer[side], z_inner[side] = outgoing("gz", out[0], out[cells_z - 1])
    pick(rows_ref, (field_out, adjoint_out), picked_out, tiles)
    for side in range(2):
        push_out[side] = KAPPA * (picked_out[side] - surface[side])
    if not ahead:
        return

    known = [*pushes, push_out]
    total = jnp.zeros((slots, width), jnp.float32)
    for late in range(STEPS):
        inside = (STEPS - late) * line(TERMS - late)
        for t in range(STEPS - late):
            inside = inside + ((STEPS - late - t) * scalars[TERMS - late - t]) * known[t][0]
        total = total + known[late][1] * inside
    patches = gradient_out.shape[0]
    ids = column(meta, 0).astype(jnp.int32)
    owners = lax.broadcasted_iota(jnp.int32, (slots, patches), 1) == ids
    gradient_out[...] = lax.dot_general(
        owners.astype(jnp.float32),
        total,
        (((0,), (0,)), ((), ())),
        precision=lax.Precision.HIGHEST,
        preferred_element_type=jnp.float32,
    )

    surface = surfaces(step + 1, known)
    for side in range(2):
        change[side] = BETA * (surface[side] - picked_out[side])
    couple(rows_ref, change, coupling)

    def next_plane(z, below, above):
        speed = speed2[z]
        keep_side(speed, z, speed_low, speed_high)
        for side, (now, before, out) in enumerate(
            ((field_out, field, partial[0]), (adjoint_out, adjoint, partial[1]))
        ):
            beside = below(side, now) + above(side, now)
            out[z] = stencil(now[z], before[z], speed, beside, None, None, extra(side, z))

    next_plane(0, lambda side, now: 0.0, lambda side, now: now[1])
    inner_planes(cells_z, next_plane)
    next_plane(cells_z - 1, lambda side, now: now[cells_z - 2], lambda side, now: 0.0)
    copies = [pltpu.make_async_copy(partial[i], partial_hbm[i], sems.at[i]) for i in range(2)]
    for copy in copies:
        copy.start()
    for copy in copies:
        copy.wait()


def step_call(step, rows, field, field_prev, adjoint, adjoint_prev, speed2, halos, lines, picked, pushes, patches):
    slots, width = pushes[0].shape[1:]
    ahead = step == STEPS - 2
    cells_z, cells_x, along = field.shape
    parts = along // width
    whole = jax.ShapeDtypeStruct(field.shape, jnp.float32)
    edges = edge_shapes(field, slots, width)
    in_vmem = pl.BlockSpec(memory_space=VMEM)
    scratch = [
        pltpu.VMEM((2 * parts, cells_z + 1, cells_x, width), jnp.float32),
        pltpu.VMEM((2, slots, width), jnp.float32),
        pltpu.VMEM((2, 8 * slots, width), jnp.float32),
    ]
    if ahead:
        sides = jax.ShapeDtypeStruct((parts, cells_z, width), jnp.float32)
        shapes = edges[:4] + [sides, sides, jax.ShapeDtypeStruct((patches, width), jnp.float32)]
        out_specs = [in_vmem] * 7 + [pl.BlockSpec(memory_space=HBM)] * 2
        shapes = shapes + [HBM(field.shape, jnp.float32)] * 2
        scratch = scratch + [pltpu.VMEM(field.shape, jnp.float32)] * 2
        scratch = scratch + [pltpu.VMEM((2, slots, width), jnp.float32)] * 2
        scratch = scratch + [pltpu.VMEM(field.shape, jnp.float32)] * 2
        scratch = scratch + [pltpu.SemaphoreType.DMA((2,))]
    else:
        shapes = [whole] * 2 + edges
        if step == 0:
            shapes = shapes + [whole] * 3
            scratch = scratch + [pltpu.VMEM(field.shape, jnp.float32)] * 2
            scratch = scratch + [pltpu.SemaphoreType.DMA((5,))]
        out_specs = [in_vmem] * len(shapes)
    arrays = [field, field_prev, adjoint, adjoint_prev, speed2]
    if step == 0:
        arrays = in_hbm(*arrays)
    operands = [*arrays, *halos, lines, picked, *pushes]
    return pl.pallas_call(
        functools.partial(step_kernel, step),
        in_specs=[pl.BlockSpec(memory_space=SMEM)]
        + [pl.BlockSpec(memory_space=HBM) if step == 0 else in_vmem] * 5
        + [in_vmem] * (len(operands) - 5),
        out_specs=out_specs,
        out_shape=shapes,
        scratch_shapes=scratch,
        compiler_params=params(16),
        name=f"step{step}",
    )(rows, *operands)


def keep_side(cells, z, x_low, x_high):
    last_x, width = cells.shape[0] - 1, x_low.shape[2]
    for part in range(x_low.shape[0]):
        lanes = slice(part * width, (part + 1) * width)
        x_low[part, pl.ds(z, 1), :] = cells[0:1, lanes]
        x_high[part, pl.ds(z, 1), :] = cells[last_x : last_x + 1, lanes]


def finish_kernel(field, adjoint, speed_z_low, speed_z_high, speed_low, speed_high, x_from_outer, x_from_inner, z_from_outer, z_from_inner, field_out, adjoint_out):
    block, cells_x, along = field.shape
    row_id = lax.broadcasted_iota(jnp.int32, (cells_x, along), 0)
    step, steps = pl.program_id(0), pl.num_programs(0)

    def speeds(side_plane, z):
        parts = side_plane.shape[0]
        return jnp.concatenate([side_plane[p, pl.ds(z, 1), :] for p in range(parts)], axis=1)

    for side, (partial, out) in enumerate(((field, field_out), (adjoint, adjoint_out))):
        for z in range(block):
            low, high = incoming(
                "gx", side_row(x_from_outer, side, z), side_row(x_from_inner, side, z)
            )
            low, high = low * speeds(speed_low, z), high * speeds(speed_high, z)
            added = jnp.where(row_id == 0, low, jnp.where(row_id == cells_x - 1, high, 0.0))
            out[z] = partial[z] + added

        before, after = incoming("gz", z_from_outer[side], z_from_inner[side])

        @pl.when(step == 0)
        def _():
            out[0] = out[0] + speed_z_low[0] * before

        @pl.when(step == steps - 1)
        def _():
            out[block - 1] = out[block - 1] + speed_z_high[0] * after


def finish_call(field, adjoint, speed2, speed_low, speed_high, halos):
    cells_z, cells_x, along = field.shape
    parts, _, width = speed_low.shape
    block = 8
    planes = pl.BlockSpec((block, cells_x, along), lambda i: (i, 0, 0))
    sides = pl.BlockSpec((parts, block, width), lambda i: (0, i, 0))
    both = pl.BlockSpec((2, parts, block, width), lambda i: (0, 0, i, 0))
    edge = pl.BlockSpec((2, cells_x, along), lambda i: (0, 0, 0))
    return pl.pallas_call(
        finish_kernel,
        grid=(cells_z // block,),
        in_specs=[
            planes,
            planes,
            pl.BlockSpec((1, cells_x, along), lambda i: (0, 0, 0)),
            pl.BlockSpec((1, cells_x, along), lambda i: (cells_z - 1, 0, 0)),
            sides,
            sides,
            both,
            both,
            edge,
            edge,
        ],
        out_specs=[planes, planes],
        out_shape=[jax.ShapeDtypeStruct(field.shape, jnp.float32)] * 2,
        compiler_params=params(8),
        name="finish",
    )(*in_hbm(field, adjoint), speed2, speed2, speed_low, speed_high, *halos)


def swaps(axis, first):
    count = lax.axis_size(axis)
    if first:
        return [(i, i ^ 1) for i in range(count)]
    return [(i, (i + 1 if i % 2 else i - 1) % count) for i in range(count)]


def exchange(edges):
    axes = (("gx", False), ("gx", True), ("gz", False), ("gz", True))
    return [lax.ppermute(edge, axis, swaps(axis, first)) for edge, (axis, first) in zip(edges, axes)]


def body(
    pressure_now,
    pressure_prev,
    adjoint_now,
    adjoint_prev,
    speed2,
    layer_state,
    layer_maps,
    send_rows,
    slot_patch,
    patch_material,
):
    slots, _, width = layer_state.shape
    patches = patch_material.shape[0]
    devices = lax.axis_size(("gx", "gz"))
    rows = send_rows.reshape(-1)

    lines = surface_rows(layer_maps, slot_patch, patch_material, layer_state)
    lines = lax.all_to_all(lines, ("gx", "gz"), split_axis=0, concat_axis=0, tiled=True)
    lines = lines.reshape(slots * LINES, width)

    results = first_edges(rows, pressure_now, adjoint_now, slots, width)
    fields = (pressure_now, pressure_prev, adjoint_now, adjoint_prev)
    speed = speed2
    halos = exchange(results[:4])
    pushes, picked = [results[4]], results[5]
    for step in range(STEPS - 1):
        results = step_call(step, rows, *fields, speed, halos, lines, picked, pushes, patches)
        if step < STEPS - 2:
            if step == 0:
                fields, speed = (results[8], None, results[9], None), results[10]
            fields = (results[0], fields[0], results[1], fields[2])
            halos = exchange(results[2:6])
            pushes.append(results[6])
            picked = results[7]
    speed_low, speed_high, gradient, *partial = results[4:]
    parts = gradient.reshape(devices, patches // devices, width)
    parts = lax.all_to_all(parts, ("gx", "gz"), split_axis=0, concat_axis=0, tiled=True)
    halos = exchange(results[:4])
    field, adjoint = finish_call(*partial, speed2, speed_low, speed_high, halos)
    return field, adjoint, jnp.sum(parts, axis=0)


def solution(mesh):
    grid = P("gz", "gx", None)
    split = P(("gx", "gz"), None, None)
    in_specs = (grid, grid, grid, grid, grid, split, P(), split, P(("gx", "gz")), P())
    out_specs = (grid, grid, P(("gx", "gz"), None))
    return jax.shard_map(body, mesh=mesh, in_specs=in_specs, out_specs=out_specs, check_vma=False)
```

```python
import functools

import jax
import jax.numpy as jnp
from jax import lax
from jax.experimental import pallas as pl
from jax.experimental.pallas import tpu as pltpu
from jax.sharding import PartitionSpec as P

STEPS = 4
KAPPA = 0.5
BETA = 0.3
TERMS = STEPS + 1
LINES = 8
META = TERMS
MIB = 1 << 20
VMEM = pltpu.VMEM
SMEM = pltpu.SMEM
HBM = pltpu.HBM
UNROLL = 10


def in_hbm(*arrays):
    return [pltpu.with_memory_space_constraint(array, HBM) for array in arrays]


def params(mib):
    return pltpu.CompilerParams(vmem_limit_bytes=mib * MIB)


def surface_kernel(maps_hbm, patch_hbm, material_hbm, layer_hbm, out, maps, patch_ref, material_ref, layer, vectors, scalars, sems):
    mats, _, depth = maps.shape
    slots, _, width = layer.shape
    chunks = sems.shape[0] - 3
    block = slots // chunks
    small = [
        pltpu.make_async_copy(maps_hbm, maps, sems.at[chunks]),
        pltpu.make_async_copy(patch_hbm, patch_ref, sems.at[chunks + 1]),
        pltpu.make_async_copy(material_hbm, material_ref, sems.at[chunks + 2]),
    ]
    large = [
        pltpu.make_async_copy(
            layer_hbm.at[pl.ds(i * block, block)], layer.at[pl.ds(i * block, block)], sems.at[i]
        )
        for i in range(chunks)
    ]
    for copy in small + large:
        copy.start()

    lane = lax.broadcasted_iota(jnp.int32, (1, width), 1)
    first = lax.broadcasted_iota(jnp.int32, (depth, 1), 0) == 0
    small[0].wait()
    matrices = [maps[mat] for mat in range(mats)]
    turned = [matrix.T for matrix in matrices]
    rows = [matrix[0:1, :] for matrix in matrices]
    cols = [matrix[:, 0:1] for matrix in turned]
    kept = [jnp.zeros((1, width), jnp.float32)] * mats
    for n in range(TERMS):
        for mat in range(mats):
            if n > 0:
                rows[mat], cols[mat] = (
                    jnp.sum(matrices[mat] * cols[mat], axis=0, keepdims=True),
                    jnp.sum(turned[mat] * rows[mat], axis=1, keepdims=True),
                )
            scaled = jnp.where(first, (1.0 - KAPPA) * cols[mat], cols[mat])
            vectors[mat, n] = jnp.broadcast_to(scaled, (depth, width))
            kept[mat] = jnp.where(lane == n + 1, cols[mat][0:1, 0:1], kept[mat])
    for mat in range(mats):
        scalars[mat] = jnp.broadcast_to(kept[mat], (8, width))
    small[1].wait()
    small[2].wait()

    def one(j, carry):
        patch = patch_ref[j]
        mat = material_ref[patch]
        sums = [jnp.zeros((8, width), jnp.float32)] * TERMS
        for c in range(depth // 8):
            part = layer[j, pl.ds(8 * c, 8), :]
            sums = [
                s + vectors[mat, n, pl.ds(8 * c, 8), :] * part for n, s in enumerate(sums)
            ]
        rows = [jnp.sum(s, axis=0, keepdims=True) for s in sums]
        scalar_row = jnp.where(lane == 0, patch.astype(jnp.float32), scalars[mat][0:1, :])
        rows.append(scalar_row)
        rows.extend([jnp.zeros((1, width), jnp.float32)] * (LINES - len(rows)))
        out[j] = jnp.concatenate(rows, axis=0)
        return carry

    for i in range(chunks):
        large[i].wait()
        lax.fori_loop(i * block, (i + 1) * block, one, 0, unroll=4)


def surface_rows(layer_maps, slot_patch, patch_material, layer_state):
    slots, depth, width = layer_state.shape
    mats = layer_maps.shape[0]
    chunks = 4
    return pl.pallas_call(
        surface_kernel,
        in_specs=[pl.BlockSpec(memory_space=HBM)] * 4,
        out_specs=pl.BlockSpec(memory_space=VMEM),
        out_shape=jax.ShapeDtypeStruct((slots, LINES, width), jnp.float32),
        scratch_shapes=[
            pltpu.VMEM((mats, depth, depth), jnp.float32),
            pltpu.SMEM(slot_patch.shape, jnp.int32),
            pltpu.SMEM(patch_material.shape, jnp.int32),
            pltpu.VMEM((slots, depth, width), jnp.float32),
            pltpu.VMEM((mats, TERMS, depth, width), jnp.float32),
            pltpu.VMEM((mats, 8, width), jnp.float32),
            pltpu.SemaphoreType.DMA((chunks + 3,)),
        ],
        compiler_params=params(24),
        name="surface_rows",
    )(*in_hbm(layer_maps, slot_patch, patch_material, layer_state))


def place(index, cells_x, parts):
    low, middle = parts.bit_length() - 1, cells_x.bit_length() - 1
    return (
        jnp.right_shift(index, low + middle),
        jnp.bitwise_and(jnp.right_shift(index, low), cells_x - 1),
        jnp.bitwise_and(index, parts - 1),
    )


def pick(rows_ref, fields, picked, tiles):
    cells_x = fields[0].shape[1]
    slots, width = picked.shape[1:]
    parts = fields[0].shape[2] // width

    def fetch(k, carry):
        z, x, part = place(jnp.maximum(rows_ref[k], 0), cells_x, parts)
        lines = pl.ds(pl.multiple_of(jnp.bitwise_and(x, -8), 8), 8)
        lanes = pl.ds(pl.multiple_of(part * width, width), width)
        for side, field in enumerate(fields):
            tiles[side, pl.ds(pl.multiple_of(8 * k, 8), 8), :] = field[z, lines, lanes]
        return carry

    lax.fori_loop(0, slots, fetch, 0, unroll=8)

    def choose(k, carry):
        index = rows_ref[k]
        line = 8 * k + jnp.bitwise_and(place(jnp.maximum(index, 0), cells_x, parts)[1], 7)
        for side in range(len(fields)):
            row = tiles[side, pl.ds(line, 1), :]
            picked[side, pl.ds(k, 1), :] = jnp.where(index >= 0, row, 0.0)
        return carry

    lax.fori_loop(0, slots, choose, 0, unroll=8)


def even(axis):
    return lax.axis_index(axis) % 2 == 0


def at_start(axis):
    return lax.axis_index(axis) == 0


def at_end(axis):
    return lax.axis_index(axis) == lax.axis_size(axis) - 1


def outgoing(axis, low, high):
    choice = even(axis)
    return jnp.where(choice, low, high), jnp.where(choice, high, low)


def incoming(axis, outer, inner):
    choice = even(axis)
    before = jnp.where(at_start(axis), 0.0, jnp.where(choice, outer, inner))
    after = jnp.where(at_end(axis), 0.0, jnp.where(choice, inner, outer))
    return before, after


def keep_sides(cells, side, z, x_outer, x_inner):
    last_x, width = cells.shape[0] - 1, x_outer.shape[3]
    for part in range(x_outer.shape[1]):
        lanes = slice(part * width, (part + 1) * width)
        x_outer[side, part, pl.ds(z, 1), :], x_inner[side, part, pl.ds(z, 1), :] = outgoing(
            "gx", cells[0:1, lanes], cells[last_x : last_x + 1, lanes]
        )


def side_row(plane, side, z):
    parts = plane.shape[1]
    return jnp.concatenate([plane[side, part, pl.ds(z, 1), :] for part in range(parts)], axis=1)


def keep_edges(z_planes, side, z_outer, z_inner):
    z_outer[side], z_inner[side] = outgoing("gz", *z_planes)


def edges_kernel(field_hbm, adjoint_hbm, x_outer, x_inner, z_outer, z_inner, field, adjoint, sems):
    copies = [
        pltpu.make_async_copy(field_hbm, field, sems.at[0]),
        pltpu.make_async_copy(adjoint_hbm, adjoint, sems.at[1]),
    ]
    for copy in copies:
        copy.start()
    for side, array in enumerate((field, adjoint)):
        copies[side].wait()

        def one(z, carry):
            keep_sides(array[z], side, z, x_outer, x_inner)
            return carry

        lax.fori_loop(0, array.shape[0], one, 0, unroll=8)
        keep_edges((array[0], array[array.shape[0] - 1]), side, z_outer, z_inner)


def edge_shapes(field, width):
    cells_z, cells_x, along = field.shape
    f32 = jnp.float32
    x_shape = jax.ShapeDtypeStruct((2, along // width, cells_z, width), f32)
    z_shape = jax.ShapeDtypeStruct((2, cells_x, along), f32)
    return [x_shape, x_shape, z_shape, z_shape]


def first_edges(field, adjoint, width):
    return pl.pallas_call(
        edges_kernel,
        in_specs=[pl.BlockSpec(memory_space=HBM)] * 2,
        out_specs=[pl.BlockSpec(memory_space=VMEM)] * 4,
        out_shape=edge_shapes(field, width),
        scratch_shapes=[
            pltpu.VMEM(field.shape, jnp.float32),
            pltpu.VMEM(field.shape, jnp.float32),
            pltpu.SemaphoreType.DMA((2,)),
        ],
        compiler_params=params(8),
        name="edges",
    )(*in_hbm(field, adjoint))


def couple(rows_ref, change, coupling):
    parts, cells_z, cells_x = coupling.shape[0] // 2, coupling.shape[1] - 1, coupling.shape[2]

    def put(k, carry):
        index = rows_ref[k]
        z, x, part = place(jnp.maximum(index, 0), cells_x, parts)
        z = jnp.where(index >= 0, z, cells_z)
        for side in range(2):
            coupling[side * parts + part, z, pl.ds(x, 1), :] = change[side, pl.ds(k, 1), :]
        return carry

    lax.fori_loop(0, change.shape[1], put, 0, unroll=8)


def local_planes(fields, befores, outs, speed2, extra, sends=None):
    cells_z = speed2.shape[0]

    def plane(z, below, above):
        speed = speed2[z]
        for side in range(2):
            now = fields[side]
            beside = below(now) + above(now)
            outs[side][z] = stencil(now[z], befores[side][z], speed, beside, extra(side, z))

    def inner(z, carry):
        plane(z, lambda now: now[z - 1], lambda now: now[z + 1])
        return carry

    plane(0, lambda now: 0.0, lambda now: now[1])
    plane(cells_z - 1, lambda now: now[cells_z - 2], lambda now: 0.0)
    shares = len(sends) if sends else 1
    share = cells_z // shares
    for i in range(shares):
        start, stop = max(i * share, 1), min((i + 1) * share, cells_z - 1)
        lax.fori_loop(start, stop, inner, 0, unroll=(stop - start) // -(-(stop - start) // UNROLL))
        for send in sends[i] if sends else ():
            send.start()


def stencil(cells, before, speed, beside, extra):
    cells_x, along = cells.shape
    row_id = lax.broadcasted_iota(jnp.int32, cells.shape, 0)
    lane_id = lax.broadcasted_iota(jnp.int32, cells.shape, 1)
    beside = beside + jnp.where(row_id == 0, 0.0, pltpu.roll(cells, 1, axis=0))
    beside = beside + jnp.where(row_id == cells_x - 1, 0.0, pltpu.roll(cells, cells_x - 1, axis=0))
    beside = beside + jnp.where(lane_id == 0, 0.0, pltpu.roll(cells, 1, axis=1))
    beside = beside + jnp.where(lane_id == along - 1, 0.0, pltpu.roll(cells, along - 1, axis=1))
    return 2.0 * cells - before + speed * (beside - 6.0 * cells) + extra


def shares_of(source, target, sems, first, count):
    share = source.shape[0] // count
    return [
        pltpu.make_async_copy(
            source.at[pl.ds(i * share, share)], target.at[pl.ds(i * share, share)], sems.at[first + i]
        )
        for i in range(count)
    ]


class Lines:
    def __init__(self, ref, slots):
        self.ref, self.slots = ref, slots
        self.meta = self.row(META + 1)

    def row(self, n):
        return self.ref[pl.ds(n - 1, self.slots, stride=LINES), :]

    def scalar(self, n):
        return self.meta[:, n : n + 1]

    def surface(self, step, pushes, side):
        new = self.row(step + 1) if side == 0 else None
        for t in range(step + 1):
            term = self.scalar(step + 1 - t) * pushes[t][side]
            new = term if new is None else new + term
        return new


def extra_of(coupling, side, z):
    parts = coupling.shape[0] // 2
    return jnp.concatenate([coupling[side * parts + part, z] for part in range(parts)], axis=1)


def couple_step(rows_ref, lines, step, pushes, picked, surface, change, coupling):
    for side in range(2):
        surface[side] = lines.surface(step, pushes, side)
        change[side] = BETA * (surface[side] - picked[side])
    couple(rows_ref, change, coupling)


def x_added(speed_first, speed_last, from_outer, from_inner, side, z, shape):
    row_id = lax.broadcasted_iota(jnp.int32, shape, 0)
    low, high = incoming("gx", side_row(from_outer, side, z), side_row(from_inner, side, z))
    low, high = speed_first * low, speed_last * high
    return jnp.where(row_id == 0, low, jnp.where(row_id == shape[0] - 1, high, 0.0))


def border_planes(partials, speed2, halos, outs, edges, extra):
    x_from_outer, x_from_inner, z_from_outer, z_from_inner = halos
    x_outer, x_inner, z_outer, z_inner = edges
    cells_z, cells_x, along = speed2.shape

    def plane(z, side, more):
        first, last = speed2[z, 0:1, :], speed2[z, cells_x - 1 : cells_x, :]
        new = partials[side][z] + x_added(
            first, last, x_from_outer, x_from_inner, side, z, (cells_x, along)
        )
        if extra is not None:
            new = new + extra(side, z)
        if more is not None:
            new = new + speed2[z] * more
        outs[side][z] = new
        keep_sides(new, side, z, x_outer, x_inner)
        return new

    for side in range(2):
        before, after = incoming("gz", z_from_outer[side], z_from_inner[side])
        ends = plane(0, side, before), plane(cells_z - 1, side, after)
        keep_edges(ends, side, z_outer, z_inner)

    def inner(z, carry):
        for side in range(2):
            plane(z, side, None)
        return carry

    lax.fori_loop(1, cells_z - 1, inner, 0, unroll=UNROLL)


def first_local_kernel(rows_hbm, field_hbm, field_prev_hbm, adjoint_hbm, adjoint_prev_hbm, speed2_hbm, out_hbm, adjoint_out_hbm, push, picked, rows_ref, field, field_prev, adjoint, adjoint_prev, speed2, out, adjoint_out, tiles, sems):
    loads = [
        pltpu.make_async_copy(source, target, sems.at[i])
        for i, (source, target) in enumerate(
            (
                (rows_hbm, rows_ref),
                (field_hbm, field),
                (adjoint_hbm, adjoint),
                (speed2_hbm, speed2),
                (field_prev_hbm, field_prev),
                (adjoint_prev_hbm, adjoint_prev),
            )
        )
    ]
    for copy in loads:
        copy.start()
    for copy in loads[:3]:
        copy.wait()
    pick(rows_ref, (field, adjoint), picked, tiles)
    push[...] = KAPPA * picked[...]
    for copy in loads[3:]:
        copy.wait()
    sends = list(
        zip(
            shares_of(out, out_hbm, sems, 6, 4), shares_of(adjoint_out, adjoint_out_hbm, sems, 10, 4)
        )
    )
    local_planes(
        (field, adjoint),
        (field_prev, adjoint_prev),
        (out, adjoint_out),
        speed2,
        lambda side, z: 0.0,
        sends,
    )
    for pair in sends:
        for send in pair:
            send.wait()


def first_local(rows, field, field_prev, adjoint, adjoint_prev, speed2, slots, width):
    rows_shape = jax.ShapeDtypeStruct((2, slots, width), jnp.float32)
    return pl.pallas_call(
        first_local_kernel,
        in_specs=[pl.BlockSpec(memory_space=HBM)] * 6,
        out_specs=[pl.BlockSpec(memory_space=HBM)] * 2 + [pl.BlockSpec(memory_space=VMEM)] * 2,
        out_shape=[HBM(field.shape, jnp.float32)] * 2 + [rows_shape] * 2,
        scratch_shapes=[pltpu.SMEM((slots,), jnp.int32)]
        + [pltpu.VMEM(field.shape, jnp.float32)] * 7
        + [pltpu.VMEM((2, 8 * slots, width), jnp.float32), pltpu.SemaphoreType.DMA((14,))],
        compiler_params=params(16),
        cost_estimate=pl.CostEstimate(flops=8 << 20, bytes_accessed=12 << 20, transcendentals=0),
        name="local0",
    )(*in_hbm(rows, field, field_prev, adjoint, adjoint_prev, speed2))


def first_border_kernel(rows_ref, partial_hbm, partial_adjoint_hbm, field_hbm, adjoint_hbm, speed2_hbm, x_from_outer, x_from_inner, z_from_outer, z_from_inner, lines_ref, push, picked, out, adjoint_out, field, adjoint, speed2, x_outer, x_inner, z_outer, z_inner, surface, partial, partial_adjoint, coupling, change, sems):
    loads = [
        pltpu.make_async_copy(source, target, sems.at[i])
        for i, (source, target) in enumerate(
            (
                (speed2_hbm, speed2),
                (partial_hbm, partial),
                (partial_adjoint_hbm, partial_adjoint),
                (field_hbm, field),
                (adjoint_hbm, adjoint),
            )
        )
    ]
    for copy in loads:
        copy.start()
    coupling[...] = jnp.zeros_like(coupling)
    lines = Lines(lines_ref, change.shape[1])
    couple_step(rows_ref, lines, 0, [push], picked, surface, change, coupling)
    for copy in loads[:3]:
        copy.wait()
    border_planes(
        (partial, partial_adjoint),
        speed2,
        (x_from_outer, x_from_inner, z_from_outer, z_from_inner),
        (out, adjoint_out),
        (x_outer, x_inner, z_outer, z_inner),
        functools.partial(extra_of, coupling),
    )
    for copy in loads[3:]:
        copy.wait()


def coupling_scratch(field, slots, width):
    cells_z, cells_x, along = field.shape
    return [
        pltpu.VMEM((2 * (along // width), cells_z + 1, cells_x, width), jnp.float32),
        pltpu.VMEM((2, slots, width), jnp.float32),
    ]


def first_border(rows, partials, field, adjoint, speed2, halos, lines, push, picked):
    _, slots, width = push.shape
    whole = jax.ShapeDtypeStruct(field.shape, jnp.float32)
    in_vmem = pl.BlockSpec(memory_space=VMEM)
    return pl.pallas_call(
        first_border_kernel,
        in_specs=[pl.BlockSpec(memory_space=SMEM)]
        + [pl.BlockSpec(memory_space=HBM)] * 5
        + [in_vmem] * 7,
        out_specs=[in_vmem] * 10,
        out_shape=[whole] * 5
        + edge_shapes(field, width)
        + [jax.ShapeDtypeStruct((2, slots, width), jnp.float32)],
        scratch_shapes=[pltpu.VMEM(field.shape, jnp.float32)] * 2
        + coupling_scratch(field, slots, width)
        + [pltpu.SemaphoreType.DMA((5,))],
        compiler_params=params(12),
        name="border0",
    )(rows, *in_hbm(*partials, field, adjoint, speed2), *halos, lines, push, picked)


def local_kernel(step, rows_ref, field, field_prev, adjoint, adjoint_prev, speed2, lines_ref, surface, *refs):
    pushes, refs = list(refs[:step]), refs[step:]
    out, adjoint_out, push, next_surface, coupling, change, tiles, picked = refs
    pick(rows_ref, (field, adjoint), picked, tiles)
    push[...] = KAPPA * (picked[...] - surface[...])
    coupling[...] = jnp.zeros_like(coupling)
    lines = Lines(lines_ref, change.shape[1])
    couple_step(rows_ref, lines, step, pushes + [push], picked, next_surface, change, coupling)
    local_planes(
        (field, adjoint),
        (field_prev, adjoint_prev),
        (out, adjoint_out),
        speed2,
        functools.partial(extra_of, coupling),
    )


def local_step(step, rows, field, field_prev, adjoint, adjoint_prev, speed2, lines, surface, pushes):
    _, slots, width = surface.shape
    whole = jax.ShapeDtypeStruct(field.shape, jnp.float32)
    rows_shape = jax.ShapeDtypeStruct(surface.shape, jnp.float32)
    in_vmem = pl.BlockSpec(memory_space=VMEM)
    return pl.pallas_call(
        functools.partial(local_kernel, step),
        in_specs=[pl.BlockSpec(memory_space=SMEM)] + [in_vmem] * (7 + step),
        out_specs=[in_vmem] * 4,
        out_shape=[whole, whole, rows_shape, rows_shape],
        scratch_shapes=coupling_scratch(field, slots, width)
        + [
            pltpu.VMEM((2, 8 * slots, width), jnp.float32),
            pltpu.VMEM((2, slots, width), jnp.float32),
        ],
        compiler_params=params(8),
        cost_estimate=pl.CostEstimate(flops=8 << 20, bytes_accessed=12 << 20, transcendentals=0),
        name=f"local{step}",
    )(rows, field, field_prev, adjoint, adjoint_prev, speed2, lines, surface, *pushes)


def border_kernel(partial, partial_adjoint, speed2, x_from_outer, x_from_inner, z_from_outer, z_from_inner, out, adjoint_out, *edges):
    border_planes(
        (partial, partial_adjoint),
        speed2,
        (x_from_outer, x_from_inner, z_from_outer, z_from_inner),
        (out, adjoint_out),
        edges,
        None,
    )


def border_step(step, partials, speed2, halos, width):
    field = partials[0]
    whole = jax.ShapeDtypeStruct(field.shape, jnp.float32)
    in_vmem = pl.BlockSpec(memory_space=VMEM)
    return pl.pallas_call(
        border_kernel,
        in_specs=[in_vmem] * 7,
        out_specs=[in_vmem] * 6,
        out_shape=[whole, whole] + edge_shapes(field, width),
        compiler_params=params(8),
        name=f"border{step}",
    )(*partials, speed2, *halos)


def ahead_kernel(rows_ref, partial, partial_adjoint, field_prev, adjoint_prev, speed2, x_from_outer, x_from_inner, z_from_outer, z_from_inner, lines_ref, surface, *refs):
    pushes, refs = list(refs[: STEPS - 1]), refs[STEPS - 1 :]
    x_outer, x_inner, z_outer, z_inner, speed_first, speed_last, speed_ends, gradient = refs[:8]
    next_hbm, next_adjoint_hbm, coupling, change, tiles, picked, push, next_surface = refs[8:16]
    field, adjoint, out, adjoint_out, sems = refs[16:]
    cells_z, cells_x, _ = speed2.shape
    coupling[...] = jnp.zeros_like(coupling)
    border_planes(
        (partial, partial_adjoint),
        speed2,
        (x_from_outer, x_from_inner, z_from_outer, z_from_inner),
        (field, adjoint),
        (x_outer, x_inner, z_outer, z_inner),
        None,
    )
    speed_ends[0], speed_ends[1] = speed2[0], speed2[cells_z - 1]

    def sides(z, carry):
        keep_side(speed2[z], z, speed_first, speed_last)
        return carry

    lax.fori_loop(0, cells_z, sides, 0, unroll=8)
    pick(rows_ref, (field, adjoint), picked, tiles)
    push[...] = KAPPA * (picked[...] - surface[...])

    slots = change.shape[1]
    lines = Lines(lines_ref, slots)
    known = pushes + [push]
    total = jnp.zeros(change.shape[1:], jnp.float32)
    for late in range(STEPS):
        inside = (STEPS - late) * lines.row(TERMS - late)
        for t in range(STEPS - late):
            scale = (STEPS - late - t) * lines.scalar(TERMS - late - t)
            inside = inside + scale * known[t][0]
        total = total + known[late][1] * inside
    ids = lines.scalar(0).astype(jnp.int32)
    owners = lax.broadcasted_iota(jnp.int32, (slots, gradient.shape[0]), 1) == ids
    gradient[...] = lax.dot_general(
        owners.astype(jnp.float32),
        total,
        (((0,), (0,)), ((), ())),
        precision=lax.Precision.HIGHEST,
        preferred_element_type=jnp.float32,
    )

    couple_step(rows_ref, lines, STEPS - 1, known, picked, next_surface, change, coupling)
    sends = list(
        zip(shares_of(out, next_hbm, sems, 0, 4), shares_of(adjoint_out, next_adjoint_hbm, sems, 4, 4))
    )
    local_planes(
        (field, adjoint),
        (field_prev, adjoint_prev),
        (out, adjoint_out),
        speed2,
        functools.partial(extra_of, coupling),
        sends,
    )
    for pair in sends:
        for send in pair:
            send.wait()


def ahead_step(rows, partials, field_prev, adjoint_prev, speed2, halos, lines, surface, pushes, patches):
    _, slots, width = surface.shape
    cells_z, cells_x, along = field_prev.shape
    in_vmem = pl.BlockSpec(memory_space=VMEM)
    f32 = jnp.float32
    sides = jax.ShapeDtypeStruct((along // width, cells_z, width), f32)
    return pl.pallas_call(
        ahead_kernel,
        in_specs=[pl.BlockSpec(memory_space=SMEM)] + [in_vmem] * (11 + len(pushes)),
        out_specs=[in_vmem] * 8 + [pl.BlockSpec(memory_space=HBM)] * 2,
        out_shape=edge_shapes(field_prev, width)
        + [sides, sides, jax.ShapeDtypeStruct((2, cells_x, along), f32)]
        + [jax.ShapeDtypeStruct((patches, width), f32)]
        + [HBM(field_prev.shape, f32)] * 2,
        scratch_shapes=coupling_scratch(field_prev, slots, width)
        + [pltpu.VMEM((2, 8 * slots, width), f32)]
        + [pltpu.VMEM((2, slots, width), f32)] * 3
        + [pltpu.VMEM(field_prev.shape, f32)] * 4
        + [pltpu.SemaphoreType.DMA((8,))],
        compiler_params=params(16),
        name="ahead",
    )(rows, *partials, field_prev, adjoint_prev, speed2, *halos, lines, surface, *pushes)


def keep_side(cells, z, first, last):
    last_x, width = cells.shape[0] - 1, first.shape[2]
    for part in range(first.shape[0]):
        lanes = slice(part * width, (part + 1) * width)
        first[part, pl.ds(z, 1), :] = cells[0:1, lanes]
        last[part, pl.ds(z, 1), :] = cells[last_x : last_x + 1, lanes]


def finish_kernel(field_hbm, adjoint_hbm, speed_first, speed_last, speed_ends, x_from_outer, x_from_inner, z_from_outer, z_from_inner, out_hbm, adjoint_out_hbm, field, adjoint, sems):
    cells_z, cells_x, along = field.shape
    parts = speed_first.shape[0]
    shares = 4
    share = cells_z // shares
    loads, sends = [], []
    for side, (source, held, target) in enumerate(
        ((field_hbm, field, out_hbm), (adjoint_hbm, adjoint, adjoint_out_hbm))
    ):
        loads.append(shares_of(source, held, sems, 2 * side * shares, shares))
        sends.append(shares_of(held, target, sems, (2 * side + 1) * shares, shares))
    for i in range(shares):
        for side in range(2):
            loads[side][i].start()
    for i in range(shares):
        for side, held in enumerate((field, adjoint)):
            loads[side][i].wait()

            def one(z, carry):
                first, last = (
                    jnp.concatenate([ref[p, pl.ds(z, 1), :] for p in range(parts)], axis=1)
                    for ref in (speed_first, speed_last)
                )
                held[z] = held[z] + x_added(
                    first, last, x_from_outer, x_from_inner, side, z, (cells_x, along)
                )
                return carry

            lax.fori_loop(i * share, (i + 1) * share, one, 0, unroll=share)
            before, after = incoming("gz", z_from_outer[side], z_from_inner[side])
            if i == 0:
                held[0] = held[0] + speed_ends[0] * before
            if i == shares - 1:
                held[cells_z - 1] = held[cells_z - 1] + speed_ends[1] * after
            sends[side][i].start()
    for side in range(2):
        for send in sends[side]:
            send.wait()


def finish_call(field, adjoint, speed_first, speed_last, speed_ends, halos):
    return pl.pallas_call(
        finish_kernel,
        in_specs=[pl.BlockSpec(memory_space=HBM)] * 2 + [pl.BlockSpec(memory_space=VMEM)] * 7,
        out_specs=[pl.BlockSpec(memory_space=HBM)] * 2,
        out_shape=[HBM(field.shape, jnp.float32)] * 2,
        scratch_shapes=[pltpu.VMEM(field.shape, jnp.float32)] * 2 + [pltpu.SemaphoreType.DMA((16,))],
        compiler_params=params(8),
        name="finish",
    )(*in_hbm(field, adjoint), speed_first, speed_last, speed_ends, *halos)


def swaps(axis, first):
    count = lax.axis_size(axis)
    if first:
        return [(i, i ^ 1) for i in range(count)]
    return [(i, (i + 1 if i % 2 else i - 1) % count) for i in range(count)]


def exchange(edges):
    axes = (("gx", False), ("gx", True), ("gz", False), ("gz", True))
    return [lax.ppermute(edge, axis, swaps(axis, first)) for edge, (axis, first) in zip(edges, axes)]


def body(
    pressure_now,
    pressure_prev,
    adjoint_now,
    adjoint_prev,
    speed2,
    layer_state,
    layer_maps,
    send_rows,
    slot_patch,
    patch_material,
):
    slots, _, width = layer_state.shape
    patches = patch_material.shape[0]
    devices = lax.axis_size(("gx", "gz"))
    rows = send_rows.reshape(-1)

    lines = surface_rows(layer_maps, slot_patch, patch_material, layer_state)
    lines = lax.all_to_all(lines, ("gx", "gz"), split_axis=0, concat_axis=0, tiled=True)
    lines = lines.reshape(slots * LINES, width)

    halos = exchange(first_edges(pressure_now, adjoint_now, width))
    *partials, push, picked = first_local(
        rows, pressure_now, pressure_prev, adjoint_now, adjoint_prev, speed2, slots, width
    )
    pushes = [push]
    results = first_border(
        rows, partials, pressure_now, adjoint_now, speed2, halos, lines, push, picked
    )
    field, adjoint, field_prev, adjoint_prev, speed = results[:5]
    edges, surface = results[5:9], results[9]
    for step in range(1, STEPS - 1):
        halos = exchange(edges)
        *partials, push, surface = local_step(
            step, rows, field, field_prev, adjoint, adjoint_prev, speed, lines, surface, pushes
        )
        pushes.append(push)
        field_prev, adjoint_prev = field, adjoint
        if step < STEPS - 2:
            field, adjoint, *edges = border_step(step, partials, speed, halos, width)
    results = ahead_step(
        rows, partials, field_prev, adjoint_prev, speed, halos, lines, surface, pushes, patches
    )
    edges, speeds, gradient, partials = results[:4], results[4:7], results[7], results[8:]
    parts = gradient.reshape(devices, patches // devices, width)
    parts = lax.all_to_all(parts, ("gx", "gz"), split_axis=0, concat_axis=0, tiled=True)
    halos = exchange(edges)
    field, adjoint = finish_call(*partials, *speeds, halos)
    return field, adjoint, jnp.sum(parts, axis=0)


def solution(mesh):
    grid = P("gz", "gx", None)
    split = P(("gx", "gz"), None, None)
    in_specs = (grid, grid, grid, grid, grid, split, P(), split, P(("gx", "gz")), P())
    out_specs = (grid, grid, P(("gx", "gz"), None))
    return jax.shard_map(body, mesh=mesh, in_specs=in_specs, out_specs=out_specs, check_vma=False)
```

```python
import functools

import jax
import jax.numpy as jnp
from jax import lax
from jax.experimental import pallas as pl
from jax.experimental.pallas import tpu as pltpu
from jax.sharding import PartitionSpec as P

STEPS = 4
KAPPA = 0.5
BETA = 0.3
TERMS = STEPS + 1
LINES = 8
META = TERMS
MIB = 1 << 20
VMEM = pltpu.VMEM
SMEM = pltpu.SMEM
HBM = pltpu.HBM
UNROLL = 10


def in_hbm(*arrays):
    return [pltpu.with_memory_space_constraint(array, HBM) for array in arrays]


def params(mib):
    return pltpu.CompilerParams(vmem_limit_bytes=mib * MIB)


def surface_kernel(maps_hbm, patch_hbm, material_hbm, layer_hbm, out_hbm, out, maps, patch_ref, material_ref, layer, vectors, scalars, sems):
    mats, _, depth = maps.shape
    slots, _, width = layer.shape
    chunks = (sems.shape[0] - 3) // 2
    block = slots // chunks
    small = [
        pltpu.make_async_copy(maps_hbm, maps, sems.at[2 * chunks]),
        pltpu.make_async_copy(patch_hbm, patch_ref, sems.at[2 * chunks + 1]),
        pltpu.make_async_copy(material_hbm, material_ref, sems.at[2 * chunks + 2]),
    ]
    large = [
        pltpu.make_async_copy(
            layer_hbm.at[pl.ds(i * block, block)], layer.at[pl.ds(i * block, block)], sems.at[i]
        )
        for i in range(chunks)
    ]
    for copy in small + large:
        copy.start()

    lane = lax.broadcasted_iota(jnp.int32, (1, width), 1)
    first = lax.broadcasted_iota(jnp.int32, (depth, 1), 0) == 0
    small[0].wait()
    matrices = [maps[mat] for mat in range(mats)]
    turned = [matrix.T for matrix in matrices]
    rows = [matrix[0:1, :] for matrix in matrices]
    cols = [matrix[:, 0:1] for matrix in turned]
    kept = [jnp.zeros((1, width), jnp.float32)] * mats
    for n in range(TERMS):
        for mat in range(mats):
            if n > 0:
                rows[mat], cols[mat] = (
                    jnp.sum(matrices[mat] * cols[mat], axis=0, keepdims=True),
                    jnp.sum(turned[mat] * rows[mat], axis=1, keepdims=True),
                )
            scaled = jnp.where(first, (1.0 - KAPPA) * cols[mat], cols[mat])
            vectors[mat, n] = jnp.broadcast_to(scaled, (depth, width))
            kept[mat] = jnp.where(lane == n + 1, cols[mat][0:1, 0:1], kept[mat])
    for mat in range(mats):
        scalars[mat] = jnp.broadcast_to(kept[mat], (8, width))
    small[1].wait()
    small[2].wait()

    def one(j, carry):
        patch = patch_ref[j]
        mat = material_ref[patch]
        sums = [jnp.zeros((8, width), jnp.float32)] * TERMS
        for c in range(depth // 8):
            part = layer[j, pl.ds(8 * c, 8), :]
            sums = [
                s + vectors[mat, n, pl.ds(8 * c, 8), :] * part for n, s in enumerate(sums)
            ]
        rows = [jnp.sum(s, axis=0, keepdims=True) for s in sums]
        scalar_row = jnp.where(lane == 0, patch.astype(jnp.float32), scalars[mat][0:1, :])
        rows.append(scalar_row)
        rows.extend([jnp.zeros((1, width), jnp.float32)] * (LINES - len(rows)))
        out[j] = jnp.concatenate(rows, axis=0)
        return carry

    sends = shares_of(out, out_hbm, sems, chunks, chunks)
    for i in range(chunks):
        large[i].wait()
        lax.fori_loop(i * block, (i + 1) * block, one, 0, unroll=4)
        sends[i].start()
    for send in sends:
        send.wait()


def surface_rows(layer_maps, slot_patch, patch_material, layer_state):
    slots, depth, width = layer_state.shape
    mats = layer_maps.shape[0]
    chunks = 8
    return pl.pallas_call(
        surface_kernel,
        in_specs=[pl.BlockSpec(memory_space=HBM)] * 4,
        out_specs=pl.BlockSpec(memory_space=HBM),
        out_shape=HBM((slots, LINES, width), jnp.float32),
        scratch_shapes=[
            pltpu.VMEM((slots, LINES, width), jnp.float32),
            pltpu.VMEM((mats, depth, depth), jnp.float32),
            pltpu.SMEM(slot_patch.shape, jnp.int32),
            pltpu.SMEM(patch_material.shape, jnp.int32),
            pltpu.VMEM((slots, depth, width), jnp.float32),
            pltpu.VMEM((mats, TERMS, depth, width), jnp.float32),
            pltpu.VMEM((mats, 8, width), jnp.float32),
            pltpu.SemaphoreType.DMA((2 * chunks + 3,)),
        ],
        compiler_params=params(24),
        name="surface_rows",
    )(*in_hbm(layer_maps, slot_patch, patch_material, layer_state))


def place(index, cells_x, parts):
    low, middle = parts.bit_length() - 1, cells_x.bit_length() - 1
    return (
        jnp.right_shift(index, low + middle),
        jnp.bitwise_and(jnp.right_shift(index, low), cells_x - 1),
        jnp.bitwise_and(index, parts - 1),
    )


def pick(rows_ref, fields, picked, tiles):
    cells_x = fields[0].shape[1]
    slots, width = picked.shape[1:]
    parts = fields[0].shape[2] // width

    def fetch(k, carry):
        z, x, part = place(jnp.maximum(rows_ref[k], 0), cells_x, parts)
        lines = pl.ds(pl.multiple_of(jnp.bitwise_and(x, -8), 8), 8)
        lanes = pl.ds(pl.multiple_of(part * width, width), width)
        for side, field in enumerate(fields):
            tiles[side, pl.ds(pl.multiple_of(8 * k, 8), 8), :] = field[z, lines, lanes]
        return carry

    lax.fori_loop(0, slots, fetch, 0, unroll=8)

    def choose(k, carry):
        index = rows_ref[k]
        line = 8 * k + jnp.bitwise_and(place(jnp.maximum(index, 0), cells_x, parts)[1], 7)
        for side in range(len(fields)):
            row = tiles[side, pl.ds(line, 1), :]
            picked[side, pl.ds(k, 1), :] = jnp.where(index >= 0, row, 0.0)
        return carry

    lax.fori_loop(0, slots, choose, 0, unroll=8)


def even(axis):
    return lax.axis_index(axis) % 2 == 0


def at_start(axis):
    return lax.axis_index(axis) == 0


def at_end(axis):
    return lax.axis_index(axis) == lax.axis_size(axis) - 1


def outgoing(axis, low, high):
    choice = even(axis)
    return jnp.where(choice, low, high), jnp.where(choice, high, low)


def incoming(axis, outer, inner):
    choice = even(axis)
    before = jnp.where(at_start(axis), 0.0, jnp.where(choice, outer, inner))
    after = jnp.where(at_end(axis), 0.0, jnp.where(choice, inner, outer))
    return before, after


def keep_sides(cells, side, z, x_outer, x_inner):
    last_x, width = cells.shape[0] - 1, x_outer.shape[3]
    for part in range(x_outer.shape[1]):
        lanes = slice(part * width, (part + 1) * width)
        x_outer[side, part, pl.ds(z, 1), :], x_inner[side, part, pl.ds(z, 1), :] = outgoing(
            "gx", cells[0:1, lanes], cells[last_x : last_x + 1, lanes]
        )


def side_row(plane, side, z):
    parts = plane.shape[1]
    return jnp.concatenate([plane[side, part, pl.ds(z, 1), :] for part in range(parts)], axis=1)


def keep_edges(z_planes, side, z_outer, z_inner):
    z_outer[side], z_inner[side] = outgoing("gz", *z_planes)


def edges_kernel(field_hbm, adjoint_hbm, x_outer, x_inner, z_outer, z_inner, field, adjoint, sems):
    copies = [
        pltpu.make_async_copy(field_hbm, field, sems.at[0]),
        pltpu.make_async_copy(adjoint_hbm, adjoint, sems.at[1]),
    ]
    for copy in copies:
        copy.start()
    for side, array in enumerate((field, adjoint)):
        copies[side].wait()

        def one(z, carry):
            keep_sides(array[z], side, z, x_outer, x_inner)
            return carry

        lax.fori_loop(0, array.shape[0], one, 0, unroll=8)
        keep_edges((array[0], array[array.shape[0] - 1]), side, z_outer, z_inner)


def edge_shapes(field, width):
    cells_z, cells_x, along = field.shape
    f32 = jnp.float32
    x_shape = jax.ShapeDtypeStruct((2, along // width, cells_z, width), f32)
    z_shape = jax.ShapeDtypeStruct((2, cells_x, along), f32)
    return [x_shape, x_shape, z_shape, z_shape]


def first_edges(field, adjoint, width):
    return pl.pallas_call(
        edges_kernel,
        in_specs=[pl.BlockSpec(memory_space=HBM)] * 2,
        out_specs=[pl.BlockSpec(memory_space=VMEM)] * 4,
        out_shape=edge_shapes(field, width),
        scratch_shapes=[
            pltpu.VMEM(field.shape, jnp.float32),
            pltpu.VMEM(field.shape, jnp.float32),
            pltpu.SemaphoreType.DMA((2,)),
        ],
        compiler_params=params(8),
        name="edges",
    )(*in_hbm(field, adjoint))


def couple(rows_ref, change, coupling):
    parts, cells_z, cells_x = coupling.shape[0] // 2, coupling.shape[1] - 1, coupling.shape[2]

    def put(k, carry):
        index = rows_ref[k]
        z, x, part = place(jnp.maximum(index, 0), cells_x, parts)
        z = jnp.where(index >= 0, z, cells_z)
        for side in range(2):
            coupling[side * parts + part, z, pl.ds(x, 1), :] = change[side, pl.ds(k, 1), :]
        return carry

    lax.fori_loop(0, change.shape[1], put, 0, unroll=8)


def local_planes(fields, befores, outs, speed2, extra, sends=None):
    cells_z = speed2.shape[0]

    def plane(z, below, above):
        speed = speed2[z]
        for side in range(2):
            now = fields[side]
            beside = below(now) + above(now)
            outs[side][z] = stencil(now[z], befores[side][z], speed, beside, extra(side, z))

    def inner(z, carry):
        plane(z, lambda now: now[z - 1], lambda now: now[z + 1])
        return carry

    plane(0, lambda now: 0.0, lambda now: now[1])
    plane(cells_z - 1, lambda now: now[cells_z - 2], lambda now: 0.0)
    shares = len(sends) if sends else 1
    share = cells_z // shares
    for i in range(shares):
        start, stop = max(i * share, 1), min((i + 1) * share, cells_z - 1)
        lax.fori_loop(start, stop, inner, 0, unroll=(stop - start) // -(-(stop - start) // UNROLL))
        for send in sends[i] if sends else ():
            send.start()


def stencil(cells, before, speed, beside, extra):
    cells_x, along = cells.shape
    row_id = lax.broadcasted_iota(jnp.int32, cells.shape, 0)
    lane_id = lax.broadcasted_iota(jnp.int32, cells.shape, 1)
    beside = beside + jnp.where(row_id == 0, 0.0, pltpu.roll(cells, 1, axis=0))
    beside = beside + jnp.where(row_id == cells_x - 1, 0.0, pltpu.roll(cells, cells_x - 1, axis=0))
    beside = beside + jnp.where(lane_id == 0, 0.0, pltpu.roll(cells, 1, axis=1))
    beside = beside + jnp.where(lane_id == along - 1, 0.0, pltpu.roll(cells, along - 1, axis=1))
    return 2.0 * cells - before + speed * (beside - 6.0 * cells) + extra


def shares_of(source, target, sems, first, count):
    share = source.shape[0] // count
    return [
        pltpu.make_async_copy(
            source.at[pl.ds(i * share, share)], target.at[pl.ds(i * share, share)], sems.at[first + i]
        )
        for i in range(count)
    ]


class Lines:
    def __init__(self, ref, slots):
        self.ref, self.slots = ref, slots
        self.meta = self.row(META + 1)

    def row(self, n):
        return self.ref[pl.ds(n - 1, self.slots, stride=LINES), :]

    def scalar(self, n):
        return self.meta[:, n : n + 1]

    def surface(self, step, pushes, side):
        new = self.row(step + 1) if side == 0 else None
        for t in range(step + 1):
            term = self.scalar(step + 1 - t) * pushes[t][side]
            new = term if new is None else new + term
        return new


def extra_of(coupling, side, z):
    parts = coupling.shape[0] // 2
    return jnp.concatenate([coupling[side * parts + part, z] for part in range(parts)], axis=1)


def couple_step(rows_ref, lines, step, pushes, picked, surface, change, coupling):
    for side in range(2):
        surface[side] = lines.surface(step, pushes, side)
        change[side] = BETA * (surface[side] - picked[side])
    couple(rows_ref, change, coupling)


def x_added(speed_first, speed_last, from_outer, from_inner, side, z, shape):
    row_id = lax.broadcasted_iota(jnp.int32, shape, 0)
    low, high = incoming("gx", side_row(from_outer, side, z), side_row(from_inner, side, z))
    low, high = speed_first * low, speed_last * high
    return jnp.where(row_id == 0, low, jnp.where(row_id == shape[0] - 1, high, 0.0))


def border_planes(partials, speed2, halos, outs, edges, extra):
    x_from_outer, x_from_inner, z_from_outer, z_from_inner = halos
    x_outer, x_inner, z_outer, z_inner = edges
    cells_z, cells_x, along = speed2.shape

    def plane(z, side, more):
        first, last = speed2[z, 0:1, :], speed2[z, cells_x - 1 : cells_x, :]
        new = partials[side][z] + x_added(
            first, last, x_from_outer, x_from_inner, side, z, (cells_x, along)
        )
        if extra is not None:
            new = new + extra(side, z)
        if more is not None:
            new = new + speed2[z] * more
        outs[side][z] = new
        keep_sides(new, side, z, x_outer, x_inner)
        return new

    for side in range(2):
        before, after = incoming("gz", z_from_outer[side], z_from_inner[side])
        ends = plane(0, side, before), plane(cells_z - 1, side, after)
        keep_edges(ends, side, z_outer, z_inner)

    def inner(z, carry):
        for side in range(2):
            plane(z, side, None)
        return carry

    lax.fori_loop(1, cells_z - 1, inner, 0, unroll=UNROLL)


def first_local_kernel(rows_hbm, field_hbm, field_prev_hbm, adjoint_hbm, adjoint_prev_hbm, speed2_hbm, out_hbm, adjoint_out_hbm, push, picked, rows_ref, field, field_prev, adjoint, adjoint_prev, speed2, out, adjoint_out, tiles, sems):
    loads = [
        pltpu.make_async_copy(source, target, sems.at[i])
        for i, (source, target) in enumerate(
            (
                (rows_hbm, rows_ref),
                (field_hbm, field),
                (adjoint_hbm, adjoint),
                (speed2_hbm, speed2),
                (field_prev_hbm, field_prev),
                (adjoint_prev_hbm, adjoint_prev),
            )
        )
    ]
    for copy in loads:
        copy.start()
    for copy in loads[:3]:
        copy.wait()
    pick(rows_ref, (field, adjoint), picked, tiles)
    push[...] = KAPPA * picked[...]
    for copy in loads[3:]:
        copy.wait()
    sends = list(
        zip(
            shares_of(out, out_hbm, sems, 6, 4), shares_of(adjoint_out, adjoint_out_hbm, sems, 10, 4)
        )
    )
    local_planes(
        (field, adjoint),
        (field_prev, adjoint_prev),
        (out, adjoint_out),
        speed2,
        lambda side, z: 0.0,
        sends,
    )
    for pair in sends:
        for send in pair:
            send.wait()


def first_local(rows, field, field_prev, adjoint, adjoint_prev, speed2, slots, width):
    rows_shape = jax.ShapeDtypeStruct((2, slots, width), jnp.float32)
    return pl.pallas_call(
        first_local_kernel,
        in_specs=[pl.BlockSpec(memory_space=HBM)] * 6,
        out_specs=[pl.BlockSpec(memory_space=HBM)] * 2 + [pl.BlockSpec(memory_space=VMEM)] * 2,
        out_shape=[HBM(field.shape, jnp.float32)] * 2 + [rows_shape] * 2,
        scratch_shapes=[pltpu.SMEM((slots,), jnp.int32)]
        + [pltpu.VMEM(field.shape, jnp.float32)] * 7
        + [pltpu.VMEM((2, 8 * slots, width), jnp.float32), pltpu.SemaphoreType.DMA((14,))],
        compiler_params=params(16),
        cost_estimate=pl.CostEstimate(flops=8 << 20, bytes_accessed=12 << 20, transcendentals=0),
        name="local0",
    )(*in_hbm(rows, field, field_prev, adjoint, adjoint_prev, speed2))


def first_border_kernel(rows_ref, partial_hbm, partial_adjoint_hbm, speed2_hbm, x_from_outer, x_from_inner, z_from_outer, z_from_inner, lines_ref, push, picked, out, adjoint_out, speed2, x_outer, x_inner, z_outer, z_inner, surface, partial, partial_adjoint, coupling, change, sems):
    loads = [
        pltpu.make_async_copy(source, target, sems.at[i])
        for i, (source, target) in enumerate(
            ((speed2_hbm, speed2), (partial_hbm, partial), (partial_adjoint_hbm, partial_adjoint))
        )
    ]
    for copy in loads:
        copy.start()
    coupling[...] = jnp.zeros_like(coupling)
    lines = Lines(lines_ref, change.shape[1])
    couple_step(rows_ref, lines, 0, [push], picked, surface, change, coupling)
    for copy in loads:
        copy.wait()
    border_planes(
        (partial, partial_adjoint),
        speed2,
        (x_from_outer, x_from_inner, z_from_outer, z_from_inner),
        (out, adjoint_out),
        (x_outer, x_inner, z_outer, z_inner),
        functools.partial(extra_of, coupling),
    )


def coupling_scratch(field, slots, width):
    cells_z, cells_x, along = field.shape
    return [
        pltpu.VMEM((2 * (along // width), cells_z + 1, cells_x, width), jnp.float32),
        pltpu.VMEM((2, slots, width), jnp.float32),
    ]


def first_border(rows, partials, speed2, halos, lines, push, picked):
    _, slots, width = push.shape
    field = partials[0]
    whole = jax.ShapeDtypeStruct(field.shape, jnp.float32)
    in_vmem = pl.BlockSpec(memory_space=VMEM)
    return pl.pallas_call(
        first_border_kernel,
        in_specs=[pl.BlockSpec(memory_space=SMEM)]
        + [pl.BlockSpec(memory_space=HBM)] * 3
        + [in_vmem] * 7,
        out_specs=[in_vmem] * 8,
        out_shape=[whole] * 3
        + edge_shapes(field, width)
        + [jax.ShapeDtypeStruct((2, slots, width), jnp.float32)],
        scratch_shapes=[pltpu.VMEM(field.shape, jnp.float32)] * 2
        + coupling_scratch(field, slots, width)
        + [pltpu.SemaphoreType.DMA((3,))],
        compiler_params=params(12),
        name="border0",
    )(rows, *in_hbm(*partials, speed2), *halos, lines, push, picked)


def local_kernel(step, rows_ref, field, field_prev, adjoint, adjoint_prev, speed2, lines_ref, surface, *refs):
    pushes, refs = list(refs[:step]), refs[step:]
    out, adjoint_out, push, next_surface, coupling, change, tiles, picked = refs[:8]
    loads = []
    if step == 1:
        *held, sems = refs[8:]
        loads = [
            pltpu.make_async_copy(source, target, sems.at[i])
            for i, (source, target) in enumerate(zip((field_prev, adjoint_prev), held))
        ]
        field_prev, adjoint_prev = held
    for copy in loads:
        copy.start()
    pick(rows_ref, (field, adjoint), picked, tiles)
    push[...] = KAPPA * (picked[...] - surface[...])
    coupling[...] = jnp.zeros_like(coupling)
    lines = Lines(lines_ref, change.shape[1])
    couple_step(rows_ref, lines, step, pushes + [push], picked, next_surface, change, coupling)
    for copy in loads:
        copy.wait()
    local_planes(
        (field, adjoint),
        (field_prev, adjoint_prev),
        (out, adjoint_out),
        speed2,
        functools.partial(extra_of, coupling),
    )


def local_step(step, rows, field, field_prev, adjoint, adjoint_prev, speed2, lines, surface, pushes):
    _, slots, width = surface.shape
    whole = jax.ShapeDtypeStruct(field.shape, jnp.float32)
    rows_shape = jax.ShapeDtypeStruct(surface.shape, jnp.float32)
    in_vmem = pl.BlockSpec(memory_space=VMEM)
    before, held = in_vmem, []
    if step == 1:
        before = pl.BlockSpec(memory_space=HBM)
        held = [pltpu.VMEM(field.shape, jnp.float32)] * 2 + [pltpu.SemaphoreType.DMA((2,))]
        field_prev, adjoint_prev = in_hbm(field_prev, adjoint_prev)
    return pl.pallas_call(
        functools.partial(local_kernel, step),
        in_specs=[pl.BlockSpec(memory_space=SMEM), in_vmem, before, in_vmem, before]
        + [in_vmem] * (3 + step),
        out_specs=[in_vmem] * 4,
        out_shape=[whole, whole, rows_shape, rows_shape],
        scratch_shapes=coupling_scratch(field, slots, width)
        + [
            pltpu.VMEM((2, 8 * slots, width), jnp.float32),
            pltpu.VMEM((2, slots, width), jnp.float32),
        ]
        + held,
        compiler_params=params(10),
        cost_estimate=pl.CostEstimate(flops=8 << 20, bytes_accessed=12 << 20, transcendentals=0),
        name=f"local{step}",
    )(rows, field, field_prev, adjoint, adjoint_prev, speed2, lines, surface, *pushes)


def border_kernel(partial, partial_adjoint, speed2, x_from_outer, x_from_inner, z_from_outer, z_from_inner, out, adjoint_out, *edges):
    border_planes(
        (partial, partial_adjoint),
        speed2,
        (x_from_outer, x_from_inner, z_from_outer, z_from_inner),
        (out, adjoint_out),
        edges,
        None,
    )


def border_step(step, partials, speed2, halos, width):
    field = partials[0]
    whole = jax.ShapeDtypeStruct(field.shape, jnp.float32)
    in_vmem = pl.BlockSpec(memory_space=VMEM)
    return pl.pallas_call(
        border_kernel,
        in_specs=[in_vmem] * 7,
        out_specs=[in_vmem] * 6,
        out_shape=[whole, whole] + edge_shapes(field, width),
        compiler_params=params(8),
        name=f"border{step}",
    )(*partials, speed2, *halos)


def correlation_kernel(rows_ref, field, field_prev, adjoint, adjoint_prev, lines_ref, surface, *refs):
    pushes, refs = list(refs[: STEPS - 1]), refs[STEPS - 1 :]
    gradient_hbm, change = refs[:2]
    targets, (gradient, tiles, picked, push, sems) = refs[2:6], refs[6:]
    sends = [
        pltpu.make_async_copy(source, target, sems.at[i])
        for i, (source, target) in enumerate(
            zip((field, field_prev, adjoint, adjoint_prev), targets)
        )
    ]
    for send in sends:
        send.start()
    pick(rows_ref, (field, adjoint), picked, tiles)
    push[...] = KAPPA * (picked[...] - surface[...])

    slots, width = change.shape[1:]
    lines = Lines(lines_ref, slots)
    known = pushes + [push]
    total = jnp.zeros((slots, width), jnp.float32)
    for late in range(STEPS):
        inside = (STEPS - late) * lines.row(TERMS - late)
        for t in range(STEPS - late):
            scale = (STEPS - late - t) * lines.scalar(TERMS - late - t)
            inside = inside + scale * known[t][0]
        total = total + known[late][1] * inside
    patches = gradient.shape[0]
    parts, rest = [], total
    for _ in range(3):
        parts.append(rest.astype(jnp.bfloat16))
        rest = rest - parts[-1].astype(jnp.float32)
    ids = lines.meta.T[0:1, :].astype(jnp.int32)
    owners = lax.broadcasted_iota(jnp.int32, (patches, slots), 0) == ids
    sums = jnp.dot(
        jnp.where(owners, 1.0, 0.0).astype(jnp.bfloat16),
        jnp.concatenate(parts, axis=1),
        preferred_element_type=jnp.float32,
    )
    gradient[...] = sums[:, :width] + (sums[:, width : 2 * width] + sums[:, 2 * width :])
    sends.append(pltpu.make_async_copy(gradient, gradient_hbm, sems.at[4]))
    sends[-1].start()

    for side in range(2):
        change[side] = BETA * (lines.surface(STEPS - 1, known, side) - picked[side])
    for send in sends:
        send.wait()


def correlate(rows, field, field_prev, adjoint, adjoint_prev, lines, surface, pushes, patches):
    _, slots, width = surface.shape
    f32 = jnp.float32
    in_vmem = pl.BlockSpec(memory_space=VMEM)
    return pl.pallas_call(
        correlation_kernel,
        in_specs=[pl.BlockSpec(memory_space=SMEM)] + [in_vmem] * (6 + len(pushes)),
        out_specs=[pl.BlockSpec(memory_space=HBM), in_vmem] + [pl.BlockSpec(memory_space=HBM)] * 4,
        out_shape=[
            HBM((patches, width), f32),
            jax.ShapeDtypeStruct(surface.shape, f32),
        ]
        + [HBM(field.shape, f32)] * 4,
        scratch_shapes=[
            pltpu.VMEM((patches, width), f32),
            pltpu.VMEM((2, 8 * slots, width), f32),
        ]
        + [pltpu.VMEM((2, slots, width), f32)] * 2
        + [pltpu.SemaphoreType.DMA((5,))],
        compiler_params=params(10),
        name="correlation",
    )(rows, field, field_prev, adjoint, adjoint_prev, lines, surface, *pushes)


def last_local_kernel(rows_hbm, field_hbm, field_prev_hbm, adjoint_hbm, adjoint_prev_hbm, speed2_hbm, change, out, adjoint_out, speed_first, speed_last, speed_ends, rows_ref, field, field_prev, adjoint, adjoint_prev, speed2, coupling, sems):
    loads = [
        pltpu.make_async_copy(source, target, sems.at[i])
        for i, (source, target) in enumerate(
            (
                (rows_hbm, rows_ref),
                (speed2_hbm, speed2),
                (field_hbm, field),
                (adjoint_hbm, adjoint),
                (field_prev_hbm, field_prev),
                (adjoint_prev_hbm, adjoint_prev),
            )
        )
    ]
    for copy in loads:
        copy.start()
    coupling[...] = jnp.zeros_like(coupling)
    loads[0].wait()
    couple(rows_ref, change, coupling)
    loads[1].wait()
    cells_z = speed2.shape[0]
    speed_ends[0], speed_ends[1] = speed2[0], speed2[cells_z - 1]

    def sides(z, carry):
        keep_side(speed2[z], z, speed_first, speed_last)
        return carry

    lax.fori_loop(0, cells_z, sides, 0, unroll=8)
    for copy in loads[2:]:
        copy.wait()
    local_planes(
        (field, adjoint),
        (field_prev, adjoint_prev),
        (out, adjoint_out),
        speed2,
        functools.partial(extra_of, coupling),
    )


def last_local(rows, field, field_prev, adjoint, adjoint_prev, speed2, change):
    _, slots, width = change.shape
    cells_z, cells_x, along = field.shape
    sides = jax.ShapeDtypeStruct((along // width, cells_z, width), jnp.float32)
    in_vmem = pl.BlockSpec(memory_space=VMEM)
    return pl.pallas_call(
        last_local_kernel,
        in_specs=[pl.BlockSpec(memory_space=HBM)] * 6 + [in_vmem],
        out_specs=[in_vmem] * 5,
        out_shape=[jax.ShapeDtypeStruct(field.shape, jnp.float32)] * 2
        + [sides, sides, jax.ShapeDtypeStruct((2, cells_x, along), jnp.float32)],
        scratch_shapes=[pltpu.SMEM((slots,), jnp.int32)]
        + [pltpu.VMEM(field.shape, jnp.float32)] * 5
        + coupling_scratch(field, slots, width)[:1]
        + [pltpu.SemaphoreType.DMA((6,))],
        compiler_params=params(16),
        cost_estimate=pl.CostEstimate(flops=8 << 20, bytes_accessed=12 << 20, transcendentals=0),
        name=f"local{STEPS - 1}",
    )(*in_hbm(rows, field, field_prev, adjoint, adjoint_prev, speed2), change)


def keep_side(cells, z, first, last):
    last_x, width = cells.shape[0] - 1, first.shape[2]
    for part in range(first.shape[0]):
        lanes = slice(part * width, (part + 1) * width)
        first[part, pl.ds(z, 1), :] = cells[0:1, lanes]
        last[part, pl.ds(z, 1), :] = cells[last_x : last_x + 1, lanes]


def finish_kernel(field_in, adjoint_in, speed_first, speed_last, speed_ends, x_from_outer, x_from_inner, z_from_outer, z_from_inner, out_hbm, adjoint_out_hbm, field, adjoint, sems):
    cells_z, cells_x, along = field.shape
    parts = speed_first.shape[0]
    shares = 4
    share = cells_z // shares
    sends = [
        shares_of(field, out_hbm, sems, 0, shares),
        shares_of(adjoint, adjoint_out_hbm, sems, shares, shares),
    ]
    for i in range(shares):
        for side, (source, held) in enumerate(((field_in, field), (adjoint_in, adjoint))):

            def one(z, carry):
                first, last = (
                    jnp.concatenate([ref[p, pl.ds(z, 1), :] for p in range(parts)], axis=1)
                    for ref in (speed_first, speed_last)
                )
                held[z] = source[z] + x_added(
                    first, last, x_from_outer, x_from_inner, side, z, (cells_x, along)
                )
                return carry

            lax.fori_loop(i * share, (i + 1) * share, one, 0, unroll=share)
            before, after = incoming("gz", z_from_outer[side], z_from_inner[side])
            if i == 0:
                held[0] = held[0] + speed_ends[0] * before
            if i == shares - 1:
                held[cells_z - 1] = held[cells_z - 1] + speed_ends[1] * after
            sends[side][i].start()
    for side in range(2):
        for send in sends[side]:
            send.wait()


def finish_call(field, adjoint, speed_first, speed_last, speed_ends, halos):
    return pl.pallas_call(
        finish_kernel,
        in_specs=[pl.BlockSpec(memory_space=VMEM)] * 9,
        out_specs=[pl.BlockSpec(memory_space=HBM)] * 2,
        out_shape=[HBM(field.shape, jnp.float32)] * 2,
        scratch_shapes=[pltpu.VMEM(field.shape, jnp.float32)] * 2 + [pltpu.SemaphoreType.DMA((8,))],
        compiler_params=params(8),
        name="finish",
    )(field, adjoint, speed_first, speed_last, speed_ends, *halos)


def swaps(axis, first):
    count = lax.axis_size(axis)
    if first:
        return [(i, i ^ 1) for i in range(count)]
    return [(i, (i + 1 if i % 2 else i - 1) % count) for i in range(count)]


def exchange(edges):
    axes = (("gx", False), ("gx", True), ("gz", False), ("gz", True))
    return [lax.ppermute(edge, axis, swaps(axis, first)) for edge, (axis, first) in zip(edges, axes)]


def body(
    pressure_now,
    pressure_prev,
    adjoint_now,
    adjoint_prev,
    speed2,
    layer_state,
    layer_maps,
    send_rows,
    slot_patch,
    patch_material,
):
    slots, _, width = layer_state.shape
    patches = patch_material.shape[0]
    devices = lax.axis_size(("gx", "gz"))
    rows = send_rows.reshape(-1)

    edges = first_edges(pressure_now, adjoint_now, width)
    halos = exchange(edges)
    lines = surface_rows(layer_maps, slot_patch, patch_material, layer_state)
    lines = lax.all_to_all(lines, ("gx", "gz"), split_axis=0, concat_axis=0, tiled=True)
    lines = lines.reshape(slots * LINES, width)

    *partials, push, picked = first_local(
        rows, pressure_now, pressure_prev, adjoint_now, adjoint_prev, speed2, slots, width
    )
    pushes = [push]
    field, adjoint, speed, *edges, surface = first_border(
        rows, partials, speed2, halos, lines, push, picked
    )
    field_prev, adjoint_prev = pressure_now, adjoint_now
    for step in range(1, STEPS - 1):
        halos = exchange(edges)
        *partials, push, surface = local_step(
            step, rows, field, field_prev, adjoint, adjoint_prev, speed, lines, surface, pushes
        )
        pushes.append(push)
        field_prev, adjoint_prev = field, adjoint
        field, adjoint, *edges = border_step(step, partials, speed, halos, width)
    halos = exchange(edges)
    gradient, change, *held = correlate(
        rows, field, field_prev, adjoint, adjoint_prev, lines, surface, pushes, patches
    )
    parts = gradient.reshape(devices, patches // devices, width)
    parts = lax.all_to_all(parts, ("gx", "gz"), split_axis=0, concat_axis=0, tiled=True)
    *partials, first, last, ends = last_local(rows, *held, speed2, change)
    field, adjoint = finish_call(*partials, first, last, ends, halos)
    return field, adjoint, jnp.sum(parts, axis=0)


def solution(mesh):
    grid = P("gz", "gx", None)
    split = P(("gx", "gz"), None, None)
    in_specs = (grid, grid, grid, grid, grid, split, P(), split, P(("gx", "gz")), P())
    out_specs = (grid, grid, P(("gx", "gz"), None))
    return jax.shard_map(body, mesh=mesh, in_specs=in_specs, out_specs=out_specs, check_vma=False)
```

```python
import functools

import jax
import jax.numpy as jnp
from jax import lax
from jax.experimental import pallas as pl
from jax.experimental.pallas import tpu as pltpu
from jax.sharding import PartitionSpec as P

STEPS = 4
KAPPA = 0.5
BETA = 0.3
TERMS = STEPS + 1
LINES = TERMS + 1
META = TERMS
MIB = 1 << 20
VMEM = pltpu.VMEM
SMEM = pltpu.SMEM
HBM = pltpu.HBM
UNROLL = 10


def in_hbm(*arrays):
    return [pltpu.with_memory_space_constraint(array, HBM) for array in arrays]


def params(mib):
    return pltpu.CompilerParams(vmem_limit_bytes=mib * MIB)


def surface_kernel(maps_hbm, patch_hbm, material_hbm, layer_hbm, out_hbm, out, maps, patch_ref, material_ref, layer, vectors, scalars, sems):
    mats, _, depth = maps.shape
    slots, _, width = layer.shape
    chunks = (sems.shape[0] - 3) // 2
    block = slots // chunks
    small = [
        pltpu.make_async_copy(maps_hbm, maps, sems.at[2 * chunks]),
        pltpu.make_async_copy(patch_hbm, patch_ref, sems.at[2 * chunks + 1]),
        pltpu.make_async_copy(material_hbm, material_ref, sems.at[2 * chunks + 2]),
    ]
    large = [
        pltpu.make_async_copy(
            layer_hbm.at[pl.ds(i * block, block)], layer.at[pl.ds(i * block, block)], sems.at[i]
        )
        for i in range(chunks)
    ]
    for copy in small + large:
        copy.start()

    lane = lax.broadcasted_iota(jnp.int32, (1, width), 1)
    first = lax.broadcasted_iota(jnp.int32, (depth, 1), 0) == 0
    small[0].wait()
    matrices = [maps[mat] for mat in range(mats)]
    turned = [matrix.T for matrix in matrices]
    rows = [matrix[0:1, :] for matrix in matrices]
    cols = [matrix[:, 0:1] for matrix in turned]
    kept = [jnp.zeros((1, width), jnp.float32)] * mats
    for n in range(TERMS):
        for mat in range(mats):
            if n > 0:
                rows[mat], cols[mat] = (
                    jnp.sum(matrices[mat] * cols[mat], axis=0, keepdims=True),
                    jnp.sum(turned[mat] * rows[mat], axis=1, keepdims=True),
                )
            scaled = jnp.where(first, (1.0 - KAPPA) * cols[mat], cols[mat])
            vectors[mat, n] = jnp.broadcast_to(scaled, (depth, width))
            kept[mat] = jnp.where(lane == n + 1, cols[mat][0:1, 0:1], kept[mat])
    for mat in range(mats):
        scalars[mat] = jnp.broadcast_to(kept[mat], (8, width))
    small[1].wait()
    small[2].wait()

    def one(j, carry):
        patch = patch_ref[j]
        mat = material_ref[patch]
        sums = [jnp.zeros((8, width), jnp.float32)] * TERMS
        for c in range(depth // 8):
            part = layer[j, pl.ds(8 * c, 8), :]
            sums = [
                s + vectors[mat, n, pl.ds(8 * c, 8), :] * part for n, s in enumerate(sums)
            ]
        rows = [jnp.sum(s, axis=0, keepdims=True) for s in sums]
        scalar_row = jnp.where(lane == 0, patch.astype(jnp.float32), scalars[mat][0:1, :])
        for n, row in enumerate([*rows, scalar_row]):
            out[pl.ds(LINES * j + n, 1), :] = row
        return carry

    sends = shares_of(out, out_hbm, sems, chunks, chunks)
    for i in range(chunks):
        large[i].wait()
        lax.fori_loop(i * block, (i + 1) * block, one, 0, unroll=4)
        sends[i].start()
    for send in sends:
        send.wait()


def surface_rows(layer_maps, slot_patch, patch_material, layer_state):
    slots, depth, width = layer_state.shape
    mats = layer_maps.shape[0]
    chunks = 8
    return pl.pallas_call(
        surface_kernel,
        in_specs=[pl.BlockSpec(memory_space=HBM)] * 4,
        out_specs=pl.BlockSpec(memory_space=HBM),
        out_shape=HBM((slots * LINES, width), jnp.float32),
        scratch_shapes=[
            pltpu.VMEM((slots * LINES, width), jnp.float32),
            pltpu.VMEM((mats, depth, depth), jnp.float32),
            pltpu.SMEM(slot_patch.shape, jnp.int32),
            pltpu.SMEM(patch_material.shape, jnp.int32),
            pltpu.VMEM((slots, depth, width), jnp.float32),
            pltpu.VMEM((mats, TERMS, depth, width), jnp.float32),
            pltpu.VMEM((mats, 8, width), jnp.float32),
            pltpu.SemaphoreType.DMA((2 * chunks + 3,)),
        ],
        compiler_params=params(24),
        name="surface_rows",
    )(*in_hbm(layer_maps, slot_patch, patch_material, layer_state))


def bits(index, low, count):
    return jnp.bitwise_and(jnp.right_shift(index, low), (1 << count) - 1)


class Place:
    def __init__(self, cells_z, cells_x, parts):
        self.parts, self.x, self.z = (n.bit_length() - 1 for n in (parts, cells_x, cells_z))

    def part(self, index):
        return bits(index, 0, self.parts)

    def x_of(self, index):
        return bits(index, self.parts, self.x)

    def x_low(self, index):
        return bits(index, self.parts, 3)

    def tile(self, index):
        group = bits(index, self.parts + 3, self.x - 3)
        return bits(index, self.parts + self.x, self.z), jnp.left_shift(group, 3)

    def z_or_past(self, index):
        return bits(index, self.parts + self.x, self.z + 1)


def pick(rows_ref, fields, picked, tiles):
    slots, width = picked.shape[1:]
    cells_z, cells_x, along = fields[0].shape
    place = Place(cells_z, cells_x, along // width)

    def fetch(k, carry):
        index = rows_ref[k]
        z, first = place.tile(index)
        lines = pl.ds(pl.multiple_of(first, 8), 8)
        lanes = pl.ds(pl.multiple_of(place.part(index) * width, width), width)
        for side, field in enumerate(fields):
            tiles[side, pl.ds(pl.multiple_of(8 * k, 8), 8), :] = field[z, lines, lanes]
        return carry

    lax.fori_loop(0, slots, fetch, 0, unroll=16)

    def choose(k, carry):
        line = 8 * k + place.x_low(rows_ref[k])
        for side in range(len(fields)):
            picked[side, pl.ds(k, 1), :] = tiles[side, pl.ds(line, 1), :]
        return carry

    lax.fori_loop(0, slots, choose, 0, unroll=16)


def even(axis):
    return lax.axis_index(axis) % 2 == 0


def at_start(axis):
    return lax.axis_index(axis) == 0


def at_end(axis):
    return lax.axis_index(axis) == lax.axis_size(axis) - 1


def outgoing(axis, low, high):
    choice = even(axis)
    return jnp.where(choice, low, high), jnp.where(choice, high, low)


def incoming(axis, outer, inner):
    choice = even(axis)
    before = jnp.where(at_start(axis), 0.0, jnp.where(choice, outer, inner))
    after = jnp.where(at_end(axis), 0.0, jnp.where(choice, inner, outer))
    return before, after


def keep_sides(cells, side, z, x_outer, x_inner):
    last_x, width = cells.shape[0] - 1, x_outer.shape[3]
    for part in range(x_outer.shape[1]):
        lanes = slice(part * width, (part + 1) * width)
        x_outer[side, part, pl.ds(z, 1), :], x_inner[side, part, pl.ds(z, 1), :] = outgoing(
            "gx", cells[0:1, lanes], cells[last_x : last_x + 1, lanes]
        )


def side_row(plane, side, z):
    parts = plane.shape[1]
    return jnp.concatenate([plane[side, part, pl.ds(z, 1), :] for part in range(parts)], axis=1)


def keep_edges(z_planes, side, z_outer, z_inner):
    z_outer[side], z_inner[side] = outgoing("gz", *z_planes)


def edges_kernel(field_hbm, adjoint_hbm, field, adjoint, x_outer, x_inner, z_outer, z_inner, sems):
    copies = [
        pltpu.make_async_copy(field_hbm, field, sems.at[0]),
        pltpu.make_async_copy(adjoint_hbm, adjoint, sems.at[1]),
    ]
    for copy in copies:
        copy.start()
    for side, array in enumerate((field, adjoint)):
        copies[side].wait()

        def one(z, carry):
            keep_sides(array[z], side, z, x_outer, x_inner)
            return carry

        lax.fori_loop(0, array.shape[0], one, 0, unroll=8)
        keep_edges((array[0], array[array.shape[0] - 1]), side, z_outer, z_inner)


def edge_shapes(field, width):
    cells_z, cells_x, along = field.shape
    f32 = jnp.float32
    x_shape = jax.ShapeDtypeStruct((2, along // width, cells_z, width), f32)
    z_shape = jax.ShapeDtypeStruct((2, cells_x, along), f32)
    return [x_shape, x_shape, z_shape, z_shape]


def first_edges(field, adjoint, width):
    return pl.pallas_call(
        edges_kernel,
        in_specs=[pl.BlockSpec(memory_space=HBM)] * 2,
        out_specs=[pl.BlockSpec(memory_space=VMEM)] * 6,
        out_shape=[jax.ShapeDtypeStruct(field.shape, jnp.float32)] * 2 + edge_shapes(field, width),
        scratch_shapes=[pltpu.SemaphoreType.DMA((2,))],
        compiler_params=params(8),
        name="edges",
    )(*in_hbm(field, adjoint))


def couple(rows_ref, change, coupling):
    parts, heights, cells_x = coupling.shape[0] // 2, coupling.shape[1], coupling.shape[2]
    place = Place(heights // 2, cells_x, parts)

    def put(k, carry):
        index = rows_ref[k]
        z, x, part = place.z_or_past(index), place.x_of(index), place.part(index)
        for side in range(2):
            coupling[side * parts + part, z, pl.ds(x, 1), :] = change[side, pl.ds(k, 1), :]
        return carry

    lax.fori_loop(0, change.shape[1], put, 0, unroll=16)


def clear(coupling):
    heights = coupling.shape[1] // 2
    coupling[:, :heights] = jnp.zeros((coupling.shape[0], heights, *coupling.shape[2:]), jnp.float32)


def local_planes(fields, befores, outs, speed2, extra, sends=None):
    cells_z = speed2.shape[0]

    def plane(z, below, above):
        speed = speed2[z]
        for side in range(2):
            now = fields[side]
            beside = below(now) + above(now)
            outs[side][z] = stencil(now[z], befores[side][z], speed, beside, extra(side, z))

    def inner(z, carry):
        plane(z, lambda now: now[z - 1], lambda now: now[z + 1])
        return carry

    plane(0, lambda now: 0.0, lambda now: now[1])
    plane(cells_z - 1, lambda now: now[cells_z - 2], lambda now: 0.0)
    shares = len(sends) if sends else 1
    share = cells_z // shares
    for i in range(shares):
        start, stop = max(i * share, 1), min((i + 1) * share, cells_z - 1)
        lax.fori_loop(start, stop, inner, 0, unroll=(stop - start) // -(-(stop - start) // UNROLL))
        for send in sends[i] if sends else ():
            send.start()


def stencil(cells, before, speed, beside, extra):
    cells_x, along = cells.shape
    row_id = lax.broadcasted_iota(jnp.int32, cells.shape, 0)
    lane_id = lax.broadcasted_iota(jnp.int32, cells.shape, 1)
    beside = beside + jnp.where(row_id == 0, 0.0, pltpu.roll(cells, 1, axis=0))
    beside = beside + jnp.where(row_id == cells_x - 1, 0.0, pltpu.roll(cells, cells_x - 1, axis=0))
    beside = beside + jnp.where(lane_id == 0, 0.0, pltpu.roll(cells, 1, axis=1))
    beside = beside + jnp.where(lane_id == along - 1, 0.0, pltpu.roll(cells, along - 1, axis=1))
    return 2.0 * cells - before + speed * (beside - 6.0 * cells) + extra


def shares_of(source, target, sems, first, count):
    share = source.shape[0] // count
    return [
        pltpu.make_async_copy(
            source.at[pl.ds(i * share, share)], target.at[pl.ds(i * share, share)], sems.at[first + i]
        )
        for i in range(count)
    ]


class Lines:
    def __init__(self, ref, slots):
        self.ref, self.slots = ref, slots
        self.meta = self.row(META + 1)

    def row(self, n):
        return self.ref[pl.ds(n - 1, self.slots, stride=LINES), :]

    def scalar(self, n):
        return self.meta[:, n : n + 1]

    def surface(self, step, pushes, side):
        new = self.row(step + 1) if side == 0 else None
        for t in range(step + 1):
            term = self.scalar(step + 1 - t) * pushes[t][side]
            new = term if new is None else new + term
        return new


def extra_of(coupling, side, z):
    parts = coupling.shape[0] // 2
    return jnp.concatenate([coupling[side * parts + part, z] for part in range(parts)], axis=1)


def couple_step(rows_ref, lines, step, pushes, picked, surface, change, coupling):
    for side in range(2):
        surface[side] = lines.surface(step, pushes, side)
        change[side] = BETA * (surface[side] - picked[side])
    couple(rows_ref, change, coupling)


def x_added(speed_first, speed_last, from_outer, from_inner, side, z, shape):
    row_id = lax.broadcasted_iota(jnp.int32, shape, 0)
    low, high = incoming("gx", side_row(from_outer, side, z), side_row(from_inner, side, z))
    low, high = speed_first * low, speed_last * high
    return jnp.where(row_id == 0, low, jnp.where(row_id == shape[0] - 1, high, 0.0))


def border_planes(partials, speed2, halos, outs, edges, extra, arrivals=((),)):
    x_from_outer, x_from_inner, z_from_outer, z_from_inner = halos
    x_outer, x_inner, z_outer, z_inner = edges
    cells_z, cells_x, along = speed2.shape
    z_halos = [incoming("gz", z_from_outer[side], z_from_inner[side]) for side in range(2)]

    def plane(z, side, more):
        first, last = speed2[z, 0:1, :], speed2[z, cells_x - 1 : cells_x, :]
        new = partials[side][z] + x_added(
            first, last, x_from_outer, x_from_inner, side, z, (cells_x, along)
        )
        if extra is not None:
            new = new + extra(side, z)
        if more is not None:
            new = new + speed2[z] * more
        outs[side][z] = new
        keep_sides(new, side, z, x_outer, x_inner)

    def inner(z, carry):
        for side in range(2):
            plane(z, side, None)
        return carry

    shares = len(arrivals)
    share = cells_z // shares
    for i, copies in enumerate(arrivals):
        for copy in copies:
            copy.wait()
        start, stop = max(i * share, 1), min((i + 1) * share, cells_z - 1)
        for side in range(2):
            if i == 0:
                plane(0, side, z_halos[side][0])
            if i == shares - 1:
                plane(cells_z - 1, side, z_halos[side][1])
        lax.fori_loop(start, stop, inner, 0, unroll=min(stop - start, UNROLL))
    for side in range(2):
        keep_edges((outs[side][0], outs[side][cells_z - 1]), side, z_outer, z_inner)


def first_local_kernel(rows_hbm, field_prev_hbm, adjoint_prev_hbm, speed2_hbm, field, adjoint, out_hbm, adjoint_out_hbm, push, picked, rows_ref, field_prev, adjoint_prev, speed2, out, adjoint_out, tiles, sems):
    loads = [
        pltpu.make_async_copy(source, target, sems.at[i])
        for i, (source, target) in enumerate(
            (
                (rows_hbm, rows_ref),
                (speed2_hbm, speed2),
                (field_prev_hbm, field_prev),
                (adjoint_prev_hbm, adjoint_prev),
            )
        )
    ]
    for copy in loads:
        copy.start()
    loads[0].wait()
    pick(rows_ref, (field, adjoint), picked, tiles)
    push[...] = KAPPA * picked[...]
    for copy in loads[1:]:
        copy.wait()
    sends = list(
        zip(
            shares_of(out, out_hbm, sems, 6, 4), shares_of(adjoint_out, adjoint_out_hbm, sems, 10, 4)
        )
    )
    local_planes(
        (field, adjoint),
        (field_prev, adjoint_prev),
        (out, adjoint_out),
        speed2,
        lambda side, z: 0.0,
        sends,
    )
    for pair in sends:
        for send in pair:
            send.wait()


def first_local(rows, field, field_prev, adjoint, adjoint_prev, speed2, slots, width):
    rows_shape = jax.ShapeDtypeStruct((2, slots, width), jnp.float32)
    return pl.pallas_call(
        first_local_kernel,
        in_specs=[pl.BlockSpec(memory_space=HBM)] * 4 + [pl.BlockSpec(memory_space=VMEM)] * 2,
        out_specs=[pl.BlockSpec(memory_space=HBM)] * 2 + [pl.BlockSpec(memory_space=VMEM)] * 2,
        out_shape=[HBM(field.shape, jnp.float32)] * 2 + [rows_shape] * 2,
        scratch_shapes=[pltpu.SMEM((slots,), jnp.int32)]
        + [pltpu.VMEM(field.shape, jnp.float32)] * 5
        + [pltpu.VMEM((2, 8 * slots, width), jnp.float32), pltpu.SemaphoreType.DMA((14,))],
        compiler_params=params(16),
        cost_estimate=pl.CostEstimate(flops=8 << 20, bytes_accessed=12 << 20, transcendentals=0),
        name="local0",
    )(*in_hbm(rows, field_prev, adjoint_prev, speed2), field, adjoint)


def first_border_kernel(rows_ref, partial_hbm, partial_adjoint_hbm, speed2_hbm, x_from_outer, x_from_inner, z_from_outer, z_from_inner, lines_ref, push, picked, out, adjoint_out, speed2, x_outer, x_inner, z_outer, z_inner, surface, partial, partial_adjoint, coupling, change, sems):
    shares = 4
    loads = [
        shares_of(source, target, sems, shares * i, shares)
        for i, (source, target) in enumerate(
            ((speed2_hbm, speed2), (partial_hbm, partial), (partial_adjoint_hbm, partial_adjoint))
        )
    ]
    arrivals = [[copies[i] for copies in loads] for i in range(shares)]
    for copies in arrivals:
        for copy in copies:
            copy.start()
    clear(coupling)
    lines = Lines(lines_ref, change.shape[1])
    couple_step(rows_ref, lines, 0, [push], picked, surface, change, coupling)
    border_planes(
        (partial, partial_adjoint),
        speed2,
        (x_from_outer, x_from_inner, z_from_outer, z_from_inner),
        (out, adjoint_out),
        (x_outer, x_inner, z_outer, z_inner),
        functools.partial(extra_of, coupling),
        arrivals,
    )


def coupling_scratch(field, slots, width):
    cells_z, cells_x, along = field.shape
    return [
        pltpu.VMEM((2 * (along // width), 2 * cells_z, cells_x, width), jnp.float32),
        pltpu.VMEM((2, slots, width), jnp.float32),
    ]


def first_border(rows, partials, speed2, halos, lines, push, picked):
    _, slots, width = push.shape
    field = partials[0]
    whole = jax.ShapeDtypeStruct(field.shape, jnp.float32)
    in_vmem = pl.BlockSpec(memory_space=VMEM)
    return pl.pallas_call(
        first_border_kernel,
        in_specs=[pl.BlockSpec(memory_space=SMEM)]
        + [pl.BlockSpec(memory_space=HBM)] * 3
        + [in_vmem] * 7,
        out_specs=[in_vmem] * 8,
        out_shape=[whole] * 3
        + edge_shapes(field, width)
        + [jax.ShapeDtypeStruct((2, slots, width), jnp.float32)],
        scratch_shapes=[pltpu.VMEM(field.shape, jnp.float32)] * 2
        + coupling_scratch(field, slots, width)
        + [pltpu.SemaphoreType.DMA((12,))],
        compiler_params=params(14),
        name="border0",
    )(rows, *in_hbm(*partials, speed2), *halos, lines, push, picked)


def local_kernel(step, rows_ref, field, field_prev, adjoint, adjoint_prev, speed2, lines_ref, surface, *refs):
    pushes, refs = list(refs[:step]), refs[step:]
    out, adjoint_out, push, next_surface = refs[:4]
    sends = []
    if step == STEPS - 2:
        sends = [
            pltpu.make_async_copy(source, target, refs[-1].at[i])
            for i, (source, target) in enumerate(zip((field, adjoint), refs[4:6]))
        ]
        refs = refs[:4] + refs[6:-1]
    for send in sends:
        send.start()
    coupling, change, tiles, picked = refs[4:8]
    loads = []
    if step == 1:
        *held, sems = refs[8:]
        loads = [
            pltpu.make_async_copy(source, target, sems.at[i])
            for i, (source, target) in enumerate(zip((field_prev, adjoint_prev), held))
        ]
        field_prev, adjoint_prev = held
    for copy in loads:
        copy.start()
    pick(rows_ref, (field, adjoint), picked, tiles)
    push[...] = KAPPA * (picked[...] - surface[...])
    clear(coupling)
    lines = Lines(lines_ref, change.shape[1])
    couple_step(rows_ref, lines, step, pushes + [push], picked, next_surface, change, coupling)
    for copy in loads:
        copy.wait()
    local_planes(
        (field, adjoint),
        (field_prev, adjoint_prev),
        (out, adjoint_out),
        speed2,
        functools.partial(extra_of, coupling),
    )
    for send in sends:
        send.wait()


def local_step(step, rows, field, field_prev, adjoint, adjoint_prev, speed2, lines, surface, pushes):
    _, slots, width = surface.shape
    whole = jax.ShapeDtypeStruct(field.shape, jnp.float32)
    rows_shape = jax.ShapeDtypeStruct(surface.shape, jnp.float32)
    in_vmem = pl.BlockSpec(memory_space=VMEM)
    before, held, kept = in_vmem, [], []
    if step == STEPS - 2:
        kept = [HBM(field.shape, jnp.float32)] * 2
        held = [pltpu.SemaphoreType.DMA((2,))]
    if step == 1:
        before = pl.BlockSpec(memory_space=HBM)
        held = [pltpu.VMEM(field.shape, jnp.float32)] * 2 + [pltpu.SemaphoreType.DMA((2,))]
        field_prev, adjoint_prev = in_hbm(field_prev, adjoint_prev)
    return pl.pallas_call(
        functools.partial(local_kernel, step),
        in_specs=[pl.BlockSpec(memory_space=SMEM), in_vmem, before, in_vmem, before]
        + [in_vmem] * (3 + step),
        out_specs=[in_vmem] * 4 + [pl.BlockSpec(memory_space=HBM)] * len(kept),
        out_shape=[whole, whole, rows_shape, rows_shape, *kept],
        scratch_shapes=coupling_scratch(field, slots, width)
        + [
            pltpu.VMEM((2, 8 * slots, width), jnp.float32),
            pltpu.VMEM((2, slots, width), jnp.float32),
        ]
        + held,
        compiler_params=params(12),
        cost_estimate=pl.CostEstimate(flops=8 << 20, bytes_accessed=12 << 20, transcendentals=0),
        name=f"local{step}",
    )(rows, field, field_prev, adjoint, adjoint_prev, speed2, lines, surface, *pushes)


def border_kernel(partial, partial_adjoint, speed2, x_from_outer, x_from_inner, z_from_outer, z_from_inner, out, adjoint_out, *edges):
    border_planes(
        (partial, partial_adjoint),
        speed2,
        (x_from_outer, x_from_inner, z_from_outer, z_from_inner),
        (out, adjoint_out),
        edges,
        None,
    )


def border_step(step, partials, speed2, halos, width):
    field = partials[0]
    whole = jax.ShapeDtypeStruct(field.shape, jnp.float32)
    in_vmem = pl.BlockSpec(memory_space=VMEM)
    return pl.pallas_call(
        border_kernel,
        in_specs=[in_vmem] * 7,
        out_specs=[in_vmem] * 6,
        out_shape=[whole, whole] + edge_shapes(field, width),
        compiler_params=params(8),
        name=f"border{step}",
    )(*partials, speed2, *halos)


def correlation_kernel(rows_ref, used, field, adjoint, lines_ref, surface, *refs):
    pushes, refs = list(refs[: STEPS - 1]), refs[STEPS - 1 :]
    gradient_hbm, change = refs[:2]
    targets, (gradient, tiles, picked, push, sems) = refs[2:4], refs[4:]
    sends = [
        pltpu.make_async_copy(source, target, sems.at[i])
        for i, (source, target) in enumerate(zip((field, adjoint), targets))
    ]
    for send in sends:
        send.start()
    pick(rows_ref, (field, adjoint), picked, tiles)
    push[...] = KAPPA * (picked[...] - surface[...])

    slots, width = change.shape[1:]
    lines = Lines(lines_ref, slots)
    known = pushes + [push]
    total = jnp.zeros((slots, width), jnp.float32)
    for late in range(STEPS):
        inside = (STEPS - late) * lines.row(TERMS - late)
        for t in range(STEPS - late):
            scale = (STEPS - late - t) * lines.scalar(TERMS - late - t)
            inside = inside + scale * known[t][0]
        total = total + known[late][1] * inside
    patches = gradient.shape[0]
    parts, rest = [], total
    for _ in range(3):
        parts.append(rest.astype(jnp.bfloat16))
        rest = rest - parts[-1].astype(jnp.float32)
    ids = lines.meta.T[0:1, :].astype(jnp.int32)
    ids = jnp.where(used[...] >= 0, ids, -1)
    owners = lax.broadcasted_iota(jnp.int32, (patches, slots), 0) == ids
    sums = jnp.dot(
        jnp.where(owners, 1.0, 0.0).astype(jnp.bfloat16),
        jnp.concatenate(parts, axis=1),
        preferred_element_type=jnp.float32,
    )
    gradient[...] = sums[:, :width] + (sums[:, width : 2 * width] + sums[:, 2 * width :])
    sends.append(pltpu.make_async_copy(gradient, gradient_hbm, sems.at[2]))
    sends[-1].start()

    for side in range(2):
        change[side] = BETA * (lines.surface(STEPS - 1, known, side) - picked[side])
    for send in sends:
        send.wait()


def correlate(rows, field, adjoint, lines, surface, pushes, patches):
    _, slots, width = surface.shape
    f32 = jnp.float32
    in_vmem = pl.BlockSpec(memory_space=VMEM)
    return pl.pallas_call(
        correlation_kernel,
        in_specs=[pl.BlockSpec(memory_space=SMEM)] + [in_vmem] * (5 + len(pushes)),
        out_specs=[pl.BlockSpec(memory_space=HBM), in_vmem] + [pl.BlockSpec(memory_space=HBM)] * 2,
        out_shape=[
            HBM((patches, width), f32),
            jax.ShapeDtypeStruct(surface.shape, f32),
        ]
        + [HBM(field.shape, f32)] * 2,
        scratch_shapes=[
            pltpu.VMEM((patches, width), f32),
            pltpu.VMEM((2, 8 * slots, width), f32),
        ]
        + [pltpu.VMEM((2, slots, width), f32)] * 2
        + [pltpu.SemaphoreType.DMA((3,))],
        compiler_params=params(10),
        name="correlation",
    )(rows, rows.reshape(1, slots), field, adjoint, lines, surface, *pushes)


def last_local_kernel(rows_hbm, field_hbm, field_prev_hbm, adjoint_hbm, adjoint_prev_hbm, speed2_hbm, change, out, adjoint_out, speed_first, speed_last, speed_ends, rows_ref, field, field_prev, adjoint, adjoint_prev, speed2, coupling, sems):
    loads = [
        pltpu.make_async_copy(source, target, sems.at[i])
        for i, (source, target) in enumerate(
            (
                (rows_hbm, rows_ref),
                (speed2_hbm, speed2),
                (field_hbm, field),
                (adjoint_hbm, adjoint),
                (field_prev_hbm, field_prev),
                (adjoint_prev_hbm, adjoint_prev),
            )
        )
    ]
    for copy in loads:
        copy.start()
    clear(coupling)
    loads[0].wait()
    couple(rows_ref, change, coupling)
    loads[1].wait()
    cells_z = speed2.shape[0]
    speed_ends[0], speed_ends[1] = speed2[0], speed2[cells_z - 1]

    def sides(z, carry):
        keep_side(speed2[z], z, speed_first, speed_last)
        return carry

    lax.fori_loop(0, cells_z, sides, 0, unroll=8)
    for copy in loads[2:]:
        copy.wait()
    local_planes(
        (field, adjoint),
        (field_prev, adjoint_prev),
        (out, adjoint_out),
        speed2,
        functools.partial(extra_of, coupling),
    )


def last_local(rows, field, field_prev, adjoint, adjoint_prev, speed2, change):
    _, slots, width = change.shape
    cells_z, cells_x, along = field.shape
    sides = jax.ShapeDtypeStruct((along // width, cells_z, width), jnp.float32)
    in_vmem = pl.BlockSpec(memory_space=VMEM)
    return pl.pallas_call(
        last_local_kernel,
        in_specs=[pl.BlockSpec(memory_space=HBM)] * 6 + [in_vmem],
        out_specs=[in_vmem] * 5,
        out_shape=[jax.ShapeDtypeStruct(field.shape, jnp.float32)] * 2
        + [sides, sides, jax.ShapeDtypeStruct((2, cells_x, along), jnp.float32)],
        scratch_shapes=[pltpu.SMEM((slots,), jnp.int32)]
        + [pltpu.VMEM(field.shape, jnp.float32)] * 5
        + coupling_scratch(field, slots, width)[:1]
        + [pltpu.SemaphoreType.DMA((6,))],
        compiler_params=params(16),
        cost_estimate=pl.CostEstimate(flops=8 << 20, bytes_accessed=12 << 20, transcendentals=0),
        name=f"local{STEPS - 1}",
    )(*in_hbm(rows, field, field_prev, adjoint, adjoint_prev, speed2), change)


def keep_side(cells, z, first, last):
    last_x, width = cells.shape[0] - 1, first.shape[2]
    for part in range(first.shape[0]):
        lanes = slice(part * width, (part + 1) * width)
        first[part, pl.ds(z, 1), :] = cells[0:1, lanes]
        last[part, pl.ds(z, 1), :] = cells[last_x : last_x + 1, lanes]


def finish_kernel(field_in, adjoint_in, speed_first, speed_last, speed_ends, x_from_outer, x_from_inner, z_from_outer, z_from_inner, out_hbm, adjoint_out_hbm, field, adjoint, sems):
    cells_z, cells_x, along = field.shape
    parts = speed_first.shape[0]
    shares = 4
    share = cells_z // shares
    sends = [
        shares_of(field, out_hbm, sems, 0, shares),
        shares_of(adjoint, adjoint_out_hbm, sems, shares, shares),
    ]
    for i in range(shares):
        for side, (source, held) in enumerate(((field_in, field), (adjoint_in, adjoint))):

            def one(z, carry):
                first, last = (
                    jnp.concatenate([ref[p, pl.ds(z, 1), :] for p in range(parts)], axis=1)
                    for ref in (speed_first, speed_last)
                )
                held[z] = source[z] + x_added(
                    first, last, x_from_outer, x_from_inner, side, z, (cells_x, along)
                )
                return carry

            lax.fori_loop(i * share, (i + 1) * share, one, 0, unroll=share)
            before, after = incoming("gz", z_from_outer[side], z_from_inner[side])
            if i == 0:
                held[0] = held[0] + speed_ends[0] * before
            if i == shares - 1:
                held[cells_z - 1] = held[cells_z - 1] + speed_ends[1] * after
            sends[side][i].start()
    for side in range(2):
        for send in sends[side]:
            send.wait()


def finish_call(field, adjoint, speed_first, speed_last, speed_ends, halos):
    return pl.pallas_call(
        finish_kernel,
        in_specs=[pl.BlockSpec(memory_space=VMEM)] * 9,
        out_specs=[pl.BlockSpec(memory_space=HBM)] * 2,
        out_shape=[HBM(field.shape, jnp.float32)] * 2,
        scratch_shapes=[pltpu.VMEM(field.shape, jnp.float32)] * 2 + [pltpu.SemaphoreType.DMA((8,))],
        compiler_params=params(8),
        name="finish",
    )(field, adjoint, speed_first, speed_last, speed_ends, *halos)


def swaps(axis, first):
    count = lax.axis_size(axis)
    if first:
        return [(i, i ^ 1) for i in range(count)]
    return [(i, (i + 1 if i % 2 else i - 1) % count) for i in range(count)]


def exchange(edges):
    axes = (("gx", False), ("gx", True), ("gz", False), ("gz", True))
    return [lax.ppermute(edge, axis, swaps(axis, first)) for edge, (axis, first) in zip(edges, axes)]


def body(
    pressure_now,
    pressure_prev,
    adjoint_now,
    adjoint_prev,
    speed2,
    layer_state,
    layer_maps,
    send_rows,
    slot_patch,
    patch_material,
):
    slots, _, width = layer_state.shape
    patches = patch_material.shape[0]
    devices = lax.axis_size(("gx", "gz"))
    rows = send_rows.reshape(-1)

    field, adjoint, *edges = first_edges(pressure_now, adjoint_now, width)
    halos = exchange(edges)
    lines = surface_rows(layer_maps, slot_patch, patch_material, layer_state)
    lines = lines.reshape(slots, 1, LINES * width)
    lines = lax.all_to_all(lines, ("gx", "gz"), split_axis=0, concat_axis=0, tiled=True)
    lines = lines.reshape(slots * LINES, width)

    *partials, push, picked = first_local(
        rows, field, pressure_prev, adjoint, adjoint_prev, speed2, slots, width
    )
    pushes = [push]
    field, adjoint, speed, *edges, surface = first_border(
        rows, partials, speed2, halos, lines, push, picked
    )
    field_prev, adjoint_prev = pressure_now, adjoint_now
    for step in range(1, STEPS - 1):
        halos = exchange(edges)
        field_next, adjoint_next, push, surface, *sent = local_step(
            step, rows, field, field_prev, adjoint, adjoint_prev, speed, lines, surface, pushes
        )
        partials = (field_next, adjoint_next)
        pushes.append(push)
        field_prev, adjoint_prev = field, adjoint
        field, adjoint, *edges = border_step(step, partials, speed, halos, width)
    halos = exchange(edges)
    gradient, change, *held = correlate(
        rows, field, adjoint, lines, surface, pushes, patches
    )
    parts = gradient.reshape(devices, patches // devices, width)
    parts = lax.all_to_all(parts, ("gx", "gz"), split_axis=0, concat_axis=0, tiled=True)
    *partials, first, last, ends = last_local(
        rows, held[0], sent[0], held[1], sent[1], speed2, change
    )
    field, adjoint = finish_call(*partials, first, last, ends, halos)
    return field, adjoint, jnp.sum(parts, axis=0)


def solution(mesh):
    grid = P("gz", "gx", None)
    split = P(("gx", "gz"), None, None)
    in_specs = (grid, grid, grid, grid, grid, split, P(), split, P(("gx", "gz")), P())
    out_specs = (grid, grid, P(("gx", "gz"), None))
    return jax.shard_map(body, mesh=mesh, in_specs=in_specs, out_specs=out_specs, check_vma=False)
```

```python
import functools

import jax
import jax.numpy as jnp
from jax import lax
from jax.experimental import pallas as pl
from jax.experimental.pallas import tpu as pltpu
from jax.sharding import PartitionSpec as P

STEPS = 4
KAPPA = 0.5
BETA = 0.3
TERMS = STEPS + 1
LINES = TERMS + 1
META = TERMS
MIB = 1 << 20
VMEM = pltpu.VMEM
SMEM = pltpu.SMEM
HBM = pltpu.HBM
UNROLL = 10


def in_hbm(*arrays):
    return [pltpu.with_memory_space_constraint(array, HBM) for array in arrays]


def params(mib):
    return pltpu.CompilerParams(vmem_limit_bytes=mib * MIB)


def surface_kernel(maps_hbm, patch_hbm, material_hbm, layer_hbm, out_hbm, out, maps, patch_ref, material_ref, layer, vectors, scalars, sems):
    mats, _, depth = maps.shape
    slots, _, width = layer.shape
    chunks = (sems.shape[0] - 3) // 2
    block = slots // chunks
    small = [
        pltpu.make_async_copy(maps_hbm, maps, sems.at[2 * chunks]),
        pltpu.make_async_copy(patch_hbm, patch_ref, sems.at[2 * chunks + 1]),
        pltpu.make_async_copy(material_hbm, material_ref, sems.at[2 * chunks + 2]),
    ]
    large = [
        pltpu.make_async_copy(
            layer_hbm.at[pl.ds(i * block, block)], layer.at[pl.ds(i * block, block)], sems.at[i]
        )
        for i in range(chunks)
    ]
    for copy in small + large:
        copy.start()

    lane = lax.broadcasted_iota(jnp.int32, (1, width), 1)
    first = lax.broadcasted_iota(jnp.int32, (depth, 1), 0) == 0
    small[0].wait()
    matrices = [maps[mat] for mat in range(mats)]
    turned = [matrix.T for matrix in matrices]
    rows = [matrix[0:1, :] for matrix in matrices]
    cols = [matrix[:, 0:1] for matrix in turned]
    kept = [jnp.zeros((1, width), jnp.float32)] * mats
    for n in range(TERMS):
        for mat in range(mats):
            if n > 0:
                rows[mat], cols[mat] = (
                    jnp.sum(matrices[mat] * cols[mat], axis=0, keepdims=True),
                    jnp.sum(turned[mat] * rows[mat], axis=1, keepdims=True),
                )
            scaled = jnp.where(first, (1.0 - KAPPA) * cols[mat], cols[mat])
            vectors[mat, n] = jnp.broadcast_to(scaled, (depth, width))
            kept[mat] = jnp.where(lane == n + 1, cols[mat][0:1, 0:1], kept[mat])
    for mat in range(mats):
        scalars[mat] = jnp.broadcast_to(kept[mat], (8, width))
    small[1].wait()
    small[2].wait()

    def one(j, carry):
        patch = patch_ref[j]
        mat = material_ref[patch]
        sums = [jnp.zeros((8, width), jnp.float32)] * TERMS
        for c in range(depth // 8):
            part = layer[j, pl.ds(8 * c, 8), :]
            sums = [
                s + vectors[mat, n, pl.ds(8 * c, 8), :] * part for n, s in enumerate(sums)
            ]
        rows = [jnp.sum(s, axis=0, keepdims=True) for s in sums]
        scalar_row = jnp.where(lane == 0, patch.astype(jnp.float32), scalars[mat][0:1, :])
        for n, row in enumerate([*rows, scalar_row]):
            out[pl.ds(LINES * j + n, 1), :] = row
        return carry

    sends = shares_of(out, out_hbm, sems, chunks, chunks)
    for i in range(chunks):
        large[i].wait()
        lax.fori_loop(i * block, (i + 1) * block, one, 0, unroll=4)
        sends[i].start()
    for send in sends:
        send.wait()


def surface_rows(layer_maps, slot_patch, patch_material, layer_state):
    slots, depth, width = layer_state.shape
    mats = layer_maps.shape[0]
    chunks = 8
    return pl.pallas_call(
        surface_kernel,
        in_specs=[pl.BlockSpec(memory_space=HBM)] * 4,
        out_specs=pl.BlockSpec(memory_space=HBM),
        out_shape=HBM((slots * LINES, width), jnp.float32),
        scratch_shapes=[
            pltpu.VMEM((slots * LINES, width), jnp.float32),
            pltpu.VMEM((mats, depth, depth), jnp.float32),
            pltpu.SMEM(slot_patch.shape, jnp.int32),
            pltpu.SMEM(patch_material.shape, jnp.int32),
            pltpu.VMEM((slots, depth, width), jnp.float32),
            pltpu.VMEM((mats, TERMS, depth, width), jnp.float32),
            pltpu.VMEM((mats, 8, width), jnp.float32),
            pltpu.SemaphoreType.DMA((2 * chunks + 3,)),
        ],
        compiler_params=params(24),
        name="surface_rows",
    )(*in_hbm(layer_maps, slot_patch, patch_material, layer_state))


def bits(index, low, count):
    return jnp.bitwise_and(jnp.right_shift(index, low), (1 << count) - 1)


class Place:
    def __init__(self, cells_z, cells_x, parts):
        self.parts, self.x, self.z = (n.bit_length() - 1 for n in (parts, cells_x, cells_z))

    def part(self, index):
        return bits(index, 0, self.parts)

    def x_of(self, index):
        return bits(index, self.parts, self.x)

    def x_low(self, index):
        return bits(index, self.parts, 3)

    def tile(self, index):
        group = bits(index, self.parts + 3, self.x - 3)
        return bits(index, self.parts + self.x, self.z), jnp.left_shift(group, 3)

    def z_or_past(self, index):
        return bits(index, self.parts + self.x, self.z + 1)


def pick(rows_ref, fields, picked, tiles):
    slots, width = picked.shape[1:]
    cells_z, cells_x, along = fields[0].shape
    place = Place(cells_z, cells_x, along // width)

    def fetch(k, carry):
        index = rows_ref[k]
        z, first = place.tile(index)
        lines = pl.ds(pl.multiple_of(first, 8), 8)
        lanes = pl.ds(pl.multiple_of(place.part(index) * width, width), width)
        for side, field in enumerate(fields):
            tiles[side, pl.ds(pl.multiple_of(8 * k, 8), 8), :] = field[z, lines, lanes]
        return carry

    lax.fori_loop(0, slots, fetch, 0, unroll=16)

    def choose(k, carry):
        line = 8 * k + place.x_low(rows_ref[k])
        for side in range(len(fields)):
            picked[side, pl.ds(k, 1), :] = tiles[side, pl.ds(line, 1), :]
        return carry

    lax.fori_loop(0, slots, choose, 0, unroll=16)


def even(axis):
    return lax.axis_index(axis) % 2 == 0


def at_start(axis):
    return lax.axis_index(axis) == 0


def at_end(axis):
    return lax.axis_index(axis) == lax.axis_size(axis) - 1


def outgoing(axis, low, high):
    choice = even(axis)
    return jnp.where(choice, low, high), jnp.where(choice, high, low)


def incoming(axis, outer, inner):
    choice = even(axis)
    before = jnp.where(at_start(axis), 0.0, jnp.where(choice, outer, inner))
    after = jnp.where(at_end(axis), 0.0, jnp.where(choice, inner, outer))
    return before, after


def keep_sides(cells, side, z, x_outer, x_inner):
    last_x, width = cells.shape[0] - 1, x_outer.shape[3]
    for part in range(x_outer.shape[1]):
        lanes = slice(part * width, (part + 1) * width)
        x_outer[side, part, pl.ds(z, 1), :], x_inner[side, part, pl.ds(z, 1), :] = outgoing(
            "gx", cells[0:1, lanes], cells[last_x : last_x + 1, lanes]
        )


def side_row(plane, side, z):
    parts = plane.shape[1]
    return jnp.concatenate([plane[side, part, pl.ds(z, 1), :] for part in range(parts)], axis=1)


def keep_edges(z_planes, side, z_outer, z_inner):
    z_outer[side], z_inner[side] = outgoing("gz", *z_planes)


def edges_kernel(field_hbm, adjoint_hbm, field, adjoint, x_outer, x_inner, z_outer, z_inner, sems):
    copies = [
        pltpu.make_async_copy(field_hbm, field, sems.at[0]),
        pltpu.make_async_copy(adjoint_hbm, adjoint, sems.at[1]),
    ]
    for copy in copies:
        copy.start()
    for side, array in enumerate((field, adjoint)):
        copies[side].wait()

        def one(z, carry):
            keep_sides(array[z], side, z, x_outer, x_inner)
            return carry

        lax.fori_loop(0, array.shape[0], one, 0, unroll=8)
        keep_edges((array[0], array[array.shape[0] - 1]), side, z_outer, z_inner)


def edge_shapes(field, width):
    cells_z, cells_x, along = field.shape
    f32 = jnp.float32
    x_shape = jax.ShapeDtypeStruct((2, along // width, cells_z, width), f32)
    z_shape = jax.ShapeDtypeStruct((2, cells_x, along), f32)
    return [x_shape, x_shape, z_shape, z_shape]


def first_edges(field, adjoint, width):
    return pl.pallas_call(
        edges_kernel,
        in_specs=[pl.BlockSpec(memory_space=HBM)] * 2,
        out_specs=[pl.BlockSpec(memory_space=VMEM)] * 6,
        out_shape=[jax.ShapeDtypeStruct(field.shape, jnp.float32)] * 2 + edge_shapes(field, width),
        scratch_shapes=[pltpu.SemaphoreType.DMA((2,))],
        compiler_params=params(8),
        name="edges",
    )(*in_hbm(field, adjoint))


def couple(rows_ref, change, coupling):
    parts, heights, cells_x = coupling.shape[0] // 2, coupling.shape[1], coupling.shape[2]
    place = Place(heights // 2, cells_x, parts)

    def put(k, carry):
        index = rows_ref[k]
        z, x, part = place.z_or_past(index), place.x_of(index), place.part(index)
        for side in range(2):
            coupling[side * parts + part, z, pl.ds(x, 1), :] = change[side, pl.ds(k, 1), :]
        return carry

    lax.fori_loop(0, change.shape[1], put, 0, unroll=16)


def clear(coupling):
    heights = coupling.shape[1] // 2
    coupling[:, :heights] = jnp.zeros((coupling.shape[0], heights, *coupling.shape[2:]), jnp.float32)


def local_planes(fields, befores, outs, speed2, extra, sends=None, arrivals=None, lag=0):
    cells_z = speed2.shape[0]

    def plane(z, below, above):
        speed = speed2[z]
        for side in range(2):
            now = fields[side]
            beside = below(now) + above(now)
            outs[side][z] = stencil(now[z], befores[side][z], speed, beside, extra(side, z))

    def inner(z, carry):
        plane(z, lambda now: now[z - 1], lambda now: now[z + 1])
        return carry

    shares = len(sends or arrivals or ((),))
    share = cells_z // shares
    for i in range(shares):
        for copy in arrivals[i] if arrivals else ():
            copy.wait()
        start, stop = max(i * share - lag, 1), (i + 1) * share - lag
        if i == 0:
            plane(0, lambda now: 0.0, lambda now: now[1])
        if i == shares - 1:
            plane(cells_z - 1, lambda now: now[cells_z - 2], lambda now: 0.0)
            stop = cells_z - 1
        lax.fori_loop(start, stop, inner, 0, unroll=min(stop - start, UNROLL))
        for send in sends[i] if sends else ():
            send.start()


def stencil(cells, before, speed, beside, extra):
    cells_x, along = cells.shape
    row_id = lax.broadcasted_iota(jnp.int32, cells.shape, 0)
    lane_id = lax.broadcasted_iota(jnp.int32, cells.shape, 1)
    beside = beside + jnp.where(row_id == 0, 0.0, pltpu.roll(cells, 1, axis=0))
    beside = beside + jnp.where(row_id == cells_x - 1, 0.0, pltpu.roll(cells, cells_x - 1, axis=0))
    beside = beside + jnp.where(lane_id == 0, 0.0, pltpu.roll(cells, 1, axis=1))
    beside = beside + jnp.where(lane_id == along - 1, 0.0, pltpu.roll(cells, along - 1, axis=1))
    return 2.0 * cells - before + speed * (beside - 6.0 * cells) + extra


def shares_of(source, target, sems, first, count):
    share = source.shape[0] // count
    return [
        pltpu.make_async_copy(
            source.at[pl.ds(i * share, share)], target.at[pl.ds(i * share, share)], sems.at[first + i]
        )
        for i in range(count)
    ]


def arrivals_of(pairs, sems, first, count):
    loads = [
        shares_of(source, target, sems, first + i * count, count)
        for i, (source, target) in enumerate(pairs)
    ]
    arrivals = [[copies[i] for copies in loads] for i in range(count)]
    for copies in arrivals:
        for copy in copies:
            copy.start()
    return arrivals


class Lines:
    def __init__(self, ref, slots):
        self.ref, self.slots = ref, slots
        self.meta = self.row(META + 1)

    def row(self, n):
        return self.ref[pl.ds(n - 1, self.slots, stride=LINES), :]

    def scalar(self, n):
        return self.meta[:, n : n + 1]

    def surface(self, step, pushes, side):
        new = self.row(step + 1) if side == 0 else None
        for t in range(step + 1):
            term = self.scalar(step + 1 - t) * pushes[t][side]
            new = term if new is None else new + term
        return new


def extra_of(coupling, side, z):
    parts = coupling.shape[0] // 2
    return jnp.concatenate([coupling[side * parts + part, z] for part in range(parts)], axis=1)


def couple_step(rows_ref, lines, step, pushes, picked, surface, change, coupling):
    for side in range(2):
        surface[side] = lines.surface(step, pushes, side)
        change[side] = BETA * (surface[side] - picked[side])
    couple(rows_ref, change, coupling)


def x_added(speed_first, speed_last, from_outer, from_inner, side, z, shape):
    row_id = lax.broadcasted_iota(jnp.int32, shape, 0)
    low, high = incoming("gx", side_row(from_outer, side, z), side_row(from_inner, side, z))
    low, high = speed_first * low, speed_last * high
    return jnp.where(row_id == 0, low, jnp.where(row_id == shape[0] - 1, high, 0.0))


def border_planes(partials, speed2, halos, outs, edges, extra, arrivals=((),)):
    x_from_outer, x_from_inner, z_from_outer, z_from_inner = halos
    x_outer, x_inner, z_outer, z_inner = edges
    cells_z, cells_x, along = speed2.shape
    z_halos = [incoming("gz", z_from_outer[side], z_from_inner[side]) for side in range(2)]

    def plane(z, side, more):
        first, last = speed2[z, 0:1, :], speed2[z, cells_x - 1 : cells_x, :]
        new = partials[side][z] + x_added(
            first, last, x_from_outer, x_from_inner, side, z, (cells_x, along)
        )
        if extra is not None:
            new = new + extra(side, z)
        if more is not None:
            new = new + speed2[z] * more
        outs[side][z] = new
        keep_sides(new, side, z, x_outer, x_inner)

    def inner(z, carry):
        for side in range(2):
            plane(z, side, None)
        return carry

    shares = len(arrivals)
    share = cells_z // shares
    for i, copies in enumerate(arrivals):
        for copy in copies:
            copy.wait()
        start, stop = max(i * share, 1), min((i + 1) * share, cells_z - 1)
        for side in range(2):
            if i == 0:
                plane(0, side, z_halos[side][0])
            if i == shares - 1:
                plane(cells_z - 1, side, z_halos[side][1])
        lax.fori_loop(start, stop, inner, 0, unroll=min(stop - start, UNROLL))
    for side in range(2):
        keep_edges((outs[side][0], outs[side][cells_z - 1]), side, z_outer, z_inner)


def first_local_kernel(rows_hbm, field_prev_hbm, adjoint_prev_hbm, speed2_hbm, field, adjoint, out_hbm, adjoint_out_hbm, push, picked, rows_ref, field_prev, adjoint_prev, speed2, out, adjoint_out, tiles, sems):
    shares = 4
    rows_load = pltpu.make_async_copy(rows_hbm, rows_ref, sems.at[0])
    rows_load.start()
    pairs = ((speed2_hbm, speed2), (field_prev_hbm, field_prev), (adjoint_prev_hbm, adjoint_prev))
    arrivals = arrivals_of(pairs, sems, 14, shares)
    rows_load.wait()
    pick(rows_ref, (field, adjoint), picked, tiles)
    push[...] = KAPPA * picked[...]
    sends = list(
        zip(
            shares_of(out, out_hbm, sems, 6, 4), shares_of(adjoint_out, adjoint_out_hbm, sems, 10, 4)
        )
    )
    local_planes(
        (field, adjoint),
        (field_prev, adjoint_prev),
        (out, adjoint_out),
        speed2,
        lambda side, z: 0.0,
        sends,
        arrivals,
    )
    for pair in sends:
        for send in pair:
            send.wait()


def first_local(rows, field, field_prev, adjoint, adjoint_prev, speed2, slots, width):
    rows_shape = jax.ShapeDtypeStruct((2, slots, width), jnp.float32)
    return pl.pallas_call(
        first_local_kernel,
        in_specs=[pl.BlockSpec(memory_space=HBM)] * 4 + [pl.BlockSpec(memory_space=VMEM)] * 2,
        out_specs=[pl.BlockSpec(memory_space=HBM)] * 2 + [pl.BlockSpec(memory_space=VMEM)] * 2,
        out_shape=[HBM(field.shape, jnp.float32)] * 2 + [rows_shape] * 2,
        scratch_shapes=[pltpu.SMEM((slots,), jnp.int32)]
        + [pltpu.VMEM(field.shape, jnp.float32)] * 5
        + [pltpu.VMEM((2, 8 * slots, width), jnp.float32), pltpu.SemaphoreType.DMA((26,))],
        compiler_params=params(16),
        cost_estimate=pl.CostEstimate(flops=8 << 20, bytes_accessed=12 << 20, transcendentals=0),
        name="local0",
    )(*in_hbm(rows, field_prev, adjoint_prev, speed2), field, adjoint)


def first_border_kernel(rows_ref, partial_hbm, partial_adjoint_hbm, speed2_hbm, x_from_outer, x_from_inner, z_from_outer, z_from_inner, lines_ref, push, picked, out, adjoint_out, speed2, x_outer, x_inner, z_outer, z_inner, surface, partial, partial_adjoint, coupling, change, sems):
    shares = 4
    loads = [
        shares_of(source, target, sems, shares * i, shares)
        for i, (source, target) in enumerate(
            ((speed2_hbm, speed2), (partial_hbm, partial), (partial_adjoint_hbm, partial_adjoint))
        )
    ]
    arrivals = [[copies[i] for copies in loads] for i in range(shares)]
    for copies in arrivals:
        for copy in copies:
            copy.start()
    clear(coupling)
    lines = Lines(lines_ref, change.shape[1])
    couple_step(rows_ref, lines, 0, [push], picked, surface, change, coupling)
    border_planes(
        (partial, partial_adjoint),
        speed2,
        (x_from_outer, x_from_inner, z_from_outer, z_from_inner),
        (out, adjoint_out),
        (x_outer, x_inner, z_outer, z_inner),
        functools.partial(extra_of, coupling),
        arrivals,
    )


def coupling_scratch(field, slots, width):
    cells_z, cells_x, along = field.shape
    return [
        pltpu.VMEM((2 * (along // width), 2 * cells_z, cells_x, width), jnp.float32),
        pltpu.VMEM((2, slots, width), jnp.float32),
    ]


def first_border(rows, partials, speed2, halos, lines, push, picked):
    _, slots, width = push.shape
    field = partials[0]
    whole = jax.ShapeDtypeStruct(field.shape, jnp.float32)
    in_vmem = pl.BlockSpec(memory_space=VMEM)
    return pl.pallas_call(
        first_border_kernel,
        in_specs=[pl.BlockSpec(memory_space=SMEM)]
        + [pl.BlockSpec(memory_space=HBM)] * 3
        + [in_vmem] * 7,
        out_specs=[in_vmem] * 8,
        out_shape=[whole] * 3
        + edge_shapes(field, width)
        + [jax.ShapeDtypeStruct((2, slots, width), jnp.float32)],
        scratch_shapes=[pltpu.VMEM(field.shape, jnp.float32)] * 2
        + coupling_scratch(field, slots, width)
        + [pltpu.SemaphoreType.DMA((12,))],
        compiler_params=params(14),
        name="border0",
    )(rows, *in_hbm(*partials, speed2), *halos, lines, push, picked)


def local_kernel(step, rows_ref, field, field_prev, adjoint, adjoint_prev, speed2, lines_ref, surface, *refs):
    pushes, refs = list(refs[:step]), refs[step:]
    out, adjoint_out, push, next_surface = refs[:4]
    sends = []
    if step == STEPS - 2:
        sends = [
            pltpu.make_async_copy(source, target, refs[-1].at[i])
            for i, (source, target) in enumerate(zip((field, adjoint), refs[4:6]))
        ]
        refs = refs[:4] + refs[6:-1]
    for send in sends:
        send.start()
    coupling, change, tiles, picked = refs[4:8]
    loads = []
    if step == 1:
        *held, sems = refs[8:]
        loads = [
            pltpu.make_async_copy(source, target, sems.at[i])
            for i, (source, target) in enumerate(zip((field_prev, adjoint_prev), held))
        ]
        field_prev, adjoint_prev = held
    for copy in loads:
        copy.start()
    pick(rows_ref, (field, adjoint), picked, tiles)
    push[...] = KAPPA * (picked[...] - surface[...])
    clear(coupling)
    lines = Lines(lines_ref, change.shape[1])
    couple_step(rows_ref, lines, step, pushes + [push], picked, next_surface, change, coupling)
    for copy in loads:
        copy.wait()
    local_planes(
        (field, adjoint),
        (field_prev, adjoint_prev),
        (out, adjoint_out),
        speed2,
        functools.partial(extra_of, coupling),
    )
    for send in sends:
        send.wait()


def local_step(step, rows, field, field_prev, adjoint, adjoint_prev, speed2, lines, surface, pushes):
    _, slots, width = surface.shape
    whole = jax.ShapeDtypeStruct(field.shape, jnp.float32)
    rows_shape = jax.ShapeDtypeStruct(surface.shape, jnp.float32)
    in_vmem = pl.BlockSpec(memory_space=VMEM)
    before, held, kept = in_vmem, [], []
    if step == STEPS - 2:
        kept = [HBM(field.shape, jnp.float32)] * 2
        held = [pltpu.SemaphoreType.DMA((2,))]
    if step == 1:
        before = pl.BlockSpec(memory_space=HBM)
        held = [pltpu.VMEM(field.shape, jnp.float32)] * 2 + [pltpu.SemaphoreType.DMA((2,))]
        field_prev, adjoint_prev = in_hbm(field_prev, adjoint_prev)
    return pl.pallas_call(
        functools.partial(local_kernel, step),
        in_specs=[pl.BlockSpec(memory_space=SMEM), in_vmem, before, in_vmem, before]
        + [in_vmem] * (3 + step),
        out_specs=[in_vmem] * 4 + [pl.BlockSpec(memory_space=HBM)] * len(kept),
        out_shape=[whole, whole, rows_shape, rows_shape, *kept],
        scratch_shapes=coupling_scratch(field, slots, width)
        + [
            pltpu.VMEM((2, 8 * slots, width), jnp.float32),
            pltpu.VMEM((2, slots, width), jnp.float32),
        ]
        + held,
        compiler_params=params(12),
        cost_estimate=pl.CostEstimate(flops=8 << 20, bytes_accessed=12 << 20, transcendentals=0),
        name=f"local{step}",
    )(rows, field, field_prev, adjoint, adjoint_prev, speed2, lines, surface, *pushes)


def border_kernel(partial, partial_adjoint, speed2, x_from_outer, x_from_inner, z_from_outer, z_from_inner, out, adjoint_out, *edges):
    border_planes(
        (partial, partial_adjoint),
        speed2,
        (x_from_outer, x_from_inner, z_from_outer, z_from_inner),
        (out, adjoint_out),
        edges,
        None,
    )


def border_step(step, partials, speed2, halos, width):
    field = partials[0]
    whole = jax.ShapeDtypeStruct(field.shape, jnp.float32)
    in_vmem = pl.BlockSpec(memory_space=VMEM)
    return pl.pallas_call(
        border_kernel,
        in_specs=[in_vmem] * 7,
        out_specs=[in_vmem] * 6,
        out_shape=[whole, whole] + edge_shapes(field, width),
        compiler_params=params(8),
        name=f"border{step}",
    )(*partials, speed2, *halos)


def correlation_kernel(rows_ref, used, field, adjoint, lines_ref, surface, *refs):
    pushes, refs = list(refs[: STEPS - 1]), refs[STEPS - 1 :]
    gradient_hbm, change = refs[:2]
    targets, (gradient, tiles, picked, push, sems) = refs[2:4], refs[4:]
    sends = [
        pltpu.make_async_copy(source, target, sems.at[i])
        for i, (source, target) in enumerate(zip((field, adjoint), targets))
    ]
    for send in sends:
        send.start()
    pick(rows_ref, (field, adjoint), picked, tiles)
    push[...] = KAPPA * (picked[...] - surface[...])

    slots, width = change.shape[1:]
    lines = Lines(lines_ref, slots)
    known = pushes + [push]
    total = jnp.zeros((slots, width), jnp.float32)
    for late in range(STEPS):
        inside = (STEPS - late) * lines.row(TERMS - late)
        for t in range(STEPS - late):
            scale = (STEPS - late - t) * lines.scalar(TERMS - late - t)
            inside = inside + scale * known[t][0]
        total = total + known[late][1] * inside
    patches = gradient.shape[0]
    parts, rest = [], total
    for _ in range(3):
        parts.append(rest.astype(jnp.bfloat16))
        rest = rest - parts[-1].astype(jnp.float32)
    ids = lines.meta.T[0:1, :].astype(jnp.int32)
    ids = jnp.where(used[...] >= 0, ids, -1)
    owners = lax.broadcasted_iota(jnp.int32, (patches, slots), 0) == ids
    sums = jnp.dot(
        jnp.where(owners, 1.0, 0.0).astype(jnp.bfloat16),
        jnp.concatenate(parts, axis=1),
        preferred_element_type=jnp.float32,
    )
    gradient[...] = sums[:, :width] + (sums[:, width : 2 * width] + sums[:, 2 * width :])
    sends.append(pltpu.make_async_copy(gradient, gradient_hbm, sems.at[2]))
    sends[-1].start()

    for side in range(2):
        change[side] = BETA * (lines.surface(STEPS - 1, known, side) - picked[side])
    for send in sends:
        send.wait()


def correlate(rows, field, adjoint, lines, surface, pushes, patches):
    _, slots, width = surface.shape
    f32 = jnp.float32
    in_vmem = pl.BlockSpec(memory_space=VMEM)
    return pl.pallas_call(
        correlation_kernel,
        in_specs=[pl.BlockSpec(memory_space=SMEM)] + [in_vmem] * (5 + len(pushes)),
        out_specs=[pl.BlockSpec(memory_space=HBM), in_vmem] + [pl.BlockSpec(memory_space=HBM)] * 2,
        out_shape=[
            HBM((patches, width), f32),
            jax.ShapeDtypeStruct(surface.shape, f32),
        ]
        + [HBM(field.shape, f32)] * 2,
        scratch_shapes=[
            pltpu.VMEM((patches, width), f32),
            pltpu.VMEM((2, 8 * slots, width), f32),
        ]
        + [pltpu.VMEM((2, slots, width), f32)] * 2
        + [pltpu.SemaphoreType.DMA((3,))],
        compiler_params=params(10),
        name="correlation",
    )(rows, rows.reshape(1, slots), field, adjoint, lines, surface, *pushes)


def last_local_kernel(rows_hbm, field_hbm, field_prev_hbm, adjoint_hbm, adjoint_prev_hbm, speed2_hbm, change, out, adjoint_out, speed_first, speed_last, speed_ends, rows_ref, field, field_prev, adjoint, adjoint_prev, speed2, coupling, sems):
    shares = 4
    rows_load = pltpu.make_async_copy(rows_hbm, rows_ref, sems.at[0])
    rows_load.start()
    pairs = (
        (speed2_hbm, speed2),
        (field_hbm, field),
        (adjoint_hbm, adjoint),
        (field_prev_hbm, field_prev),
        (adjoint_prev_hbm, adjoint_prev),
    )
    arrivals = arrivals_of(pairs, sems, 1, shares)
    clear(coupling)
    rows_load.wait()
    couple(rows_ref, change, coupling)
    local_planes(
        (field, adjoint),
        (field_prev, adjoint_prev),
        (out, adjoint_out),
        speed2,
        functools.partial(extra_of, coupling),
        None,
        arrivals,
        1,
    )
    cells_z = speed2.shape[0]
    speed_ends[0], speed_ends[1] = speed2[0], speed2[cells_z - 1]

    def sides(z, carry):
        keep_side(speed2[z], z, speed_first, speed_last)
        return carry

    lax.fori_loop(0, cells_z, sides, 0, unroll=8)


def last_local(rows, field, field_prev, adjoint, adjoint_prev, speed2, change):
    _, slots, width = change.shape
    cells_z, cells_x, along = field.shape
    sides = jax.ShapeDtypeStruct((along // width, cells_z, width), jnp.float32)
    in_vmem = pl.BlockSpec(memory_space=VMEM)
    return pl.pallas_call(
        last_local_kernel,
        in_specs=[pl.BlockSpec(memory_space=HBM)] * 6 + [in_vmem],
        out_specs=[in_vmem] * 5,
        out_shape=[jax.ShapeDtypeStruct(field.shape, jnp.float32)] * 2
        + [sides, sides, jax.ShapeDtypeStruct((2, cells_x, along), jnp.float32)],
        scratch_shapes=[pltpu.SMEM((slots,), jnp.int32)]
        + [pltpu.VMEM(field.shape, jnp.float32)] * 5
        + coupling_scratch(field, slots, width)[:1]
        + [pltpu.SemaphoreType.DMA((21,))],
        compiler_params=params(16),
        cost_estimate=pl.CostEstimate(flops=8 << 20, bytes_accessed=12 << 20, transcendentals=0),
        name=f"local{STEPS - 1}",
    )(*in_hbm(rows, field, field_prev, adjoint, adjoint_prev, speed2), change)


def keep_side(cells, z, first, last):
    last_x, width = cells.shape[0] - 1, first.shape[2]
    for part in range(first.shape[0]):
        lanes = slice(part * width, (part + 1) * width)
        first[part, pl.ds(z, 1), :] = cells[0:1, lanes]
        last[part, pl.ds(z, 1), :] = cells[last_x : last_x + 1, lanes]


def finish_kernel(field_in, adjoint_in, speed_first, speed_last, speed_ends, x_from_outer, x_from_inner, z_from_outer, z_from_inner, out_hbm, adjoint_out_hbm, field, adjoint, sems):
    cells_z, cells_x, along = field.shape
    parts = speed_first.shape[0]
    shares = 4
    share = cells_z // shares
    sends = [
        shares_of(field, out_hbm, sems, 0, shares),
        shares_of(adjoint, adjoint_out_hbm, sems, shares, shares),
    ]
    for i in range(shares):
        for side, (source, held) in enumerate(((field_in, field), (adjoint_in, adjoint))):

            def one(z, carry):
                first, last = (
                    jnp.concatenate([ref[p, pl.ds(z, 1), :] for p in range(parts)], axis=1)
                    for ref in (speed_first, speed_last)
                )
                held[z] = source[z] + x_added(
                    first, last, x_from_outer, x_from_inner, side, z, (cells_x, along)
                )
                return carry

            lax.fori_loop(i * share, (i + 1) * share, one, 0, unroll=share)
            before, after = incoming("gz", z_from_outer[side], z_from_inner[side])
            if i == 0:
                held[0] = held[0] + speed_ends[0] * before
            if i == shares - 1:
                held[cells_z - 1] = held[cells_z - 1] + speed_ends[1] * after
            sends[side][i].start()
    for side in range(2):
        for send in sends[side]:
            send.wait()


def finish_call(field, adjoint, speed_first, speed_last, speed_ends, halos):
    return pl.pallas_call(
        finish_kernel,
        in_specs=[pl.BlockSpec(memory_space=VMEM)] * 9,
        out_specs=[pl.BlockSpec(memory_space=HBM)] * 2,
        out_shape=[HBM(field.shape, jnp.float32)] * 2,
        scratch_shapes=[pltpu.VMEM(field.shape, jnp.float32)] * 2 + [pltpu.SemaphoreType.DMA((8,))],
        compiler_params=params(8),
        name="finish",
    )(field, adjoint, speed_first, speed_last, speed_ends, *halos)


def swaps(axis, first):
    count = lax.axis_size(axis)
    if first:
        return [(i, i ^ 1) for i in range(count)]
    return [(i, (i + 1 if i % 2 else i - 1) % count) for i in range(count)]


def exchange(edges):
    axes = (("gx", False), ("gx", True), ("gz", False), ("gz", True))
    return [lax.ppermute(edge, axis, swaps(axis, first)) for edge, (axis, first) in zip(edges, axes)]


def body(
    pressure_now,
    pressure_prev,
    adjoint_now,
    adjoint_prev,
    speed2,
    layer_state,
    layer_maps,
    send_rows,
    slot_patch,
    patch_material,
):
    slots, _, width = layer_state.shape
    patches = patch_material.shape[0]
    devices = lax.axis_size(("gx", "gz"))
    rows = send_rows.reshape(-1)

    field, adjoint, *edges = first_edges(pressure_now, adjoint_now, width)
    halos = exchange(edges)
    lines = surface_rows(layer_maps, slot_patch, patch_material, layer_state)
    lines = lines.reshape(slots, 1, LINES * width)
    lines = lax.all_to_all(lines, ("gx", "gz"), split_axis=0, concat_axis=0, tiled=True)
    lines = lines.reshape(slots * LINES, width)

    *partials, push, picked = first_local(
        rows, field, pressure_prev, adjoint, adjoint_prev, speed2, slots, width
    )
    pushes = [push]
    field, adjoint, speed, *edges, surface = first_border(
        rows, partials, speed2, halos, lines, push, picked
    )
    field_prev, adjoint_prev = pressure_now, adjoint_now
    for step in range(1, STEPS - 1):
        halos = exchange(edges)
        field_next, adjoint_next, push, surface, *sent = local_step(
            step, rows, field, field_prev, adjoint, adjoint_prev, speed, lines, surface, pushes
        )
        partials = (field_next, adjoint_next)
        pushes.append(push)
        field_prev, adjoint_prev = field, adjoint
        field, adjoint, *edges = border_step(step, partials, speed, halos, width)
    halos = exchange(edges)
    gradient, change, *held = correlate(
        rows, field, adjoint, lines, surface, pushes, patches
    )
    parts = gradient.reshape(devices, patches // devices, width)
    parts = lax.all_to_all(parts, ("gx", "gz"), split_axis=0, concat_axis=0, tiled=True)
    *partials, first, last, ends = last_local(
        rows, held[0], sent[0], held[1], sent[1], speed2, change
    )
    field, adjoint = finish_call(*partials, first, last, ends, halos)
    return field, adjoint, jnp.sum(parts, axis=0)


def solution(mesh):
    grid = P("gz", "gx", None)
    split = P(("gx", "gz"), None, None)
    in_specs = (grid, grid, grid, grid, grid, split, P(), split, P(("gx", "gz")), P())
    out_specs = (grid, grid, P(("gx", "gz"), None))
    return jax.shard_map(body, mesh=mesh, in_specs=in_specs, out_specs=out_specs, check_vma=False)
```

```python
import functools

import jax
import jax.numpy as jnp
from jax import lax
from jax.experimental import pallas as pl
from jax.experimental.pallas import tpu as pltpu
from jax.sharding import PartitionSpec as P

STEPS = 4
KAPPA = 0.5
BETA = 0.3
TERMS = STEPS + 1
LINES = TERMS + 1
META = TERMS
MIB = 1 << 20
VMEM = pltpu.VMEM
SMEM = pltpu.SMEM
HBM = pltpu.HBM
UNROLL = 30


def in_hbm(*arrays):
    return [pltpu.with_memory_space_constraint(array, HBM) for array in arrays]


def params(mib):
    return pltpu.CompilerParams(vmem_limit_bytes=mib * MIB)


def surface_kernel(maps_hbm, patch_hbm, material_hbm, layer_hbm, out_hbm, out, maps, patch_ref, material_ref, layer, vectors, scalars, sems):
    mats, _, depth = maps.shape
    slots, _, width = layer.shape
    chunks = (sems.shape[0] - 3) // 2
    block = slots // chunks
    small = [
        pltpu.make_async_copy(maps_hbm, maps, sems.at[2 * chunks]),
        pltpu.make_async_copy(patch_hbm, patch_ref, sems.at[2 * chunks + 1]),
        pltpu.make_async_copy(material_hbm, material_ref, sems.at[2 * chunks + 2]),
    ]
    large = [
        pltpu.make_async_copy(
            layer_hbm.at[pl.ds(i * block, block)], layer.at[pl.ds(i * block, block)], sems.at[i]
        )
        for i in range(chunks)
    ]
    for copy in small + large:
        copy.start()

    lane = lax.broadcasted_iota(jnp.int32, (1, width), 1)
    first = lax.broadcasted_iota(jnp.int32, (depth, 1), 0) == 0
    small[0].wait()
    matrices = [maps[mat] for mat in range(mats)]
    turned = [matrix.T for matrix in matrices]
    rows = [matrix[0:1, :] for matrix in matrices]
    cols = [matrix[:, 0:1] for matrix in turned]
    kept = [jnp.zeros((1, width), jnp.float32)] * mats
    for n in range(TERMS):
        for mat in range(mats):
            if n > 0:
                rows[mat], cols[mat] = (
                    jnp.sum(matrices[mat] * cols[mat], axis=0, keepdims=True),
                    jnp.sum(turned[mat] * rows[mat], axis=1, keepdims=True),
                )
            scaled = jnp.where(first, (1.0 - KAPPA) * cols[mat], cols[mat])
            vectors[mat, n] = jnp.broadcast_to(scaled, (depth, width))
            kept[mat] = jnp.where(lane == n + 1, cols[mat][0:1, 0:1], kept[mat])
    for mat in range(mats):
        scalars[mat] = jnp.broadcast_to(kept[mat], (8, width))
    small[1].wait()
    small[2].wait()

    def one(j, carry):
        patch = patch_ref[j]
        mat = material_ref[patch]
        sums = [jnp.zeros((8, width), jnp.float32)] * TERMS
        for c in range(depth // 8):
            part = layer[j, pl.ds(8 * c, 8), :]
            sums = [
                s + vectors[mat, n, pl.ds(8 * c, 8), :] * part for n, s in enumerate(sums)
            ]
        rows = [jnp.sum(s, axis=0, keepdims=True) for s in sums]
        scalar_row = jnp.where(lane == 0, patch.astype(jnp.float32), scalars[mat][0:1, :])
        for n, row in enumerate([*rows, scalar_row]):
            out[pl.ds(LINES * j + n, 1), :] = row
        return carry

    sends = shares_of(out, out_hbm, sems, chunks, chunks)
    for i in range(chunks):
        large[i].wait()
        lax.fori_loop(i * block, (i + 1) * block, one, 0, unroll=4)
        sends[i].start()
    for send in sends:
        send.wait()


def surface_rows(layer_maps, slot_patch, patch_material, layer_state):
    slots, depth, width = layer_state.shape
    mats = layer_maps.shape[0]
    chunks = 8
    return pl.pallas_call(
        surface_kernel,
        in_specs=[pl.BlockSpec(memory_space=HBM)] * 4,
        out_specs=pl.BlockSpec(memory_space=HBM),
        out_shape=HBM((slots * LINES, width), jnp.float32),
        scratch_shapes=[
            pltpu.VMEM((slots * LINES, width), jnp.float32),
            pltpu.VMEM((mats, depth, depth), jnp.float32),
            pltpu.SMEM(slot_patch.shape, jnp.int32),
            pltpu.SMEM(patch_material.shape, jnp.int32),
            pltpu.VMEM((slots, depth, width), jnp.float32),
            pltpu.VMEM((mats, TERMS, depth, width), jnp.float32),
            pltpu.VMEM((mats, 8, width), jnp.float32),
            pltpu.SemaphoreType.DMA((2 * chunks + 3,)),
        ],
        compiler_params=params(24),
        name="surface_rows",
    )(*in_hbm(layer_maps, slot_patch, patch_material, layer_state))


def bits(index, low, count):
    return jnp.bitwise_and(jnp.right_shift(index, low), (1 << count) - 1)


class Place:
    def __init__(self, cells_z, cells_x, parts):
        self.parts, self.x, self.z = (n.bit_length() - 1 for n in (parts, cells_x, cells_z))

    def part(self, index):
        return bits(index, 0, self.parts)

    def x_of(self, index):
        return bits(index, self.parts, self.x)

    def x_low(self, index):
        return bits(index, self.parts, 3)

    def tile(self, index):
        group = bits(index, self.parts + 3, self.x - 3)
        return bits(index, self.parts + self.x, self.z), jnp.left_shift(group, 3)

    def z_or_past(self, index):
        return bits(index, self.parts + self.x, self.z + 1)


def pick(rows_ref, fields, picked, tiles):
    slots, width = picked.shape[1:]
    cells_z, cells_x, along = fields[0].shape
    place = Place(cells_z, cells_x, along // width)

    def fetch(k, carry):
        index = rows_ref[k]
        z, first = place.tile(index)
        lines = pl.ds(pl.multiple_of(first, 8), 8)
        lanes = pl.ds(pl.multiple_of(place.part(index) * width, width), width)
        for side, field in enumerate(fields):
            tiles[side, pl.ds(pl.multiple_of(8 * k, 8), 8), :] = field[z, lines, lanes]
        return carry

    lax.fori_loop(0, slots, fetch, 0, unroll=16)

    def choose(k, carry):
        line = 8 * k + place.x_low(rows_ref[k])
        for side in range(len(fields)):
            picked[side, pl.ds(k, 1), :] = tiles[side, pl.ds(line, 1), :]
        return carry

    lax.fori_loop(0, slots, choose, 0, unroll=16)


def even(axis):
    return lax.axis_index(axis) % 2 == 0


def at_start(axis):
    return lax.axis_index(axis) == 0


def at_end(axis):
    return lax.axis_index(axis) == lax.axis_size(axis) - 1


def outgoing(axis, low, high):
    choice = even(axis)
    return jnp.where(choice, low, high), jnp.where(choice, high, low)


def incoming(axis, outer, inner):
    choice = even(axis)
    before = jnp.where(at_start(axis), 0.0, jnp.where(choice, outer, inner))
    after = jnp.where(at_end(axis), 0.0, jnp.where(choice, inner, outer))
    return before, after


def keep_sides(cells, side, z, x_outer, x_inner):
    last_x, width = cells.shape[0] - 1, x_outer.shape[3]
    for part in range(x_outer.shape[1]):
        lanes = slice(part * width, (part + 1) * width)
        x_outer[side, part, pl.ds(z, 1), :], x_inner[side, part, pl.ds(z, 1), :] = outgoing(
            "gx", cells[0:1, lanes], cells[last_x : last_x + 1, lanes]
        )


def side_row(plane, side, z):
    parts = plane.shape[1]
    return jnp.concatenate([plane[side, part, pl.ds(z, 1), :] for part in range(parts)], axis=1)


def keep_edges(z_planes, side, z_outer, z_inner):
    z_outer[side], z_inner[side] = outgoing("gz", *z_planes)


def edges_kernel(field_hbm, adjoint_hbm, field, adjoint, x_outer, x_inner, z_outer, z_inner, sems):
    copies = [
        pltpu.make_async_copy(field_hbm, field, sems.at[0]),
        pltpu.make_async_copy(adjoint_hbm, adjoint, sems.at[1]),
    ]
    for copy in copies:
        copy.start()
    for side, array in enumerate((field, adjoint)):
        copies[side].wait()

        def one(z, carry):
            keep_sides(array[z], side, z, x_outer, x_inner)
            return carry

        lax.fori_loop(0, array.shape[0], one, 0, unroll=8)
        keep_edges((array[0], array[array.shape[0] - 1]), side, z_outer, z_inner)


def edge_shapes(field, width):
    cells_z, cells_x, along = field.shape
    f32 = jnp.float32
    x_shape = jax.ShapeDtypeStruct((2, along // width, cells_z, width), f32)
    z_shape = jax.ShapeDtypeStruct((2, cells_x, along), f32)
    return [x_shape, x_shape, z_shape, z_shape]


def first_edges(field, adjoint, width):
    return pl.pallas_call(
        edges_kernel,
        in_specs=[pl.BlockSpec(memory_space=HBM)] * 2,
        out_specs=[pl.BlockSpec(memory_space=VMEM)] * 6,
        out_shape=[jax.ShapeDtypeStruct(field.shape, jnp.float32)] * 2 + edge_shapes(field, width),
        scratch_shapes=[pltpu.SemaphoreType.DMA((2,))],
        compiler_params=params(8),
        name="edges",
    )(*in_hbm(field, adjoint))


def couple(rows_ref, change, coupling):
    parts, heights, cells_x = coupling.shape[0] // 2, coupling.shape[1], coupling.shape[2]
    place = Place(heights // 2, cells_x, parts)

    def put(k, carry):
        index = rows_ref[k]
        z, x, part = place.z_or_past(index), place.x_of(index), place.part(index)
        for side in range(2):
            coupling[side * parts + part, z, pl.ds(x, 1), :] = change[side, pl.ds(k, 1), :]
        return carry

    lax.fori_loop(0, change.shape[1], put, 0, unroll=16)


def clear(coupling):
    heights = coupling.shape[1] // 2
    coupling[:, :heights] = jnp.zeros((coupling.shape[0], heights, *coupling.shape[2:]), jnp.float32)


def local_planes(fields, befores, outs, speed2, extra, sends=None, arrivals=None, lag=0):
    cells_z = speed2.shape[0]

    def plane(z, below, above):
        speed = speed2[z]
        for side in range(2):
            now = fields[side]
            beside = below(now) + above(now)
            outs[side][z] = stencil(now[z], befores[side][z], speed, beside, extra(side, z))

    def inner(z, carry):
        plane(z, lambda now: now[z - 1], lambda now: now[z + 1])
        return carry

    shares = len(sends or arrivals or ((),))
    share = cells_z // shares
    for i in range(shares):
        for copy in arrivals[i] if arrivals else ():
            copy.wait()
        start, stop = max(i * share - lag, 1), (i + 1) * share - lag
        if i == 0:
            plane(0, lambda now: 0.0, lambda now: now[1])
        if i == shares - 1:
            plane(cells_z - 1, lambda now: now[cells_z - 2], lambda now: 0.0)
            stop = cells_z - 1
        lax.fori_loop(start, stop, inner, 0, unroll=min(stop - start, UNROLL))
        for send in sends[i] if sends else ():
            send.start()


def stencil(cells, before, speed, beside, extra):
    cells_x, along = cells.shape
    row_id = lax.broadcasted_iota(jnp.int32, cells.shape, 0)
    lane_id = lax.broadcasted_iota(jnp.int32, cells.shape, 1)
    beside = beside + jnp.where(row_id == 0, 0.0, pltpu.roll(cells, 1, axis=0))
    beside = beside + jnp.where(row_id == cells_x - 1, 0.0, pltpu.roll(cells, cells_x - 1, axis=0))
    beside = beside + jnp.where(lane_id == 0, 0.0, pltpu.roll(cells, 1, axis=1))
    beside = beside + jnp.where(lane_id == along - 1, 0.0, pltpu.roll(cells, along - 1, axis=1))
    return 2.0 * cells - before + speed * (beside - 6.0 * cells) + extra


def shares_of(source, target, sems, first, count):
    share = source.shape[0] // count
    return [
        pltpu.make_async_copy(
            source.at[pl.ds(i * share, share)], target.at[pl.ds(i * share, share)], sems.at[first + i]
        )
        for i in range(count)
    ]


def arrivals_of(pairs, sems, first, count):
    loads = [
        shares_of(source, target, sems, first + i * count, count)
        for i, (source, target) in enumerate(pairs)
    ]
    arrivals = [[copies[i] for copies in loads] for i in range(count)]
    for copies in arrivals:
        for copy in copies:
            copy.start()
    return arrivals


class Lines:
    def __init__(self, ref, slots):
        self.ref, self.slots = ref, slots
        self.meta = self.row(META + 1)

    def row(self, n):
        return self.ref[pl.ds(n - 1, self.slots, stride=LINES), :]

    def scalar(self, n):
        return self.meta[:, n : n + 1]

    def surface(self, step, pushes, side):
        new = self.row(step + 1) if side == 0 else None
        for t in range(step + 1):
            term = self.scalar(step + 1 - t) * pushes[t][side]
            new = term if new is None else new + term
        return new


def extra_of(coupling, side, z):
    parts = coupling.shape[0] // 2
    return jnp.concatenate([coupling[side * parts + part, z] for part in range(parts)], axis=1)


def couple_step(rows_ref, lines, step, pushes, picked, surface, change, coupling):
    for side in range(2):
        surface[side] = lines.surface(step, pushes, side)
        change[side] = BETA * (surface[side] - picked[side])
    couple(rows_ref, change, coupling)


def x_added(speed_first, speed_last, from_outer, from_inner, side, z, shape):
    row_id = lax.broadcasted_iota(jnp.int32, shape, 0)
    low, high = incoming("gx", side_row(from_outer, side, z), side_row(from_inner, side, z))
    low, high = speed_first * low, speed_last * high
    return jnp.where(row_id == 0, low, jnp.where(row_id == shape[0] - 1, high, 0.0))


def border_planes(partials, speed2, halos, outs, edges, extra, arrivals=((),)):
    x_from_outer, x_from_inner, z_from_outer, z_from_inner = halos
    x_outer, x_inner, z_outer, z_inner = edges
    cells_z, cells_x, along = speed2.shape
    z_halos = [incoming("gz", z_from_outer[side], z_from_inner[side]) for side in range(2)]

    def plane(z, side, more):
        first, last = speed2[z, 0:1, :], speed2[z, cells_x - 1 : cells_x, :]
        new = partials[side][z] + x_added(
            first, last, x_from_outer, x_from_inner, side, z, (cells_x, along)
        )
        if extra is not None:
            new = new + extra(side, z)
        if more is not None:
            new = new + speed2[z] * more
        outs[side][z] = new
        keep_sides(new, side, z, x_outer, x_inner)

    def inner(z, carry):
        for side in range(2):
            plane(z, side, None)
        return carry

    shares = len(arrivals)
    share = cells_z // shares
    for i, copies in enumerate(arrivals):
        for copy in copies:
            copy.wait()
        start, stop = max(i * share, 1), min((i + 1) * share, cells_z - 1)
        for side in range(2):
            if i == 0:
                plane(0, side, z_halos[side][0])
            if i == shares - 1:
                plane(cells_z - 1, side, z_halos[side][1])
        lax.fori_loop(start, stop, inner, 0, unroll=min(stop - start, UNROLL))
    for side in range(2):
        keep_edges((outs[side][0], outs[side][cells_z - 1]), side, z_outer, z_inner)


def first_local_kernel(rows_hbm, field_prev_hbm, adjoint_prev_hbm, speed2_hbm, field, adjoint, out_hbm, adjoint_out_hbm, push, picked, rows_ref, field_prev, adjoint_prev, speed2, out, adjoint_out, tiles, sems):
    shares = 4
    rows_load = pltpu.make_async_copy(rows_hbm, rows_ref, sems.at[0])
    rows_load.start()
    pairs = ((speed2_hbm, speed2), (field_prev_hbm, field_prev), (adjoint_prev_hbm, adjoint_prev))
    arrivals = arrivals_of(pairs, sems, 14, shares)
    rows_load.wait()
    pick(rows_ref, (field, adjoint), picked, tiles)
    push[...] = KAPPA * picked[...]
    sends = list(
        zip(
            shares_of(out, out_hbm, sems, 6, 4), shares_of(adjoint_out, adjoint_out_hbm, sems, 10, 4)
        )
    )
    local_planes(
        (field, adjoint),
        (field_prev, adjoint_prev),
        (out, adjoint_out),
        speed2,
        lambda side, z: 0.0,
        sends,
        arrivals,
    )
    for pair in sends:
        for send in pair:
            send.wait()


def first_local(rows, field, field_prev, adjoint, adjoint_prev, speed2, slots, width):
    rows_shape = jax.ShapeDtypeStruct((2, slots, width), jnp.float32)
    return pl.pallas_call(
        first_local_kernel,
        in_specs=[pl.BlockSpec(memory_space=HBM)] * 4 + [pl.BlockSpec(memory_space=VMEM)] * 2,
        out_specs=[pl.BlockSpec(memory_space=HBM)] * 2 + [pl.BlockSpec(memory_space=VMEM)] * 2,
        out_shape=[HBM(field.shape, jnp.float32)] * 2 + [rows_shape] * 2,
        scratch_shapes=[pltpu.SMEM((slots,), jnp.int32)]
        + [pltpu.VMEM(field.shape, jnp.float32)] * 5
        + [pltpu.VMEM((2, 8 * slots, width), jnp.float32), pltpu.SemaphoreType.DMA((26,))],
        compiler_params=params(16),
        cost_estimate=pl.CostEstimate(flops=8 << 20, bytes_accessed=12 << 20, transcendentals=0),
        name="local0",
    )(*in_hbm(rows, field_prev, adjoint_prev, speed2), field, adjoint)


def first_border_kernel(rows_ref, partial_hbm, partial_adjoint_hbm, speed2_hbm, x_from_outer, x_from_inner, z_from_outer, z_from_inner, lines_ref, push, picked, out, adjoint_out, speed2, x_outer, x_inner, z_outer, z_inner, surface, partial, partial_adjoint, coupling, change, sems):
    shares = 4
    loads = [
        shares_of(source, target, sems, shares * i, shares)
        for i, (source, target) in enumerate(
            ((speed2_hbm, speed2), (partial_hbm, partial), (partial_adjoint_hbm, partial_adjoint))
        )
    ]
    arrivals = [[copies[i] for copies in loads] for i in range(shares)]
    for copies in arrivals:
        for copy in copies:
            copy.start()
    clear(coupling)
    lines = Lines(lines_ref, change.shape[1])
    couple_step(rows_ref, lines, 0, [push], picked, surface, change, coupling)
    border_planes(
        (partial, partial_adjoint),
        speed2,
        (x_from_outer, x_from_inner, z_from_outer, z_from_inner),
        (out, adjoint_out),
        (x_outer, x_inner, z_outer, z_inner),
        functools.partial(extra_of, coupling),
        arrivals,
    )


def coupling_scratch(field, slots, width):
    cells_z, cells_x, along = field.shape
    return [
        pltpu.VMEM((2 * (along // width), 2 * cells_z, cells_x, width), jnp.float32),
        pltpu.VMEM((2, slots, width), jnp.float32),
    ]


def first_border(rows, partials, speed2, halos, lines, push, picked):
    _, slots, width = push.shape
    field = partials[0]
    whole = jax.ShapeDtypeStruct(field.shape, jnp.float32)
    in_vmem = pl.BlockSpec(memory_space=VMEM)
    return pl.pallas_call(
        first_border_kernel,
        in_specs=[pl.BlockSpec(memory_space=SMEM)]
        + [pl.BlockSpec(memory_space=HBM)] * 3
        + [in_vmem] * 7,
        out_specs=[in_vmem] * 8,
        out_shape=[whole] * 3
        + edge_shapes(field, width)
        + [jax.ShapeDtypeStruct((2, slots, width), jnp.float32)],
        scratch_shapes=[pltpu.VMEM(field.shape, jnp.float32)] * 2
        + coupling_scratch(field, slots, width)
        + [pltpu.SemaphoreType.DMA((12,))],
        compiler_params=params(14),
        name="border0",
    )(rows, *in_hbm(*partials, speed2), *halos, lines, push, picked)


def local_kernel(step, rows_ref, field, field_prev, adjoint, adjoint_prev, speed2, lines_ref, surface, *refs):
    pushes, refs = list(refs[:step]), refs[step:]
    out, adjoint_out, push, next_surface = refs[:4]
    sends = []
    if step == STEPS - 2:
        sends = [
            pltpu.make_async_copy(source, target, refs[-1].at[i])
            for i, (source, target) in enumerate(zip((field, adjoint), refs[4:6]))
        ]
        refs = refs[:4] + refs[6:-1]
    for send in sends:
        send.start()
    coupling, change, tiles, picked = refs[4:8]
    loads = []
    if step == 1:
        *held, sems = refs[8:]
        loads = [
            pltpu.make_async_copy(source, target, sems.at[i])
            for i, (source, target) in enumerate(zip((field_prev, adjoint_prev), held))
        ]
        field_prev, adjoint_prev = held
    for copy in loads:
        copy.start()
    pick(rows_ref, (field, adjoint), picked, tiles)
    push[...] = KAPPA * (picked[...] - surface[...])
    clear(coupling)
    lines = Lines(lines_ref, change.shape[1])
    couple_step(rows_ref, lines, step, pushes + [push], picked, next_surface, change, coupling)
    for copy in loads:
        copy.wait()
    local_planes(
        (field, adjoint),
        (field_prev, adjoint_prev),
        (out, adjoint_out),
        speed2,
        functools.partial(extra_of, coupling),
    )
    for send in sends:
        send.wait()


def local_step(step, rows, field, field_prev, adjoint, adjoint_prev, speed2, lines, surface, pushes):
    _, slots, width = surface.shape
    whole = jax.ShapeDtypeStruct(field.shape, jnp.float32)
    rows_shape = jax.ShapeDtypeStruct(surface.shape, jnp.float32)
    in_vmem = pl.BlockSpec(memory_space=VMEM)
    before, held, kept = in_vmem, [], []
    if step == STEPS - 2:
        kept = [HBM(field.shape, jnp.float32)] * 2
        held = [pltpu.SemaphoreType.DMA((2,))]
    if step == 1:
        before = pl.BlockSpec(memory_space=HBM)
        held = [pltpu.VMEM(field.shape, jnp.float32)] * 2 + [pltpu.SemaphoreType.DMA((2,))]
        field_prev, adjoint_prev = in_hbm(field_prev, adjoint_prev)
    return pl.pallas_call(
        functools.partial(local_kernel, step),
        in_specs=[pl.BlockSpec(memory_space=SMEM), in_vmem, before, in_vmem, before]
        + [in_vmem] * (3 + step),
        out_specs=[in_vmem] * 4 + [pl.BlockSpec(memory_space=HBM)] * len(kept),
        out_shape=[whole, whole, rows_shape, rows_shape, *kept],
        scratch_shapes=coupling_scratch(field, slots, width)
        + [
            pltpu.VMEM((2, 8 * slots, width), jnp.float32),
            pltpu.VMEM((2, slots, width), jnp.float32),
        ]
        + held,
        compiler_params=params(12),
        cost_estimate=pl.CostEstimate(flops=8 << 20, bytes_accessed=12 << 20, transcendentals=0),
        name=f"local{step}",
    )(rows, field, field_prev, adjoint, adjoint_prev, speed2, lines, surface, *pushes)


def border_kernel(partial, partial_adjoint, speed2, x_from_outer, x_from_inner, z_from_outer, z_from_inner, out, adjoint_out, *edges):
    border_planes(
        (partial, partial_adjoint),
        speed2,
        (x_from_outer, x_from_inner, z_from_outer, z_from_inner),
        (out, adjoint_out),
        edges,
        None,
    )


def border_step(step, partials, speed2, halos, width):
    field = partials[0]
    whole = jax.ShapeDtypeStruct(field.shape, jnp.float32)
    in_vmem = pl.BlockSpec(memory_space=VMEM)
    return pl.pallas_call(
        border_kernel,
        in_specs=[in_vmem] * 7,
        out_specs=[in_vmem] * 6,
        out_shape=[whole, whole] + edge_shapes(field, width),
        compiler_params=params(8),
        name=f"border{step}",
    )(*partials, speed2, *halos)


def correlation_kernel(rows_ref, used, field, adjoint, lines_ref, surface, *refs):
    pushes, refs = list(refs[: STEPS - 1]), refs[STEPS - 1 :]
    gradient_hbm, change = refs[:2]
    targets, (gradient, tiles, picked, push, sems) = refs[2:4], refs[4:]
    sends = [
        pltpu.make_async_copy(source, target, sems.at[i])
        for i, (source, target) in enumerate(zip((field, adjoint), targets))
    ]
    for send in sends:
        send.start()
    pick(rows_ref, (field, adjoint), picked, tiles)
    push[...] = KAPPA * (picked[...] - surface[...])

    slots, width = change.shape[1:]
    lines = Lines(lines_ref, slots)
    known = pushes + [push]
    total = jnp.zeros((slots, width), jnp.float32)
    for late in range(STEPS):
        inside = (STEPS - late) * lines.row(TERMS - late)
        for t in range(STEPS - late):
            scale = (STEPS - late - t) * lines.scalar(TERMS - late - t)
            inside = inside + scale * known[t][0]
        total = total + known[late][1] * inside
    patches = gradient.shape[0]
    parts, rest = [], total
    for _ in range(3):
        parts.append(rest.astype(jnp.bfloat16))
        rest = rest - parts[-1].astype(jnp.float32)
    ids = lines.meta.T[0:1, :].astype(jnp.int32)
    ids = jnp.where(used[...] >= 0, ids, -1)
    owners = lax.broadcasted_iota(jnp.int32, (patches, slots), 0) == ids
    sums = jnp.dot(
        jnp.where(owners, 1.0, 0.0).astype(jnp.bfloat16),
        jnp.concatenate(parts, axis=1),
        preferred_element_type=jnp.float32,
    )
    gradient[...] = sums[:, :width] + (sums[:, width : 2 * width] + sums[:, 2 * width :])
    sends.append(pltpu.make_async_copy(gradient, gradient_hbm, sems.at[2]))
    sends[-1].start()

    for side in range(2):
        change[side] = BETA * (lines.surface(STEPS - 1, known, side) - picked[side])
    for send in sends:
        send.wait()


def correlate(rows, field, adjoint, lines, surface, pushes, patches):
    _, slots, width = surface.shape
    f32 = jnp.float32
    in_vmem = pl.BlockSpec(memory_space=VMEM)
    return pl.pallas_call(
        correlation_kernel,
        in_specs=[pl.BlockSpec(memory_space=SMEM)] + [in_vmem] * (5 + len(pushes)),
        out_specs=[pl.BlockSpec(memory_space=HBM), in_vmem] + [pl.BlockSpec(memory_space=HBM)] * 2,
        out_shape=[
            HBM((patches, width), f32),
            jax.ShapeDtypeStruct(surface.shape, f32),
        ]
        + [HBM(field.shape, f32)] * 2,
        scratch_shapes=[
            pltpu.VMEM((patches, width), f32),
            pltpu.VMEM((2, 8 * slots, width), f32),
        ]
        + [pltpu.VMEM((2, slots, width), f32)] * 2
        + [pltpu.SemaphoreType.DMA((3,))],
        compiler_params=params(10),
        name="correlation",
    )(rows, rows.reshape(1, slots), field, adjoint, lines, surface, *pushes)


def last_local_kernel(rows_hbm, field_hbm, field_prev_hbm, adjoint_hbm, adjoint_prev_hbm, speed2_hbm, change, out, adjoint_out, speed_first, speed_last, speed_ends, rows_ref, field, field_prev, adjoint, adjoint_prev, speed2, coupling, sems):
    shares = 4
    rows_load = pltpu.make_async_copy(rows_hbm, rows_ref, sems.at[0])
    rows_load.start()
    pairs = (
        (speed2_hbm, speed2),
        (field_hbm, field),
        (adjoint_hbm, adjoint),
        (field_prev_hbm, field_prev),
        (adjoint_prev_hbm, adjoint_prev),
    )
    arrivals = arrivals_of(pairs, sems, 1, shares)
    clear(coupling)
    rows_load.wait()
    couple(rows_ref, change, coupling)
    local_planes(
        (field, adjoint),
        (field_prev, adjoint_prev),
        (out, adjoint_out),
        speed2,
        functools.partial(extra_of, coupling),
        None,
        arrivals,
        1,
    )
    cells_z = speed2.shape[0]
    speed_ends[0], speed_ends[1] = speed2[0], speed2[cells_z - 1]

    def sides(z, carry):
        keep_side(speed2[z], z, speed_first, speed_last)
        return carry

    lax.fori_loop(0, cells_z, sides, 0, unroll=8)


def last_local(rows, field, field_prev, adjoint, adjoint_prev, speed2, change):
    _, slots, width = change.shape
    cells_z, cells_x, along = field.shape
    sides = jax.ShapeDtypeStruct((along // width, cells_z, width), jnp.float32)
    in_vmem = pl.BlockSpec(memory_space=VMEM)
    return pl.pallas_call(
        last_local_kernel,
        in_specs=[pl.BlockSpec(memory_space=HBM)] * 6 + [in_vmem],
        out_specs=[in_vmem] * 5,
        out_shape=[jax.ShapeDtypeStruct(field.shape, jnp.float32)] * 2
        + [sides, sides, jax.ShapeDtypeStruct((2, cells_x, along), jnp.float32)],
        scratch_shapes=[pltpu.SMEM((slots,), jnp.int32)]
        + [pltpu.VMEM(field.shape, jnp.float32)] * 5
        + coupling_scratch(field, slots, width)[:1]
        + [pltpu.SemaphoreType.DMA((21,))],
        compiler_params=params(16),
        cost_estimate=pl.CostEstimate(flops=8 << 20, bytes_accessed=12 << 20, transcendentals=0),
        name=f"local{STEPS - 1}",
    )(*in_hbm(rows, field, field_prev, adjoint, adjoint_prev, speed2), change)


def keep_side(cells, z, first, last):
    last_x, width = cells.shape[0] - 1, first.shape[2]
    for part in range(first.shape[0]):
        lanes = slice(part * width, (part + 1) * width)
        first[part, pl.ds(z, 1), :] = cells[0:1, lanes]
        last[part, pl.ds(z, 1), :] = cells[last_x : last_x + 1, lanes]


def finish_kernel(field_in, adjoint_in, speed_first, speed_last, speed_ends, x_from_outer, x_from_inner, z_from_outer, z_from_inner, out_hbm, adjoint_out_hbm, field, adjoint, sems):
    cells_z, cells_x, along = field.shape
    parts = speed_first.shape[0]
    shares = 4
    share = cells_z // shares
    sends = [
        shares_of(field, out_hbm, sems, 0, shares),
        shares_of(adjoint, adjoint_out_hbm, sems, shares, shares),
    ]
    for i in range(shares):
        for side, (source, held) in enumerate(((field_in, field), (adjoint_in, adjoint))):

            def one(z, carry):
                first, last = (
                    jnp.concatenate([ref[p, pl.ds(z, 1), :] for p in range(parts)], axis=1)
                    for ref in (speed_first, speed_last)
                )
                held[z] = source[z] + x_added(
                    first, last, x_from_outer, x_from_inner, side, z, (cells_x, along)
                )
                return carry

            lax.fori_loop(i * share, (i + 1) * share, one, 0, unroll=share)
            before, after = incoming("gz", z_from_outer[side], z_from_inner[side])
            if i == 0:
                held[0] = held[0] + speed_ends[0] * before
            if i == shares - 1:
                held[cells_z - 1] = held[cells_z - 1] + speed_ends[1] * after
            sends[side][i].start()
    for side in range(2):
        for send in sends[side]:
            send.wait()


def finish_call(field, adjoint, speed_first, speed_last, speed_ends, halos):
    return pl.pallas_call(
        finish_kernel,
        in_specs=[pl.BlockSpec(memory_space=VMEM)] * 9,
        out_specs=[pl.BlockSpec(memory_space=HBM)] * 2,
        out_shape=[HBM(field.shape, jnp.float32)] * 2,
        scratch_shapes=[pltpu.VMEM(field.shape, jnp.float32)] * 2 + [pltpu.SemaphoreType.DMA((8,))],
        compiler_params=params(8),
        name="finish",
    )(field, adjoint, speed_first, speed_last, speed_ends, *halos)


def swaps(axis, first):
    count = lax.axis_size(axis)
    if first:
        return [(i, i ^ 1) for i in range(count)]
    return [(i, (i + 1 if i % 2 else i - 1) % count) for i in range(count)]


def exchange(edges):
    axes = (("gx", False), ("gx", True), ("gz", False), ("gz", True))
    return [lax.ppermute(edge, axis, swaps(axis, first)) for edge, (axis, first) in zip(edges, axes)]


def body(
    pressure_now,
    pressure_prev,
    adjoint_now,
    adjoint_prev,
    speed2,
    layer_state,
    layer_maps,
    send_rows,
    slot_patch,
    patch_material,
):
    slots, _, width = layer_state.shape
    patches = patch_material.shape[0]
    devices = lax.axis_size(("gx", "gz"))
    rows = send_rows.reshape(-1)

    field, adjoint, *edges = first_edges(pressure_now, adjoint_now, width)
    halos = exchange(edges)
    lines = surface_rows(layer_maps, slot_patch, patch_material, layer_state)
    lines = lines.reshape(slots, 1, LINES * width)
    lines = lax.all_to_all(lines, ("gx", "gz"), split_axis=0, concat_axis=0, tiled=True)
    lines = lines.reshape(slots * LINES, width)

    *partials, push, picked = first_local(
        rows, field, pressure_prev, adjoint, adjoint_prev, speed2, slots, width
    )
    pushes = [push]
    field, adjoint, speed, *edges, surface = first_border(
        rows, partials, speed2, halos, lines, push, picked
    )
    field_prev, adjoint_prev = pressure_now, adjoint_now
    for step in range(1, STEPS - 1):
        halos = exchange(edges)
        field_next, adjoint_next, push, surface, *sent = local_step(
            step, rows, field, field_prev, adjoint, adjoint_prev, speed, lines, surface, pushes
        )
        partials = (field_next, adjoint_next)
        pushes.append(push)
        field_prev, adjoint_prev = field, adjoint
        field, adjoint, *edges = border_step(step, partials, speed, halos, width)
    halos = exchange(edges)
    gradient, change, *held = correlate(
        rows, field, adjoint, lines, surface, pushes, patches
    )
    parts = gradient.reshape(devices, patches // devices, width)
    parts = lax.all_to_all(parts, ("gx", "gz"), split_axis=0, concat_axis=0, tiled=True)
    *partials, first, last, ends = last_local(
        rows, held[0], sent[0], held[1], sent[1], speed2, change
    )
    field, adjoint = finish_call(*partials, first, last, ends, halos)
    return field, adjoint, jnp.sum(parts, axis=0)


def solution(mesh):
    grid = P("gz", "gx", None)
    split = P(("gx", "gz"), None, None)
    in_specs = (grid, grid, grid, grid, grid, split, P(), split, P(("gx", "gz")), P())
    out_specs = (grid, grid, P(("gx", "gz"), None))
    return jax.shard_map(body, mesh=mesh, in_specs=in_specs, out_specs=out_specs, check_vma=False)
```
